32 devices in a mesh: dp: 4 (over z), fsdp: 8 (over y, x, core).
Axes of the slice: x: 2, y: 2, z: 4, core: 2. Of those that a mesh axis runs over, the one named last changes fastest.
Arguments:
- tokens: bfloat16 [32768, 1024], P(('dp', 'fsdp')), may hold values from -6 to 6
- norm_gain: bfloat16 [2, 1024], P(None, ('dp', 'fsdp')), may hold values from 0.5 to 1.5
- norm_bias: bfloat16 [2, 1024], P(None, ('dp', 'fsdp')), may hold values from -1 to 1
- w_qkv: bfloat16 [1024, 3072], P(('dp', 'fsdp')), may hold values from -0.1875 to 0.1875
- attn_bias: bfloat16 [3, 1024], P(None, ('dp', 'fsdp')), may hold values from -1 to 1
- w_attn_out: bfloat16 [1024, 1024], P(('dp', 'fsdp')), may hold values from -0.75 to 0.75
- expert_in: bfloat16 [2, 1024, 4096], P(None, ('dp', 'fsdp')), may hold values from -0.1875 to 0.1875
- expert_in_bias: bfloat16 [2, 4096], P(None, ('dp', 'fsdp')), may hold values from -1 to 1
- expert_out: bfloat16 [2, 4096, 1024], P(None, ('dp', 'fsdp')), may hold values from -0.125 to 0.125
- expert_out_bias: bfloat16 [2, 1024], P(None, ('dp', 'fsdp')), may hold values from -1 to 1
- expert_ids: int32 [32768, 1], P(('dp', 'fsdp')), may hold values from 0 to 1, as said below
- running_load: float32 [2], replicated, may hold values from 0.5 to 1.5
- cotangent: bfloat16 [32768, 1024], P(('dp', 'fsdp')), may hold values from -6 to 6
Outputs:
- block_out: bfloat16 [32768, 1024], P(('dp', 'fsdp'))
- input_grad: float32 [32768, 1024], P(('dp', 'fsdp'))
- norm_gain_grad: float32 [2, 1024], P(None, ('dp', 'fsdp'))
- norm_bias_grad: float32 [2, 1024], P(None, ('dp', 'fsdp'))
- qkv_grad: float32 [1024, 3072], P(('dp', 'fsdp'))
- attn_bias_grad: float32 [3, 1024], P(None, ('dp', 'fsdp'))
- attn_out_grad: float32 [1024, 1024], P(('dp', 'fsdp'))
- expert_in_grad: float32 [2, 1024, 4096], P(None, ('dp', 'fsdp'))
- expert_in_bias_grad: float32 [2, 4096], P(None, ('dp', 'fsdp'))
- expert_out_grad: float32 [2, 4096, 1024], P(None, ('dp', 'fsdp'))
- expert_out_bias_grad: float32 [2, 1024], P(None, ('dp', 'fsdp'))
- expert_counts: int32 [2], replicated
- expert_load: float32 [2], replicated
The draws below stay inside these ranges and needn't reach their ends.
Inputs may be any that keep to these rules, and one draw needn't show every extreme that they name: `expert_ids`: among the tokens of one device no expert is named more than 640 times; in some device's tokens some expert is named exactly 640 times.
All inputs are finite; a program needn't handle non-finite values.
Results may differ from the reference program's by a relative error of at most 0.0095.
Values may be sent and summed in bfloat16 or wider, within the bound.
A program may use at most 448 MiB of HBM per device.

```python
import math
import jax
import jax.numpy as jnp
from jax import lax

D = 1024
HEADS = 16
HEAD = 64
FF = 4096
EXPERTS = 2
SEQ = 1024
TOK_DEV = 1024
MOST = 640
TOKENS = 32768


def draw_expert_ids(key, part):
    key = jax.random.fold_in(key, 11)
    device_count = TOKENS // TOK_DEV
    key_heavy, key_count, key_chosen, key_other, key_order = jax.random.split(key, 5)
    heavy = jax.random.randint(key_heavy, (device_count,), 0, EXPERTS, dtype=jnp.int32)
    fewest = TOK_DEV - MOST
    counts = jax.random.randint(key_count, (device_count,), fewest, MOST + 1, dtype=jnp.int32)
    chosen = jax.random.randint(key_chosen, (), 0, device_count, dtype=jnp.int32)
    counts = jnp.where(jnp.arange(device_count, dtype=jnp.int32) == chosen, MOST, counts).astype(jnp.int32)
    steps_away = jax.random.randint(key_other, (device_count, TOK_DEV), 0, max(EXPERTS - 1, 1), dtype=jnp.int32)
    others = (heavy[:, None] + 1 + steps_away) % EXPERTS
    slots = jnp.arange(TOK_DEV, dtype=jnp.int32)[None, :]
    ordered = jnp.where(slots < counts[:, None], heavy[:, None], others).astype(jnp.int32)
    order_keys = jax.random.split(key_order, device_count)
    mixed = jax.vmap(lambda row_key, row: jax.random.permutation(row_key, row))(order_keys, ordered)
    return mixed.reshape(TOKENS, 1).astype(jnp.int32)


def block_scale(stream_key, dims, cuts, low, high):
    def one(dim, shards_of):
        draws = jax.random.uniform(jax.random.fold_in(jax.random.fold_in(stream_key, 6), dim), (shards_of,), jnp.float32, low / len(cuts), high / len(cuts))
        return jnp.repeat(jnp.exp(draws), dims[dim] // shards_of).reshape((-1,) + (1,) * (len(dims) - dim - 1))

    level = one(*cuts[0])
    for cut in cuts[1:]:
        level = level * one(*cut)
    return level


def scatter_about(own_key, dims, width, reach, shards=(), kind=jnp.bfloat16):
    drawn = jax.random.normal(own_key, dims, jnp.float32) * width
    if len(shards) > 0:
        drawn = block_scale(own_key, dims, shards, -0.22, 0.18) * drawn
    return jnp.clip(drawn, min=-reach, max=reach).astype(kind)


def setup_inputs(seed: int = 0) -> dict:
    splits = jax.random.split(jax.random.key(seed), 14)
    return {
        "tokens": scatter_about(splits[0], (TOKENS, D), 1.0, 6.0, ((0, 32),)),
        "norm_gain": jnp.clip(1.0 + 0.1 * jax.random.normal(splits[1], (2, D), jnp.float32), 0.5, 1.5).astype(jnp.bfloat16),
        "norm_bias": scatter_about(splits[2], (2, D), 0.2, 1.0, ((1, 32),)),
        "w_qkv": scatter_about(splits[3], (D, 3 * D), D ** -0.5, 0.1875, ((0, 32),)),
        "attn_bias": scatter_about(splits[4], (3, D), 0.2, 1.0, ((1, 32),)),
        "w_attn_out": scatter_about(splits[5], (D, D), (D // 16) ** -0.5, 0.75, ((0, 32),)),
        "expert_in": scatter_about(splits[6], (EXPERTS, D, FF), D ** -0.5, 0.1875, ((1, 32),)),
        "expert_in_bias": scatter_about(splits[7], (EXPERTS, FF), 0.2, 1.0, ((1, 32),)),
        "expert_out": scatter_about(splits[8], (EXPERTS, FF, D), (FF // 2) ** -0.5, 0.125, ((1, 32),)),
        "expert_out_bias": scatter_about(splits[9], (EXPERTS, D), 0.2, 1.0, ((1, 32),)),
        "expert_ids": draw_expert_ids(jax.random.fold_in(splits[13], 71), 0),
        "running_load": jnp.clip(jax.random.uniform(splits[11], (EXPERTS,), jnp.float32, 0.5, 1.5), 0.5, 1.5),
        "cotangent": scatter_about(splits[12], (TOKENS, D), 1.0, 6.0, ((0, 32),)),
    }


@jax.custom_vjp
def low(v):
    return lax.optimization_barrier(v.astype(jnp.bfloat16)).astype(jnp.float32)

@jax.custom_vjp
def low_back(v):
    return v

def low_keep(v):
    return (low(v), None)

def low_pass(kept, grad):
    return (grad,)

def back_keep(v):
    return (v, None)

def back_low(kept, grad):
    return (low(grad),)
low.defvjp(low_keep, low_pass)
low_back.defvjp(back_keep, back_low)
NORM_EPS = 1e-05
SCORE_SCALE = 0.125
MASKED = -1e+30

def product(left_side, right_side):
    return jnp.dot(left_side, right_side, precision=lax.Precision.HIGHEST)

def normalize(values, gain_row, shift_row):
    center = values - lax.optimization_barrier(jnp.mean(values, axis=-1, keepdims=True))
    spread = lax.optimization_barrier(jnp.mean(center * center, axis=-1, keepdims=True))
    return center * lax.rsqrt(spread + NORM_EPS) * gain_row + shift_row

def attend(query, keys_in, values_in):
    row_count = query.shape[0]
    block_rows = min(512, SEQ)
    per_seq = SEQ // block_rows
    seq_count = row_count // SEQ
    query_blocks = query.reshape(seq_count * per_seq, block_rows, HEADS, HEAD)
    key_seqs = keys_in.reshape(seq_count, SEQ, HEADS, HEAD)
    value_seqs = values_in.reshape(seq_count, SEQ, HEADS, HEAD)
    positions = jnp.arange(seq_count * per_seq, dtype=jnp.int32)

    def one_block(block_item):
        query_block, position = block_item
        seq_index = (position // per_seq).astype(jnp.int32)
        first_row = (position % per_seq * block_rows).astype(jnp.int32)
        key_seq = lax.dynamic_index_in_dim(key_seqs, seq_index, 0, keepdims=False)
        value_seq = lax.dynamic_index_in_dim(value_seqs, seq_index, 0, keepdims=False)
        scores = jnp.einsum('qhd,khd->hqk', query_block, key_seq, precision=lax.Precision.HIGHEST) * SCORE_SCALE
        scores = low_back(scores)
        allowed = jnp.arange(SEQ, dtype=jnp.int32)[None, :] <= (first_row + jnp.arange(block_rows, dtype=jnp.int32))[:, None]
        scores = jnp.where(allowed[None], scores, MASKED)
        weights = low(jax.nn.softmax(scores, axis=-1))
        return jnp.einsum('hqk,khd->qhd', weights, value_seq, precision=lax.Precision.HIGHEST)
    attended = lax.map(jax.checkpoint(one_block), (query_blocks, positions))
    return attended.reshape(row_count, HEADS * HEAD)

def block_forward(inputs, token_experts, params):
    gains, shifts, qkv_weight, biases, attn_weight, in_weight, in_bias, out_weight, out_bias = params
    normed_one = low(normalize(inputs, gains[0], shifts[0]))
    projected = product(normed_one, qkv_weight)
    query = low(low_back(projected[:, :D] + biases[0]))
    keys_low = low(low_back(projected[:, D:2 * D]))
    values_low = low(low_back(projected[:, 2 * D:] + biases[1]))
    attended = low(low_back(attend(query, keys_low, values_low)))
    residual = inputs + low_back(product(attended, attn_weight) + biases[2])
    normed_two = low(normalize(residual, gains[1], shifts[1]))
    expert_sum = jnp.zeros_like(inputs)
    for expert in range(EXPERTS):
        hidden_pre = low_back(product(normed_two, in_weight[expert]) + in_bias[expert])
        hidden_low = low(jax.nn.gelu(hidden_pre))
        produced = product(hidden_low, out_weight[expert]) + out_bias[expert]
        expert_sum = expert_sum + jnp.where((token_experts == expert)[:, None], produced, 0.0)
    return residual + low_back(expert_sum)

def reference(tokens, norm_gain, norm_bias, w_qkv, attn_bias, w_attn_out, expert_in, expert_in_bias, expert_out, expert_out_bias, expert_ids, running_load, cotangent):
    params = tuple((entry.astype(jnp.float32) for entry in (norm_gain, norm_bias, w_qkv, attn_bias, w_attn_out, expert_in, expert_in_bias, expert_out, expert_out_bias)))
    group_seqs = math.gcd(max(1, 4096 // SEQ), TOKENS // SEQ)
    group_rows = group_seqs * SEQ
    group_count = TOKENS // group_rows
    token_experts = expert_ids[:, 0].reshape(group_count, group_rows)

    def forward(inputs, weights):

        def step(carried, group_item):
            return (carried, block_forward(group_item[0], group_item[1], weights))
        carried, outputs = lax.scan(jax.checkpoint(step), jnp.zeros((), jnp.float32), (inputs.reshape(group_count, group_rows, D), token_experts))
        return outputs.reshape(TOKENS, D)
    block_out, pull_back = jax.vjp(forward, tokens.astype(jnp.float32), params)
    input_grad, weight_grads = pull_back(cotangent.astype(jnp.float32))
    matches = expert_ids[:, 0][:, None] == jnp.arange(EXPERTS, dtype=jnp.int32)[None, :]
    counts = lax.optimization_barrier(jnp.sum(matches.astype(jnp.int32), axis=0))
    expert_load = 0.9 * running_load + 0.1 * (counts.astype(jnp.float32) * EXPERTS / TOKENS)
    return (block_out.astype(jnp.bfloat16), input_grad, weight_grads[0], weight_grads[1], weight_grads[2], weight_grads[3], weight_grads[4], weight_grads[5], weight_grads[6], weight_grads[7], weight_grads[8], counts, expert_load)
```

```python
import functools
import math

import jax
import jax.numpy as jnp
from jax import lax
from jax.experimental import pallas as pl
from jax.experimental.pallas import tpu as pltpu
from jax.sharding import Mesh, PartitionSpec as P

BF16 = jnp.bfloat16
F32 = jnp.float32
MESH_ID = pl.DeviceIdType.MESH

HEAD = 64
SEQ = 1024
MOST = 640
EXPERTS = 2
CHUNKS = 2
NORM_EPS = 1e-05
SCORE_SCALE = 0.125
SCALE_LOG2 = SCORE_SCALE * math.log2(math.e)
MASKED = -1e30
BLOCK = 256
MIB = 1 << 20


def dot(left, right):
    return lax.dot_general(left, right, (((1,), (0,)), ((), ())), preferred_element_type=F32)


def dot_last(left, right):
    return lax.dot_general(left, right, (((1,), (1,)), ((), ())), preferred_element_type=F32)


def row_stats(values):
    center = values - jnp.mean(values, axis=-1, keepdims=True)
    spread = jnp.mean(center * center, axis=-1, keepdims=True)
    inverse = lax.rsqrt(spread + NORM_EPS)
    return center * inverse, inverse


class Place:
    def __init__(self, nz, nx):
        self.nz, self.nx = nz, nx
        self.bits_z, self.bits_x = nz.bit_length() - 1, nx.bit_length() - 1
        self.z, self.xy, self.core = lax.axis_index("dp"), lax.axis_index("xy"), lax.axis_index("core")
        self.flip_z = [(1 - 2 * lax.rem(lax.div(self.z, 2**k), 2)) * 2**k for k in range(self.bits_z)]
        self.flip_x = [(1 - 2 * lax.rem(lax.div(self.xy, 2**k), 2)) * 2**k for k in range(self.bits_x)]

    def step_x(self, k, core=None):
        core = self.core if core is None else core
        return (1 - core) * self.flip_x[k] + core * self.flip_x[self.bits_x - 1 - k]

    def span_x(self, which, core=None):
        return self.xy + sum(self.step_x(k, core) for k in range(self.bits_x) if which >> k & 1)

    def span_z(self, which):
        return self.z + sum(self.flip_z[k] for k in range(self.bits_z) if which >> k & 1)

    def partners(self):
        found = [(self.z + flip, self.xy, self.core) for flip in self.flip_z]
        found += [(self.z, self.xy + flip, self.core) for flip in self.flip_x]
        return found + [(self.z, self.xy, 1 - self.core)]

    def sibling(self):
        return (self.z, self.xy, 1 - self.core)

    def barrier(self):
        semaphore = pltpu.get_barrier_semaphore()
        partners = self.partners()
        for partner in partners:
            pl.semaphore_signal(semaphore, inc=1, device_id=partner, device_id_type=MESH_ID)
        pl.semaphore_wait(semaphore, len(partners))


def remote(src, dst, send, recv, device):
    return pltpu.make_async_remote_copy(
        src_ref=src, dst_ref=dst, send_sem=send, recv_sem=recv, device_id=device, device_id_type=MESH_ID
    )


ALL = slice(None)


class Gather:
    def __init__(self, place, regions, send, recv, to_sibling=None):
        self.place, self.regions, self.send, self.recv = place, regions, send, recv
        self.to_sibling = to_sibling
        self.stages = place.bits_z + place.bits_x + (0 if to_sibling is None else 1)

    def copies(self, piece, stage):
        place, region = self.place, self.regions[piece]
        found = []
        if stage < place.bits_z:
            bit = place.bits_z - 1 - stage
            device = (place.z + place.flip_z[bit], place.xy, place.core)
            for held in range(2**stage):
                found += [(ref, device) for ref in region(place.span_z(held << (bit + 1)), place.xy)]
        elif stage < place.bits_z + place.bits_x:
            step = stage - place.bits_z
            device = (place.z, place.xy + place.step_x(step), place.core)
            for held in range(2**step):
                found += [(ref, device) for ref in region(ALL, place.span_x(held))]
        else:
            found += [(ref, place.sibling()) for ref in self.to_sibling[piece]]
        return [
            remote(ref, ref, self.send.at[piece, stage, i], self.recv.at[piece, stage, i], device)
            for i, (ref, device) in enumerate(found)
        ]

    @property
    def ticks(self):
        return len(self.regions) + self.stages

    def tick(self, now):
        for stage in range(self.stages, -1, -1):
            piece = now - stage
            if not 0 <= piece < len(self.regions):
                continue
            if stage > 0:
                for copy in self.copies(piece, stage - 1):
                    copy.wait()
            if stage < self.stages:
                for copy in self.copies(piece, stage):
                    copy.start()


def gather_semaphores(nz, nx, pieces, width, to_sibling):
    stages = nz.bit_length() - 1 + nx.bit_length() - 1 + int(to_sibling)
    shape = (pieces, stages, width * max(nz // 2, nx // 2, 1))
    return [pltpu.SemaphoreType.DMA(shape), pltpu.SemaphoreType.DMA(shape)]


HBM = pl.BlockSpec(memory_space=pl.ANY)
VMEM = pl.BlockSpec(memory_space=pltpu.VMEM)


def remote_params(collective_id, vmem=32):
    return pltpu.CompilerParams(
        collective_id=collective_id, has_side_effects=True, vmem_limit_bytes=vmem * MIB
    )


def one_hot(slots, count):
    rows = lax.broadcasted_iota(jnp.int32, (count, slots.shape[1]), 0)
    return jnp.where(rows == slots, 1.0, 0.0).astype(BF16)


def pick_rows(picked, slots_ref, values, own_row):
    chosen = one_hot(slots_ref[own_row : own_row + 1, :], picked.shape[0])
    picked[...] = dot(chosen, values).astype(BF16)


def attention_weights(nz, nx, w_qkv, w_out, small, cotangent, slots):
    depth, width = w_qkv.shape
    d = w_out.shape[1]
    parts = width // d
    pieces = parts + 1

    def kernel(
        qkv_ref, out_ref, small_ref, cot_ref, slots_ref, qkv_full, out_full, small_full, grows,
        picked, send, recv, here, pair_send, pair_recv,
    ):
        place = Place(nz, nx)
        z, xy, core = place.z, place.xy, place.core
        own = [
            pltpu.make_async_copy(qkv_ref, qkv_full.at[z, xy, core], here.at[0]),
            pltpu.make_async_copy(out_ref, out_full.at[z, xy, core], here.at[1]),
            pltpu.make_async_copy(small_ref, small_full.at[z, xy, core], here.at[2]),
        ]
        for copy in own:
            copy.start()
        place.barrier()
        for copy in own:
            copy.wait()

        def region(piece):
            if piece == parts:
                return lambda zs, xs: [out_full.at[zs, xs, core]]
            columns = pl.ds(piece * d, d)
            if piece:
                return lambda zs, xs: [qkv_full.at[zs, xs, core, :, columns]]
            return lambda zs, xs: [qkv_full.at[zs, xs, core, :, columns], small_full.at[zs, xs, core]]

        regions = [region(piece) for piece in range(pieces)]
        gather = Gather(place, regions, send, recv, [r(ALL, ALL) for r in regions])
        gather.tick(0)
        pick_rows(picked.at[0], slots_ref, cot_ref[...], 0)
        mine = pltpu.make_async_copy(picked.at[0], grows.at[0], here.at[3])
        mine.start()
        gather.tick(1)
        pick_rows(picked.at[1], slots_ref, cot_ref[...], 1)
        theirs = remote(picked.at[1], grows.at[1], pair_send, pair_recv, place.sibling())
        theirs.start()
        for now in range(2, gather.ticks):
            gather.tick(now)
        mine.wait()
        theirs.wait()

    return pl.pallas_call(
        kernel,
        out_shape=[
            jax.ShapeDtypeStruct((nz, nx, 2, depth, width), BF16),
            jax.ShapeDtypeStruct((nz, nx, 2, depth, d), BF16),
            jax.ShapeDtypeStruct((nz, nx, 2) + small.shape, BF16),
            jax.ShapeDtypeStruct((2, MOST, d), BF16),
        ],
        in_specs=[HBM, HBM, HBM, VMEM, VMEM],
        out_specs=[HBM] * 4,
        scratch_shapes=[
            pltpu.VMEM((2, MOST, d), BF16),
            *gather_semaphores(nz, nx, pieces, 2, True),
            pltpu.SemaphoreType.DMA((4,)),
            pltpu.SemaphoreType.DMA,
            pltpu.SemaphoreType.DMA,
        ],
        compiler_params=remote_params(1),
        name="attention_weights",
    )(w_qkv, w_out, small, cotangent, slots)


class Reduce:
    def __init__(self, place, pieces, pair_first, send, recv, here):
        self.place, self.pieces, self.pair_first = place, pieces, pair_first
        self.send, self.recv, self.here = send, recv, here
        self.stages = place.bits_z + place.bits_x + 1

    def plan(self, piece, stage):
        place = self.place
        source, buffers, target = self.pieces[piece]
        acc, landing = buffers[0], buffers[1:]
        nx, nz, bits_x = place.nx, place.nz, place.bits_x
        far, near, sums = [], [], []
        slot = stage
        if self.pair_first:
            if stage == 0:
                for r in range(nx):
                    far.append((source(ALL, place.span_x(r, 1 - place.core), 1 - place.core), landing[0].at[r], place.sibling()))
                    near.append((source(ALL, place.span_x(r), place.core), acc.at[r]))
                return self.copies(piece, stage, far, near), [(acc.at[r], landing[0].at[r]) for r in range(nx)]
            stage -= 1
        elif stage == self.stages - 1:
            mine = acc.at[0, place.z]
            far.append((mine.at[1 - place.core], target.at[place.core], place.sibling()))
            near.append((mine.at[place.core], target.at[place.core]))
            return self.copies(piece, slot, far, near), []
        if stage < bits_x:
            k = bits_x - 1 - stage
            device = (place.z, place.xy + place.step_x(k), place.core)
            if stage == 0 and not self.pair_first:
                for j in range(2**k):
                    far.append((source(ALL, place.span_x(2**k + j), place.core), landing[slot].at[j], device))
                    near.append((source(ALL, place.span_x(j), place.core), acc.at[j]))
            else:
                far.append((acc.at[pl.ds(2**k, 2**k)], landing[slot], device))
            sums = [(acc.at[j], landing[slot].at[j]) for j in range(2**k)]
        else:
            bit = stage - bits_x
            device = (place.z + place.flip_z[bit], place.xy, place.core)
            for s in range(2 ** (place.bits_z - 1 - bit)):
                upper = s << (bit + 1)
                far.append((acc.at[0, place.span_z(upper + 2**bit)], landing[slot].at[s], device))
                sums.append((acc.at[0, place.span_z(upper)], landing[slot].at[s]))
        return self.copies(piece, slot, far, near), sums

    def copies(self, piece, slot, far, near):
        made = [
            remote(src, dst, self.send.at[piece, slot, i], self.recv.at[piece, slot, i], device)
            for i, (src, dst, device) in enumerate(far)
        ]
        return made + [
            pltpu.make_async_copy(src, dst, self.here.at[piece, slot, i]) for i, (src, dst) in enumerate(near)
        ]

    def begin(self, piece, stage):
        for copy in self.plan(piece, stage)[0]:
            copy.start()

    def finish(self, piece, stage):
        copies, sums = self.plan(piece, stage)
        for copy in copies:
            copy.wait()
        for total, landed in sums:
            if len(total.shape) > 3:
                @pl.loop(0, total.shape[0])
                def _(i, total=total, landed=landed):
                    total[i] = (total[i].astype(F32) + landed[i].astype(F32)).astype(BF16)
            else:
                total[...] = (total[...].astype(F32) + landed[...].astype(F32)).astype(BF16)
        if self.pair_first and stage == self.stages - 1:
            source, buffers, target = self.pieces[piece]
            last = pltpu.make_async_copy(buffers[0].at[0, self.place.z], target, self.here.at[piece, stage, 0])
            last.start()
            last.wait()

    @property
    def ticks(self):
        return len(self.pieces) + self.stages

    def tick(self, now):
        for stage in range(self.stages, -1, -1):
            piece = now - stage
            if not 0 <= piece < len(self.pieces):
                continue
            if stage > 0:
                self.finish(piece, stage - 1)
            if stage < self.stages:
                self.begin(piece, stage)


def reduce_buffers(nz, nx, tail, pair_first):
    bits_z, bits_x = nz.bit_length() - 1, nx.bit_length() - 1
    held = nx if pair_first else nx // 2
    shapes = [(held, nz) + tail]
    if pair_first:
        shapes.append((nx, nz) + tail)
    shapes += [(2**k, nz) + tail for k in reversed(range(bits_x))]
    shapes += [(2 ** (bits_z - 1 - bit),) + tail for bit in range(bits_z)]
    return [pltpu.VMEM(shape, BF16) for shape in shapes]


def reduce_semaphores(nz, nx, pieces):
    stages = nz.bit_length() - 1 + nx.bit_length() - 1 + 1
    shape = (pieces, stages, max(nx, nz // 2, 1))
    return [pltpu.SemaphoreType.DMA(shape)] * 3


class Total:
    def __init__(self, place, terms, landing, send, recv):
        self.place, self.terms, self.landing, self.send, self.recv = place, terms, landing, send, recv
        self.stages = len(place.partners())

    def copy(self, stage):
        device = self.place.partners()[stage]
        return remote(self.terms.at[stage], self.landing.at[stage], self.send.at[stage], self.recv.at[stage], device)

    def begin(self, stage):
        self.copy(stage).start()

    def finish(self, stage):
        self.copy(stage).wait()
        self.terms[stage + 1] = self.terms[stage] + self.landing[stage]


class ExpertGather:
    def __init__(self, place, in_own, out_own, in_full, out_full, send, recv, pair_send, pair_recv, here):
        self.place, z, xy, core = place, place.z, place.xy, place.core
        self.near = [
            pltpu.make_async_copy(in_own.at[core], in_full.at[z, xy, core], here.at[0]),
            pltpu.make_async_copy(out_own.at[core], out_full.at[z, xy, core], here.at[1]),
        ]
        self.pair = [
            remote(in_own.at[1 - core], in_full.at[z, xy, core], pair_send.at[0], pair_recv.at[0], place.sibling()),
            remote(out_own.at[1 - core], out_full.at[z, xy, core], pair_send.at[1], pair_recv.at[1], place.sibling()),
        ]
        self.gather = Gather(
            place, expert_pieces(in_full, out_full, lambda ref, columns: lambda zs, xs: [ref.at[zs, xs, :, :, columns]]),
            send, recv,
        )
        self.ticks = self.gather.ticks

    def begin(self):
        for copy in self.near:
            copy.start()

    def tick(self, now):
        if now == 0:
            for copy in self.pair:
                copy.start()
            for copy in self.near + self.pair:
                copy.wait()
        self.gather.tick(now)


EXPERT_CUTS = 4


def expert_pieces(in_ref, out_ref, make):
    pieces = []
    for ref in (in_ref, out_ref):
        cut = ref.shape[-1] // EXPERT_CUTS
        pieces += [make(ref, pl.ds(i * cut, cut)) for i in range(EXPERT_CUTS)]
    return pieces


def expert_gather_scratch(nz, nx):
    return [
        *gather_semaphores(nz, nx, 2 * EXPERT_CUTS, 1, False),
        pltpu.SemaphoreType.DMA((2,)),
        pltpu.SemaphoreType.DMA((2,)),
        pltpu.SemaphoreType.DMA((2,)),
    ]


def full_shapes(nz, nx, in_own, out_own):
    return [jax.ShapeDtypeStruct((nz, nx, 2) + own.shape[1:], BF16) for own in (in_own, out_own)]


class ExpertReduce:
    def __init__(self, place, in_terms, out_terms, in_sum, out_sum, buffers, send, recv, here):
        sources = expert_pieces(
            in_terms, out_terms, lambda ref, columns: lambda zs, xs, core: ref.at[zs, xs, :, :, columns]
        )
        targets = expert_pieces(in_sum, out_sum, lambda ref, columns: ref.at[:, :, columns])
        size = len(buffers) // len(sources)
        pieces = [
            (source, buffers[i * size : (i + 1) * size], target)
            for i, (source, target) in enumerate(zip(sources, targets))
        ]
        self.reduce = Reduce(place, pieces, False, send, recv, here)
        self.ticks, self.tick = self.reduce.ticks, self.reduce.tick


def expert_reduce_scratch(nz, nx, in_terms, out_terms):
    buffers = []
    for terms in (in_terms, out_terms):
        tail = terms.shape[2:4] + (terms.shape[4] // EXPERT_CUTS,)
        for _ in range(EXPERT_CUTS):
            buffers += reduce_buffers(nz, nx, tail, False)
    return buffers, list(reduce_semaphores(nz, nx, 2 * EXPERT_CUTS))


def sum_shapes(in_terms, out_terms):
    return [jax.ShapeDtypeStruct((2,) + terms.shape[3:], BF16) for terms in (in_terms, out_terms)]


def attend_pair(qkv, head, attended, log_total):
    n, d = attended.shape
    low = lax.broadcasted_iota(jnp.int32, (n, 128), 1) < HEAD
    one, zero = jnp.ones((), BF16), jnp.zeros((), BF16)
    query = qkv[:, pl.ds(pl.multiple_of(head * 128, 128), 128)]
    key = qkv[:, pl.ds(pl.multiple_of(d + head * 128, 128), 128)]
    value = qkv[:, pl.ds(pl.multiple_of(2 * d + head * 128, 128), 128)]
    values = [jnp.where(low, value, one), jnp.where(low, one, value)]
    queries = [jnp.where(low, query, zero), jnp.where(low, zero, query)]
    low = low[:BLOCK]
    allowed = lax.broadcasted_iota(jnp.int32, (BLOCK, BLOCK), 1) <= lax.broadcasted_iota(
        jnp.int32, (BLOCK, BLOCK), 0
    )
    for i in range(n // BLOCK):
        first, end = i * BLOCK, (i + 1) * BLOCK
        found = []
        for j in range(2):
            near = jnp.where(allowed, dot_last(queries[j][first:end], key[first:end]), MASKED)
            top = jnp.max(near, axis=-1, keepdims=True)
            if i:
                far = dot_last(queries[j][first:end], key[:first])
                top = jnp.maximum(top, jnp.max(far, axis=-1, keepdims=True))
            top = top * SCALE_LOG2
            out = dot(jnp.exp2(near * SCALE_LOG2 - top).astype(BF16), values[j][first:end])
            if i:
                out = out + dot(jnp.exp2(far * SCALE_LOG2 - top).astype(BF16), values[j][:first])
            found.append((out, top))
        (out_a, top_a), (out_b, top_b) = found
        total = pltpu.roll(jnp.where(low, out_b, out_a), HEAD, axis=1)
        attended[first:end, pl.ds(pl.multiple_of(head * 128, 128), 128)] = (
            jnp.where(low, out_a, out_b) / total
        ).astype(BF16)
        logs = (jnp.where(low, top_a, top_b) + jnp.log2(total)).T
        log_total[head, 0:1, first:end] = logs[0:1]
        log_total[head, 1:2, first:end] = logs[HEAD : HEAD + 1]


def attention_forward(nz, nx, tokens, qkv_full, out_full, vectors, slots, in_own, out_own):
    n, d = tokens.shape
    heads = d // 128

    def kernel(
        tokens_ref, w_ref, wo_ref, vec_ref, slots_ref, in_own, out_own,
        normed_hbm, qkv_hbm, attended_hbm, log_hbm, residual_hbm, rows_hbm, in_full, out_full,
        normed, qkv, attended, logs, residual, normed_two, picked, here, pair_send, pair_recv, *gather_scratch,
    ):
        place = Place(nz, nx)
        gather = ExpertGather(place, in_own, out_own, in_full, out_full, *gather_scratch)
        gather.begin()
        place.barrier()
        gather.tick(0)

        @pl.loop(0, n // BLOCK)
        def _(i):
            rows = pl.ds(pl.multiple_of(i * BLOCK, BLOCK), BLOCK)
            scaled, _ = row_stats(tokens_ref[rows].astype(F32))
            normed[rows] = (scaled * vec_ref[0:1, :d] + vec_ref[1:2, :d]).astype(BF16)
            qkv[rows] = (dot(normed[rows], w_ref[...]) + vec_ref[2:3, :]).astype(BF16)
            for k in range(n // BLOCK):
                if k % 2 == 1:
                    @pl.when(i == k)
                    def _(k=k):
                        gather.tick(1 + k // 2)

        saves = [
            pltpu.make_async_copy(normed, normed_hbm, here.at[0]),
            pltpu.make_async_copy(qkv, qkv_hbm, here.at[1]),
        ]
        for save in saves:
            save.start()

        @pl.loop(0, heads)
        def _(head):
            attend_pair(qkv, head, attended, logs)
            for k in range(heads):
                if 3 + k < gather.ticks - 2:
                    @pl.when(head == k)
                    def _(k=k):
                        gather.tick(3 + k)

        saves += [
            pltpu.make_async_copy(attended, attended_hbm, here.at[2]),
            pltpu.make_async_copy(logs, log_hbm, here.at[3]),
        ]
        for save in saves[2:]:
            save.start()
        for now in range(3 + heads, gather.ticks - 2):
            gather.tick(now)

        @pl.loop(0, n // BLOCK)
        def _(i):
            rows = pl.ds(pl.multiple_of(i * BLOCK, BLOCK), BLOCK)
            added = dot(attended[rows], wo_ref[...]) + vec_ref[0:1, 2 * d :]
            residual[rows] = tokens_ref[rows].astype(F32) + added
            scaled, _ = row_stats(residual[rows])
            normed_two[rows] = (scaled * vec_ref[0:1, d : 2 * d] + vec_ref[1:2, d : 2 * d]).astype(BF16)

        saves.append(pltpu.make_async_copy(residual, residual_hbm, here.at[4]))
        saves[-1].start()
        gather.tick(gather.ticks - 2)
        pick_rows(picked.at[1], slots_ref, normed_two[...], 1)
        theirs = remote(picked.at[1], rows_hbm.at[1], pair_send, pair_recv, place.sibling())
        theirs.start()
        pick_rows(picked.at[0], slots_ref, normed_two[...], 0)
        saves.append(pltpu.make_async_copy(picked.at[0], rows_hbm.at[0], here.at[5]))
        saves[-1].start()
        gather.tick(gather.ticks - 1)
        for save in saves:
            save.wait()
        theirs.wait()

    shapes = [
        jax.ShapeDtypeStruct((n, d), BF16),
        jax.ShapeDtypeStruct((n, 3 * d), BF16),
        jax.ShapeDtypeStruct((n, d), BF16),
        jax.ShapeDtypeStruct((heads, 8, n), F32),
        jax.ShapeDtypeStruct((n, d), F32),
        jax.ShapeDtypeStruct((2, MOST, d), BF16),
    ]
    return pl.pallas_call(
        kernel,
        out_shape=shapes + full_shapes(nz, nx, in_own, out_own),
        in_specs=[VMEM] * 5 + [HBM] * 2,
        out_specs=[HBM] * 8,
        scratch_shapes=[
            *[pltpu.VMEM(shape.shape, shape.dtype) for shape in shapes[:5]],
            pltpu.VMEM((n, d), BF16),
            pltpu.VMEM((2, MOST, d), BF16),
            pltpu.SemaphoreType.DMA((6,)),
            pltpu.SemaphoreType.DMA,
            pltpu.SemaphoreType.DMA,
            *expert_gather_scratch(nz, nx),
        ],
        compiler_params=remote_params(2, 60),
        name="attention_forward",
    )(tokens, qkv_full, out_full, vectors, slots, in_own, out_own)


def gelu_and_slope(values):
    root = math.sqrt(2 / math.pi)
    cube = 0.044715
    square = values * values
    bent = jnp.tanh(values * (root + root * cube * square))
    half = 0.5 * (1 + bent)
    slope = half + 0.5 * values * (1 - bent * bent) * (root + 3 * root * cube * square)
    return values * half, slope


TILE = 512


def expert_step(refs, side, steps):
    (rows_ref, grads_ref, in_ref, out_ref, bias_ref, in_grad, out_grad, bias_grad, turned, made, back) = refs
    step = pl.program_id(0)

    def beside(spot):
        for k in range(steps):
            @pl.when(step == k)
            def _(k=k):
                side(k, spot)

    @pl.when(step == 0)
    def _():
        turned[...] = rows_ref[...].T

    beside(0)
    hidden_pre = dot(rows_ref[...], in_ref[...]) + bias_ref[0:1, :]
    hidden, slope = gelu_and_slope(hidden_pre)
    hidden = hidden.astype(BF16)
    grad_pre = dot_last(grads_ref[...], out_ref[...]) * slope
    bias_grad[0:1, :] = jnp.sum(grad_pre, axis=0, keepdims=True)
    grad_pre = grad_pre.astype(BF16)
    beside(1)
    made[...] += dot(hidden, out_ref[...])
    back[...] += dot_last(grad_pre, in_ref[...])
    beside(2)
    out_grad[...] = dot(hidden.T, grads_ref[...]).astype(BF16)
    in_grad[...] = dot(turned[...], grad_pre).astype(BF16)
    beside(3)


def expert_specs(rows, d, width):
    whole = pl.BlockSpec((rows, d), lambda step: (0, 0), pipeline_mode=pl.Buffered(1))
    inputs = [
        whole,
        whole,
        pl.BlockSpec((d, TILE), lambda step: (0, step)),
        pl.BlockSpec((TILE, d), lambda step: (step, 0)),
        pl.BlockSpec((1, TILE), lambda step: (0, step)),
    ]
    outputs = [inputs[2], inputs[3], inputs[4]]
    shapes = [
        jax.ShapeDtypeStruct((d, width), BF16),
        jax.ShapeDtypeStruct((width, d), BF16),
        jax.ShapeDtypeStruct((1, width), F32),
    ]
    return inputs, outputs, shapes


def experts_first(nz, nx, rows, grads, in_full, out_full, bias, in_own, out_own):
    count, d = rows.shape
    width = in_full.shape[1]
    steps = width // TILE

    def kernel(
        rows_ref, grads_ref, in_ref, out_ref, bias_ref, in_own, out_own,
        in_grad, out_grad, bias_grad, out_bias_grad, made_hbm, back_hbm, in_next, out_next,
        turned, made, back, here, *gather_scratch,
    ):
        step = pl.program_id(0)
        place = Place(nz, nx)
        gather = ExpertGather(place, in_own, out_own, in_next, out_next, *gather_scratch)

        @pl.when(step == 0)
        def _():
            gather.begin()
            place.barrier()
            made[...] = jnp.zeros_like(made)
            back[...] = jnp.zeros_like(back)
            out_bias_grad[...] = jnp.broadcast_to(
                jnp.sum(grads_ref[...].astype(F32), axis=0, keepdims=True), out_bias_grad.shape
            )

        def side(k, spot):
            now = k * 4 + spot
            if now < gather.ticks:
                gather.tick(now)

        expert_step(
            (rows_ref, grads_ref, in_ref, out_ref, bias_ref, in_grad, out_grad, bias_grad, turned, made, back),
            side, steps,
        )

        @pl.when(step == steps - 1)
        def _():
            saves = [
                pltpu.make_async_copy(made, made_hbm, here.at[0]),
                pltpu.make_async_copy(back, back_hbm, here.at[1]),
            ]
            for save in saves:
                save.start()
            for now in range(steps * 4, gather.ticks):
                gather.tick(now)
            for save in saves:
                save.wait()

    inputs, outputs, shapes = expert_specs(count, d, width)
    total = jax.ShapeDtypeStruct((count, d), F32)
    return pl.pallas_call(
        kernel,
        grid=(steps,),
        out_shape=shapes + [jax.ShapeDtypeStruct((8, d), F32), total, total] + full_shapes(nz, nx, in_own, out_own),
        in_specs=inputs + [HBM] * 2,
        out_specs=outputs + [pl.BlockSpec((8, d), lambda step: (0, 0))] + [HBM] * 4,
        scratch_shapes=[
            pltpu.VMEM((d, count), BF16),
            pltpu.VMEM((count, d), F32),
            pltpu.VMEM((count, d), F32),
            pltpu.SemaphoreType.DMA((2,)),
            *expert_gather_scratch(nz, nx),
        ],
        compiler_params=remote_params(3, 62),
        name="experts_first",
    )(rows, grads, in_full, out_full, bias, in_own, out_own)


def experts_second(nz, nx, rows, grads, in_full, out_full, bias, out_bias, made_first, back_first, in_terms, out_terms):
    count, d = rows.shape
    width = in_full.shape[1]
    steps = width // TILE
    buffers, semaphores = expert_reduce_scratch(nz, nx, in_terms, out_terms)

    def kernel(
        rows_ref, grads_ref, in_ref, out_ref, bias_ref, out_bias_ref, made_hbm, back_hbm, in_terms, out_terms,
        in_grad, out_grad, bias_grad, made_rows, back_rows, in_sum, out_sum,
        turned, made, back, result, here, pair_send, pair_recv, *scratch,
    ):
        step = pl.program_id(0)
        place = Place(nz, nx)
        reduce = ExpertReduce(place, in_terms, out_terms, in_sum, out_sum, scratch[:-3], *scratch[-3:])
        half = count // 2

        @pl.when(step == 0)
        def _():
            loads = [
                pltpu.make_async_copy(made_hbm, made, here.at[0]),
                pltpu.make_async_copy(back_hbm, back, here.at[1]),
            ]
            for load in loads:
                load.start()
            place.barrier()
            reduce.tick(0)
            for load in loads:
                load.wait()

        def side(k, spot):
            now = k * 4 + spot
            if 0 < now < reduce.ticks:
                reduce.tick(now)

        expert_step(
            (rows_ref, grads_ref, in_ref, out_ref, bias_ref, in_grad, out_grad, bias_grad, turned, made, back),
            side, steps,
        )

        @pl.when(step == steps - 1)
        def _():
            result[0] = (made[...] + out_bias_ref[0:1, :]).astype(BF16)
            result[1] = back[...].astype(BF16)
            copies = []
            for i, target in enumerate((made_rows, back_rows)):
                copies.append(
                    remote(
                        result.at[i, pl.ds(half, half)], target.at[1], pair_send.at[i], pair_recv.at[i], place.sibling()
                    )
                )
                copies.append(pltpu.make_async_copy(result.at[i, pl.ds(0, half)], target.at[0], here.at[i]))
            for copy in copies:
                copy.start()
            for now in range(steps * 4, reduce.ticks):
                reduce.tick(now)
            for copy in copies:
                copy.wait()

    inputs, outputs, shapes = expert_specs(count, d, width)
    pair = jax.ShapeDtypeStruct((2, count // 2, d), BF16)
    return pl.pallas_call(
        kernel,
        grid=(steps,),
        out_shape=shapes + [pair, pair] + sum_shapes(in_terms, out_terms),
        in_specs=inputs + [pl.BlockSpec((1, d), lambda step: (0, 0))] + [HBM] * 4,
        out_specs=outputs + [HBM] * 4,
        scratch_shapes=[
            pltpu.VMEM((d, count), BF16),
            pltpu.VMEM((count, d), F32),
            pltpu.VMEM((count, d), F32),
            pltpu.VMEM((2, count, d), BF16),
            pltpu.SemaphoreType.DMA((2,)),
            pltpu.SemaphoreType.DMA((2,)),
            pltpu.SemaphoreType.DMA((2,)),
            *buffers,
            *semaphores,
        ],
        compiler_params=remote_params(4, 63),
        name="experts_second",
    )(rows, grads, in_full, out_full, bias, out_bias, made_first, back_first, in_terms, out_terms)


def norm_backward(values, gain, grad):
    scaled, inverse = row_stats(values)
    grad_scaled = grad * gain
    mean = jnp.mean(grad_scaled, axis=-1, keepdims=True)
    along = jnp.mean(grad_scaled * scaled, axis=-1, keepdims=True)
    term = inverse * (grad_scaled - mean - scaled * along)
    return term, jnp.sum(grad * scaled, axis=0, keepdims=True), jnp.sum(grad, axis=0, keepdims=True)


def attend_pair_backward(qkv, head, attended, grad, log_total, projected, turned):
    n, d = attended.shape
    low = lax.broadcasted_iota(jnp.int32, (n, 128), 1) < HEAD
    zero = jnp.zeros((), BF16)

    def columns(part):
        return pl.ds(pl.multiple_of(part * d + head * 128, 128), 128)

    query, key, value = (qkv[:, columns(part)] for part in range(3))
    grad = grad[:, columns(0)]
    product = (attended[:, columns(0)].astype(F32) * grad.astype(F32)).T
    inner = [jnp.sum(product[j * HEAD : (j + 1) * HEAD], axis=0, keepdims=True) for j in range(2)]
    logs = [log_total[head, j : j + 1, :] for j in range(2)]
    key_turned = key.T
    keys = [jnp.where(low, key, zero), jnp.where(low, zero, key)]
    values = [jnp.where(low, value, zero), jnp.where(low, zero, value)]
    low = low[:BLOCK]
    allowed = lax.broadcasted_iota(jnp.int32, (BLOCK, BLOCK), 0) <= lax.broadcasted_iota(
        jnp.int32, (BLOCK, BLOCK), 1
    )
    for i in range(n // BLOCK):
        first, end = i * BLOCK, (i + 1) * BLOCK
        found = []
        for j in range(2):
            grad_key = grad_value = 0.0
            for start, stop in ((first, end), (end, n)):
                if start == stop:
                    continue
                scores = dot_last(keys[j][first:end], query[start:stop])
                weights = jnp.exp2(scores * SCALE_LOG2 - logs[j][:, start:stop])
                if start == first:
                    weights = jnp.where(allowed, weights, 0.0)
                grad_weights = dot_last(values[j][first:end], grad[start:stop])
                grad_scores = (weights * (grad_weights - inner[j][:, start:stop])).astype(BF16)
                grad_value = grad_value + dot(weights.astype(BF16), grad[start:stop])
                grad_key = grad_key + dot(grad_scores, query[start:stop])
                part = dot(key_turned[j * HEAD : (j + 1) * HEAD, first:end], grad_scores)
                if i == 0:
                    turned[j * HEAD : (j + 1) * HEAD, start:stop] = part
                else:
                    turned[j * HEAD : (j + 1) * HEAD, start:stop] += part
            found.append((grad_key, grad_value))
        (key_a, value_a), (key_b, value_b) = found
        projected[first:end, columns(1)] = (jnp.where(low, key_a, key_b) * SCORE_SCALE).astype(BF16)
        projected[first:end, columns(2)] = jnp.where(low, value_a, value_b).astype(BF16)
    projected[:, columns(0)] = (turned[...].T * SCORE_SCALE).astype(BF16)


def attention_backward(
    nz, nx, residual, made_rows, back_rows, slots_turned, cotangent, out_full, vectors, attended, qkv, log_total, normed,
    in_terms, out_terms,
):
    n, d = cotangent.shape
    heads = d // 128
    count = made_rows.shape[0]
    buffers, semaphores = expert_reduce_scratch(nz, nx, in_terms, out_terms)

    def kernel(
        residual_hbm, made_ref, back_ref, slots_ref, cot_ref, wo_ref, vec_ref, att_ref, qkv_ref, logs_ref, normed_ref,
        in_terms, out_terms,
        block_hbm, grad_hbm, projected_hbm, qkv_terms, out_w_terms, sums, in_sum, out_sum,
        block, grad_res, branch, grad_att, turned, projected, wide, here, *scratch,
    ):
        place = Place(nz, nx)
        reduce = ExpertReduce(place, in_terms, out_terms, in_sum, out_sum, scratch[:-3], *scratch[-3:])
        load = pltpu.make_async_copy(residual_hbm, grad_res, here.at[0])
        load.start()
        place.barrier()
        reduce.tick(0)
        sums[...] = jnp.zeros_like(sums)
        load.wait()

        @pl.loop(0, n // BLOCK)
        def _(i):
            rows = pl.ds(pl.multiple_of(i * BLOCK, BLOCK), BLOCK)
            columns = lax.broadcasted_iota(jnp.int32, (BLOCK, MOST), 1)
            chosen = jnp.concatenate(
                [jnp.where(columns == slots_ref[rows, k : k + 1], 1.0, 0.0).astype(BF16) for k in range(2)], axis=1
            )
            values = grad_res[rows]
            block[rows] = (values + dot(chosen, made_ref[...])).astype(BF16)
            grad = dot(chosen, back_ref[...])
            term, gain_sum, shift_sum = norm_backward(values, vec_ref[0:1, d : 2 * d], grad)
            sums[1:2, :] += gain_sum
            sums[3:4, :] += shift_sum
            total = cot_ref[rows].astype(F32) + term
            grad_res[rows] = total
            low = total.astype(BF16)
            branch[rows] = low
            sums[6:7, :] += jnp.sum(low.astype(F32), axis=0, keepdims=True)
            grad_att[rows] = dot_last(low, wo_ref[...]).astype(BF16)
            for k in range(n // BLOCK):
                if k % 2 == 1:
                    @pl.when(i == k)
                    def _(k=k):
                        reduce.tick(1 + k // 2)

        saves = [
            pltpu.make_async_copy(block, block_hbm, here.at[0]),
            pltpu.make_async_copy(grad_res, grad_hbm, here.at[1]),
        ]
        for save in saves:
            save.start()

        @pl.loop(0, heads)
        def _(head):
            attend_pair_backward(qkv_ref, head, att_ref, grad_att, logs_ref, projected, turned)
            for k in range(heads):
                if 3 + k < reduce.ticks:
                    @pl.when(head == k)
                    def _(k=k):
                        reduce.tick(3 + k)

        saves.append(pltpu.make_async_copy(projected, projected_hbm, here.at[2]))
        saves[-1].start()
        written = [pltpu.make_async_copy(wide.at[0], out_w_terms, here.at[3])]
        wide[0] = dot(att_ref[...].T, branch[...]).astype(BF16)
        written[0].start()
        if 3 + heads < reduce.ticks:
            reduce.tick(3 + heads)
        normed_turned = normed_ref[...].T
        for part in range(3):
            columns = slice(part * d, (part + 1) * d)
            spot = (part + 1) % 2
            if part > 0:
                written[part - 1].wait()
            wide[spot] = dot(normed_turned, projected[:, columns]).astype(BF16)
            written.append(
                pltpu.make_async_copy(wide.at[spot], qkv_terms.at[:, pl.ds(part * d, d)], here.at[4 + part])
            )
            written[-1].start()
            if part != 1:
                sums[4 + part // 2 : 5 + part // 2, :] = jnp.sum(
                    projected[:, columns].astype(F32), axis=0, keepdims=True
                )
            if 4 + heads + part < reduce.ticks:
                reduce.tick(4 + heads + part)
        saves += written[2:]
        for now in range(7 + heads, reduce.ticks):
            reduce.tick(now)
        for save in saves:
            save.wait()

    return pl.pallas_call(
        kernel,
        out_shape=[
            jax.ShapeDtypeStruct((n, d), BF16),
            jax.ShapeDtypeStruct((n, d), F32),
            jax.ShapeDtypeStruct((n, 3 * d), BF16),
            jax.ShapeDtypeStruct((d, 3 * d), BF16),
            jax.ShapeDtypeStruct((d, d), BF16),
            jax.ShapeDtypeStruct((8, d), F32),
            *sum_shapes(in_terms, out_terms),
        ],
        in_specs=[HBM] + [VMEM] * 10 + [HBM] * 2,
        out_specs=[HBM] * 5 + [VMEM] + [HBM] * 2,
        scratch_shapes=[
            pltpu.VMEM((n, d), BF16),
            pltpu.VMEM((n, d), F32),
            pltpu.VMEM((n, d), BF16),
            pltpu.VMEM((n, d), BF16),
            pltpu.VMEM((128, n), F32),
            pltpu.VMEM((n, 3 * d), BF16),
            pltpu.VMEM((2, d, d), BF16),
            pltpu.SemaphoreType.DMA((7,)),
            *buffers,
            *semaphores,
        ],
        compiler_params=remote_params(5, 63),
        name="attention_backward",
    )(
        residual, made_rows, back_rows, slots_turned, cotangent, out_full, vectors, attended, qkv, log_total, normed,
        in_terms, out_terms,
    )


def last_sums(nz, nx, projected, qkv_full, grad_res, tokens, vectors, small, qkv_terms, out_terms):
    n, d = tokens.shape
    depth = qkv_terms.shape[3]
    buffers = []
    for _ in range(4):
        buffers += reduce_buffers(nz, nx, (depth, d), True)
    size = len(buffers) // 4
    partners = nz.bit_length() - 1 + nx.bit_length() - 1 + 1

    def kernel(
        projected_ref, w_ref, grad_ref, tokens_ref, vec_ref, small_ref, qkv_terms, out_terms,
        input_grad, small_sum, qkv_sum, out_sum,
        terms, landing, small_send, small_recv, *scratch,
    ):
        place = Place(nz, nx)

        def piece(i):
            if i == 3:
                return lambda zs, xs, core: out_terms.at[zs, xs, core], scratch[3 * size : 4 * size], out_sum
            columns = pl.ds(i * d, d)
            return (
                lambda zs, xs, core: qkv_terms.at[zs, xs, core, :, columns],
                scratch[i * size : (i + 1) * size],
                qkv_sum.at[:, columns],
            )

        reduce = Reduce(place, [piece(i) for i in (3, 0, 1, 2)], True, *scratch[-3:])
        total = Total(place, terms, landing, small_send, small_recv)
        place.barrier()
        reduce.tick(0)
        terms[0] = small_ref[...]

        @pl.loop(0, n // BLOCK)
        def _(i):
            rows = pl.ds(pl.multiple_of(i * BLOCK, BLOCK), BLOCK)
            grad = dot_last(projected_ref[rows], w_ref[...])
            term, gain_sum, shift_sum = norm_backward(tokens_ref[rows].astype(F32), vec_ref[0:1, :d], grad)
            input_grad[rows] = grad_ref[rows] + term
            terms[0, 0:1, :] += gain_sum
            terms[0, 2:3, :] += shift_sum
            for k in range(n // BLOCK):
                @pl.when(i == k)
                def _(k=k):
                    reduce.tick(1 + k)

        stage = 0
        for now in range(1 + n // BLOCK, reduce.ticks):
            if stage < total.stages:
                total.begin(stage)
            reduce.tick(now)
            if stage < total.stages:
                total.finish(stage)
                stage += 1
        for late in range(stage, total.stages):
            total.begin(late)
            total.finish(late)
        small_sum[...] = terms[total.stages]

    shape = small.shape
    return pl.pallas_call(
        kernel,
        out_shape=[
            jax.ShapeDtypeStruct((n, d), F32),
            jax.ShapeDtypeStruct(shape, F32),
            jax.ShapeDtypeStruct((depth, 3 * d), BF16),
            jax.ShapeDtypeStruct((depth, d), BF16),
        ],
        in_specs=[VMEM] * 6 + [HBM] * 2,
        out_specs=[VMEM] * 2 + [HBM] * 2,
        scratch_shapes=[
            pltpu.VMEM((partners + 1,) + shape, F32),
            pltpu.VMEM((partners,) + shape, F32),
            pltpu.SemaphoreType.DMA((partners,)),
            pltpu.SemaphoreType.DMA((partners,)),
            *buffers,
            *reduce_semaphores(nz, nx, 4),
        ],
        compiler_params=remote_params(6, 60),
        name="last_sums",
    )(projected, qkv_full, grad_res, tokens, vectors, small, qkv_terms, out_terms)


def shards(
    nz, nx, tokens, norm_gain, norm_bias, w_qkv, attn_bias, w_attn_out, expert_in, expert_in_bias, expert_out,
    expert_out_bias, expert_ids, running_load, cotangent,
):
    n, d = tokens.shape
    devices = nz * nx * 2
    core = lax.axis_index("core")
    me = lax.axis_index(("dp", "xy", "core"))
    share = norm_gain.shape[1]
    in_depth, width = expert_in.shape[1:]
    out_depth = expert_out.shape[1]
    part = out_depth // CHUNKS

    ids = expert_ids[:, 0]
    second = (ids == 1).astype(jnp.int32)
    before = jnp.cumsum(second)
    count_second = before[-1]
    rank = jnp.where(ids == 1, before - 1, jnp.arange(n, dtype=jnp.int32) - before)
    own = ids == core
    slots = jnp.stack([jnp.where(own, rank, -1), jnp.where(own, -1, rank)])
    slots = jnp.concatenate([slots, jnp.full((6, n), -1, jnp.int32)])
    slots_turned = slots.T

    digits = jnp.stack([count_second // 32, count_second % 32]).astype(BF16)
    small = jnp.concatenate(
        [
            norm_gain.reshape(-1),
            norm_bias.reshape(-1),
            attn_bias.reshape(-1),
            expert_out_bias.reshape(-1),
            expert_in_bias.reshape(-1),
            digits,
        ]
    )
    used = 9 * share + 2 * out_depth
    small = jnp.concatenate([small, jnp.zeros((2048 - used - 2,), BF16)]).reshape(16, 128)

    qkv_full, out_full, small_full, grad_rows = attention_weights(
        nz, nx, w_qkv, w_attn_out, small, cotangent, slots
    )
    qkv_full = qkv_full.reshape(d, 3 * d)
    out_full = out_full.reshape(d, d)
    small_full = small_full.reshape(devices, 2048)
    rows = small_full[:, : 9 * share].reshape(devices, 9, share).transpose(1, 0, 2).reshape(9, d).astype(F32)
    none = jnp.zeros((d,), F32)
    vectors = jnp.concatenate(
        [
            jnp.stack(
                [
                    jnp.concatenate([rows[0], rows[1], rows[6]]),
                    jnp.concatenate([rows[2], rows[3], none]),
                    jnp.concatenate([rows[4], none, rows[5]]),
                ]
            ),
            jnp.zeros((5, 3 * d), F32),
        ]
    )
    out_bias = lax.dynamic_slice_in_dim(rows, 7 + core, 1)
    in_bias = small_full[:, 9 * share : used].reshape(devices, EXPERTS, CHUNKS, part)
    in_bias = lax.dynamic_index_in_dim(in_bias, core, 1, keepdims=False)
    in_bias = in_bias.transpose(1, 0, 2).reshape(CHUNKS, 1, devices * part).astype(F32)
    counts = small_full[:, used : used + 2].astype(jnp.int32)
    total_second = jnp.sum(counts[:, 0] * 32 + counts[:, 1])
    expert_counts = jnp.stack([n * devices - total_second, total_second])
    expert_load = 0.9 * running_load + 0.1 * (expert_counts.astype(F32) * EXPERTS / (n * devices))

    in_own = expert_in.reshape(EXPERTS, in_depth, devices, CHUNKS, part).transpose(3, 0, 1, 2, 4)
    in_own = in_own.reshape(CHUNKS, EXPERTS, in_depth, devices * part)
    out_own = expert_out.reshape(EXPERTS, CHUNKS, part, d)

    normed, qkv, attended, log_total, residual, picked, in_a, out_a = attention_forward(
        nz, nx, tokens, qkv_full, out_full, vectors, slots, in_own[0], out_own[:, 0]
    )
    picked = picked.reshape(2 * MOST, d)
    grad_rows = grad_rows.reshape(2 * MOST, d)
    wide = (d, devices * part)
    tall = (devices * part, d)
    in_grad_a, out_grad_a, bias_grad_a, out_bias_grad, made, back, in_b, out_b = experts_first(
        nz, nx, picked, grad_rows, in_a.reshape(wide), out_a.reshape(tall), in_bias[0], in_own[1], out_own[:, 1]
    )
    in_split = (nz, nx, 2, in_depth, devices * part)
    out_split = (nz, nx, 2, part, d)
    in_grad_b, out_grad_b, bias_grad_b, made_rows, back_rows, in_sum_a, out_sum_a = experts_second(
        nz, nx, picked, grad_rows, in_b.reshape(wide), out_b.reshape(tall), in_bias[1], out_bias, made, back,
        in_grad_a.reshape(in_split), out_grad_a.reshape(out_split),
    )
    block_out, grad_res, projected, qkv_terms, out_terms, sums, in_sum_b, out_sum_b = attention_backward(
        nz, nx, residual, made_rows.reshape(2 * MOST, d), back_rows.reshape(2 * MOST, d), slots_turned, cotangent,
        out_full, vectors, attended, qkv, log_total, normed,
        in_grad_b.reshape(in_split), out_grad_b.reshape(out_split),
    )
    bias_rows = jnp.concatenate([bias_grad_a, bias_grad_b], axis=1).reshape(-1, d)
    lines = bias_rows.shape[0]
    small_terms = jnp.concatenate([sums, jnp.zeros((2 + 2 * lines + (-(2 + 2 * lines)) % 8, d), F32)])
    small_terms = lax.dynamic_update_slice(small_terms, out_bias_grad[:1], (8 + core, 0))
    small_terms = lax.dynamic_update_slice(small_terms, bias_rows, (10 + lines * core, 0))
    input_grad, small_sum, qkv_sum, out_sum = last_sums(
        nz, nx, projected, qkv_full, grad_res, tokens, vectors, small_terms,
        qkv_terms.reshape(nz, nx, 2, d // devices, 3 * d), out_terms.reshape(nz, nx, 2, d // devices, d),
    )
    mine = lax.dynamic_slice_in_dim(small_sum[:10], me * share, share, axis=1)
    bias_sum = small_sum[10 : 10 + 2 * lines].reshape(EXPERTS, CHUNKS, devices * part)
    bias_sum = lax.dynamic_slice_in_dim(bias_sum, me * part, part, axis=2).reshape(EXPERTS, out_depth)
    in_sum = jnp.stack([in_sum_a, in_sum_b]).reshape(CHUNKS, EXPERTS, in_depth, devices, part)
    in_sum = in_sum.transpose(1, 2, 3, 0, 4).reshape(EXPERTS, in_depth, width).astype(F32)
    out_sum_experts = jnp.concatenate([out_sum_a, out_sum_b], axis=1).astype(F32)
    return (
        block_out,
        input_grad,
        mine[0:2],
        mine[2:4],
        qkv_sum.astype(F32),
        mine[4:7],
        out_sum.astype(F32),
        in_sum,
        bias_sum,
        out_sum_experts,
        mine[8:10],
        expert_counts,
        expert_load,
    )


def solution(mesh):
    nz, nx = mesh.shape["dp"], mesh.shape["fsdp"] // 2
    fine = Mesh(mesh.devices.reshape(nz, nx, 2), ("dp", "xy", "core"))
    every = ("dp", "xy", "core")
    row, column, middle = P(every, None), P(None, every), P(None, every, None)
    return jax.shard_map(
        functools.partial(shards, nz, nx),
        mesh=fine,
        in_specs=(
            row, column, column, row, column, row, middle, column, middle, column, row, P(), row,
        ),
        out_specs=(row, row, column, column, row, column, row, middle, column, middle, column, P(), P()),
        check_vma=False,
    )
```

```python
import functools
import math

import jax
import jax.numpy as jnp
from jax import lax
from jax.experimental import pallas as pl
from jax.experimental.pallas import tpu as pltpu
from jax.sharding import Mesh, PartitionSpec as P

BF16 = jnp.bfloat16
F32 = jnp.float32
MESH_ID = pl.DeviceIdType.MESH

HEAD = 64
MOST = 640
EXPERTS = 2
CHUNKS = 2
CUTS = 4
AHEAD = 1
NORM_EPS = 1e-05
SCORE_SCALE = 0.125
SCALE_LOG2 = SCORE_SCALE * math.log2(math.e)
MASKED = -1e30
BLOCK = 256
MIB = 1 << 20
ALL = slice(None)
HBM = pl.BlockSpec(memory_space=pl.ANY)
VMEM = pl.BlockSpec(memory_space=pltpu.VMEM)


def dot(left, right):
    return lax.dot_general(left, right, (((1,), (0,)), ((), ())), preferred_element_type=F32)


def dot_last(left, right):
    return lax.dot_general(left, right, (((1,), (1,)), ((), ())), preferred_element_type=F32)


def row_stats(values):
    center = values - jnp.mean(values, axis=-1, keepdims=True)
    spread = jnp.mean(center * center, axis=-1, keepdims=True)
    inverse = lax.rsqrt(spread + NORM_EPS)
    return center * inverse, inverse


def as_rows(values, rows):
    if values.dtype == BF16 and values.shape[-2] % 16:
        return values.astype(F32).reshape(rows, values.shape[-1]).astype(BF16)
    return values.reshape(rows, values.shape[-1])


def split_rows(values, shape):
    if values.dtype == BF16 and shape[-2] % 16:
        return values.astype(F32).reshape(shape).astype(BF16)
    return values.reshape(shape)


class Place:
    def __init__(self, nz, nx):
        self.nz, self.nx = nz, nx
        self.bits_z, self.bits_x = nz.bit_length() - 1, nx.bit_length() - 1
        self.z, self.xy, self.core = lax.axis_index("dp"), lax.axis_index("xy"), lax.axis_index("core")
        self.flip_z = [(1 - 2 * lax.rem(lax.div(self.z, 2**k), 2)) * 2**k for k in range(self.bits_z)]
        self.flip_x = [(1 - 2 * lax.rem(lax.div(self.xy, 2**k), 2)) * 2**k for k in range(self.bits_x)]

    def step_x(self, k, core=None):
        core = self.core if core is None else core
        return (1 - core) * self.flip_x[k] + core * self.flip_x[self.bits_x - 1 - k]

    def span_x(self, which, core=None):
        return self.xy + sum(self.step_x(k, core) for k in range(self.bits_x) if which >> k & 1)

    def span_z(self, which):
        return self.z + sum(self.flip_z[k] for k in range(self.bits_z) if which >> k & 1)

    def partners(self):
        found = [(self.z + flip, self.xy, self.core) for flip in self.flip_z]
        found += [(self.z, self.xy + flip, self.core) for flip in self.flip_x]
        return found + [self.sibling()]

    def sibling(self):
        return (self.z, self.xy, 1 - self.core)

    def barrier(self):
        semaphore = pltpu.get_barrier_semaphore()
        partners = self.partners()
        for partner in partners:
            pl.semaphore_signal(semaphore, inc=1, device_id=partner, device_id_type=MESH_ID)
        pl.semaphore_wait(semaphore, len(partners))


class Copies:
    def __init__(self, send, recv, near):
        self.send, self.recv, self.near = send, recv, near
        self.far_names, self.near_names = {}, {}

    def far(self, name, src, dst, device):
        i = self.far_names.setdefault(name, len(self.far_names))
        return pltpu.make_async_remote_copy(
            src_ref=src, dst_ref=dst, send_sem=self.send.at[i], recv_sem=self.recv.at[i],
            device_id=device, device_id_type=MESH_ID,
        )

    def local(self, name, src, dst, slot=None):
        if slot is not None:
            self.near_names.setdefault((name, 0), len(self.near_names))
            self.near_names.setdefault((name, 1), len(self.near_names))
            return pltpu.make_async_copy(src, dst, self.near.at[self.near_names[name, 0] + slot])
        i = self.near_names.setdefault(name, len(self.near_names))
        return pltpu.make_async_copy(src, dst, self.near.at[i])


def semaphores(far, near):
    return [
        pltpu.SemaphoreType.DMA((far,)),
        pltpu.SemaphoreType.DMA((far,)),
        pltpu.SemaphoreType.DMA((near,)),
    ]


class Stream:
    def __init__(self, pieces):
        self.pieces = pieces

    def tick(self, now):
        for stage in range(max(self.stages(p) for p in self.pieces) - 1, 0, -1):
            piece = now - stage
            if 0 <= piece < len(self.pieces) and stage < self.stages(self.pieces[piece]):
                self.finish(piece, stage - 1)
                self.begin(piece, stage)
        for piece in range(0 if now == 0 else now + AHEAD, now + AHEAD + 1):
            if piece < len(self.pieces):
                self.begin(piece, 0)

    def need(self, piece):
        self.finish(piece, self.stages(self.pieces[piece]) - 1)


class Gather(Stream):
    def __init__(self, name, place, copies, pieces):
        super().__init__(pieces)
        self.name, self.place, self.made = name, place, copies

    def stages(self, piece):
        return self.place.bits_z + self.place.bits_x + (piece[1] is not None)

    def copies(self, piece, stage):
        place = self.place
        region, to_sibling = self.pieces[piece]
        found = []
        if stage < place.bits_z:
            bit = place.bits_z - 1 - stage
            device = (place.z + place.flip_z[bit], place.xy, place.core)
            for held in range(2**stage):
                found += [(ref, device) for ref in region(place.span_z(held << (bit + 1)), place.xy)]
        elif stage < place.bits_z + place.bits_x:
            step = stage - place.bits_z
            device = (place.z, place.xy + place.step_x(step), place.core)
            for held in range(2**step):
                found += [(ref, device) for ref in region(ALL, place.span_x(held))]
        else:
            found += [(ref, place.sibling()) for ref in to_sibling]
        return [
            self.made.far((self.name, piece, stage, i), ref, ref, device) for i, (ref, device) in enumerate(found)
        ]

    def begin(self, piece, stage):
        for copy in self.copies(piece, stage):
            copy.start()

    def finish(self, piece, stage):
        for copy in self.copies(piece, stage):
            copy.wait()


class Reduce(Stream):
    def __init__(self, name, place, copies, pieces):
        super().__init__(pieces)
        self.name, self.place, self.made = name, place, copies

    def stages(self, piece):
        return self.place.bits_z + self.place.bits_x + 1

    def plan(self, piece, stage):
        place = self.place
        source, landing, spare, target, owner = self.pieces[piece]
        acc = landing[0]
        nx, bits_x = place.nx, place.bits_x
        far, near, sums = [], [], []
        slot = stage
        if owner == "first":
            if stage == 0:
                for r in range(nx):
                    there = 1 - place.core
                    far.append((source(ALL, place.span_x(r, there), there), acc.at[r], place.sibling()))
                    near.append((source(ALL, place.span_x(r), place.core), spare.at[r]))
                    sums.append((acc.at[r], spare.at[r]))
                return far, near, sums
            stage -= 1
        if stage < bits_x:
            k = bits_x - 1 - stage
            device = (place.z, place.xy + place.step_x(k), place.core)
            if slot == 0:
                for j in range(2**k):
                    far.append((source(ALL, place.span_x(2**k + j), place.core), acc.at[j], device))
                    near.append((source(ALL, place.span_x(j), place.core), spare.at[j]))
                    sums.append((acc.at[j], spare.at[j]))
            else:
                far.append((acc.at[pl.ds(2**k, 2**k)], landing[slot], device))
                sums += [(acc.at[j], landing[slot].at[j]) for j in range(2**k)]
        else:
            bit = stage - bits_x
            device = (place.z + place.flip_z[bit], place.xy, place.core)
            for s in range(2 ** (place.bits_z - 1 - bit)):
                upper = s << (bit + 1)
                far.append((acc.at[0, place.span_z(upper + 2**bit)], landing[slot].at[s], device))
                sums.append((acc.at[0, place.span_z(upper)], landing[slot].at[s]))
        return far, near, sums

    def made_copies(self, piece, stage, far, near):
        made = [
            self.made.far((self.name, piece, stage, i), src, dst, device) for i, (src, dst, device) in enumerate(far)
        ]
        return made + [self.made.local((self.name, piece, stage, i), src, dst) for i, (src, dst) in enumerate(near)]

    def last(self, piece, begin):
        place, core = self.place, self.place.core
        _, landing, _, target, owner = self.pieces[piece]
        mine = landing[0].at[0, place.z]
        name = (self.name, piece, "last")
        if owner == "both":
            there = self.made.far(name, mine.at[1 - core], target(core), place.sibling())
            here = self.made.local(name, mine.at[core], target(core))
            for copy in (there, here):
                copy.start() if begin else copy.wait()
            return
        there = self.made.far(name, mine, target(core), place.sibling())
        here = self.made.local(name, mine, target(core))

        @pl.when(core == owner)
        def _():
            if begin:
                here.start()
            else:
                here.wait()
                there.wait_recv()

        @pl.when(core != owner)
        def _():
            there.start() if begin else there.wait_send()

    def begin(self, piece, stage):
        if stage == self.stages(self.pieces[piece]) - 1 and self.pieces[piece][4] != "first":
            self.last(piece, True)
            return
        far, near, _ = self.plan(piece, stage)
        for copy in self.made_copies(piece, stage, far, near):
            copy.start()

    def finish(self, piece, stage):
        owner = self.pieces[piece][4]
        final = stage == self.stages(self.pieces[piece]) - 1
        if final and owner != "first":
            self.last(piece, False)
            return
        far, near, sums = self.plan(piece, stage)
        for copy in self.made_copies(piece, stage, far, near):
            copy.wait()
        for total, landed in sums:
            if len(total.shape) > 3 or (owner == "first" and len(total.shape) > 2):
                @pl.loop(0, total.shape[0])
                def _(i, total=total, landed=landed):
                    total[i] = (total[i].astype(F32) + landed[i].astype(F32)).astype(BF16)
            else:
                total[...] = (total[...].astype(F32) + landed[...].astype(F32)).astype(BF16)
        if final:
            here = self.made.local((self.name, piece, "last"), self.pieces[piece][1][0].at[0, self.place.z], self.pieces[piece][3])
            here.start()
            here.wait()


def landing_shapes(nz, nx, tail, first):
    bits_z, bits_x = nz.bit_length() - 1, nx.bit_length() - 1
    shapes = [(nx, nz) + tail] if first else []
    shapes += [(2**k, nz) + tail for k in reversed(range(bits_x))]
    return shapes + [(2 ** (bits_z - 1 - bit),) + tail for bit in range(bits_z)]


class Total:
    def __init__(self, place, copies, terms, landing):
        self.place, self.made, self.terms, self.landing = place, copies, terms, landing
        self.stages = len(place.partners())

    def copy(self, stage):
        device = self.place.partners()[stage]
        return self.made.far(("total", stage), self.terms.at[stage], self.landing.at[stage], device)

    def begin(self, stage):
        self.copy(stage).start()

    def finish(self, stage):
        self.copy(stage).wait()
        self.terms[stage + 1] = self.terms[stage] + self.landing[stage]


def one_hot(slots, count):
    rows = lax.broadcasted_iota(jnp.int32, (count, slots.shape[1]), 0)
    return jnp.where(rows == slots, 1.0, 0.0).astype(BF16)


def pick_rows(picked, slots, values):
    picked[...] = dot(one_hot(slots, picked.shape[0]), values).astype(BF16)


def find_slots(slots, ids_ref, core):
    n = ids_ref.shape[1]
    ids = ids_ref[...]
    second = jnp.where(ids == 1, 1.0, 0.0)
    earlier = lax.broadcasted_iota(jnp.int32, (n, n), 0) <= lax.broadcasted_iota(jnp.int32, (n, n), 1)
    before = dot(
        jnp.broadcast_to(second, (16, n)).astype(BF16), jnp.where(earlier, 1.0, 0.0).astype(BF16)
    )[0:1].astype(jnp.int32)
    rank = jnp.where(ids == 1, before - 1, lax.broadcasted_iota(jnp.int32, (1, n), 1) - before)
    own = ids == core
    slots[0:1, :] = jnp.where(own, rank, -1)
    slots[1:2, :] = jnp.where(own, -1, rank)
    slots[2:8, :] = jnp.full((6, n), -1, jnp.int32)
    return jnp.sum(second, axis=1, keepdims=True)


GAIN, SHIFT, ATTN_BIAS, OUT_BIAS, IN_BIAS, DIGITS = 0, 2, 4, 7, 9, 11


def pack_small(small, refs, count_second):
    small[...] = jnp.zeros_like(small)
    for row, ref in zip((GAIN, SHIFT, ATTN_BIAS, OUT_BIAS, IN_BIAS), refs):
        count, share = ref.shape
        small[row : row + count, :share] = ref[...].astype(F32)
    high = jnp.floor(count_second * (1 / 32))
    lane = lax.broadcasted_iota(jnp.int32, (1, 128), 1)
    small[DIGITS : DIGITS + 1, :] = jnp.where(lane == 0, high, jnp.where(lane == 1, count_second - 32 * high, 0.0))


def spread(shares, length, share, place_of):
    devices = shares.shape[0]
    lanes = lax.broadcasted_iota(jnp.int32, (128, length), 1)
    repeat = jnp.where(lax.rem(lanes, share) == lax.broadcasted_iota(jnp.int32, (128, length), 0), 1.0, 0.0)
    copies = dot(shares, repeat.astype(BF16))
    lanes = lax.broadcasted_iota(jnp.int32, (devices, length), 1)
    device = lax.broadcasted_iota(jnp.int32, (devices, length), 0)
    return jnp.sum(jnp.where(lax.div(lanes, share) == place_of(device), copies, 0.0), axis=0, keepdims=True)


def unpack_small(small_full, core, d, share, hidden_share, vectors, in_bias, out_bias, counts):
    nz, nx = small_full.shape[:2]
    devices = nz * nx * 2
    found = small_full[...].astype(F32).reshape(devices, 16, 128)

    def rows(row):
        return found[:, row, :].astype(BF16)

    def vector(shares):
        return spread(shares, d, share, lambda device: device)

    vectors[...] = jnp.zeros_like(vectors)
    for line, row, part in (
        (0, GAIN, 0), (0, GAIN + 1, 1), (0, ATTN_BIAS + 2, 2), (1, SHIFT, 0), (1, SHIFT + 1, 1),
        (2, ATTN_BIAS, 0), (2, ATTN_BIAS + 1, 2),
    ):
        vectors[line : line + 1, part * d : (part + 1) * d] = vector(rows(row))

    def of_expert(row):
        return jnp.where(core == 0, rows(row), rows(row + 1))

    out_bias[0:1, :] = vector(of_expert(OUT_BIAS))
    width = hidden_share * devices // CHUNKS
    tile = in_bias.shape[2]
    for chunk in range(CHUNKS):
        line = spread(
            of_expert(IN_BIAS), width, hidden_share,
            lambda device: jnp.where(lax.rem(device, 2) == chunk, lax.div(device, 2), -1),
        )
        for i in range(width // tile):
            in_bias[chunk * (width // tile) + i, 0:1, :] = line[:, i * tile : (i + 1) * tile]
    counts[...] = jnp.broadcast_to(jnp.sum(found[:, DIGITS, :], axis=0, keepdims=True), counts.shape)


def attend_pair(qkv, head, attended, log_total):
    n, d = attended.shape
    low = lax.broadcasted_iota(jnp.int32, (n, 128), 1) < HEAD
    one, zero = jnp.ones((), BF16), jnp.zeros((), BF16)
    query = qkv[:, pl.ds(pl.multiple_of(head * 128, 128), 128)]
    key = qkv[:, pl.ds(pl.multiple_of(d + head * 128, 128), 128)]
    value = qkv[:, pl.ds(pl.multiple_of(2 * d + head * 128, 128), 128)]
    values = [jnp.where(low, value, one), jnp.where(low, one, value)]
    queries = [jnp.where(low, query, zero), jnp.where(low, zero, query)]
    low = low[:BLOCK]
    allowed = lax.broadcasted_iota(jnp.int32, (BLOCK, BLOCK), 1) <= lax.broadcasted_iota(
        jnp.int32, (BLOCK, BLOCK), 0
    )
    for i in range(n // BLOCK):
        first, end = i * BLOCK, (i + 1) * BLOCK
        found = []
        for j in range(2):
            near = jnp.where(allowed, dot_last(queries[j][first:end], key[first:end]), MASKED)
            top = jnp.max(near, axis=-1, keepdims=True)
            if i:
                far = dot_last(queries[j][first:end], key[:first])
                top = jnp.maximum(top, jnp.max(far, axis=-1, keepdims=True))
            top = top * SCALE_LOG2
            out = dot(jnp.exp2(near * SCALE_LOG2 - top).astype(BF16), values[j][first:end])
            if i:
                out = out + dot(jnp.exp2(far * SCALE_LOG2 - top).astype(BF16), values[j][:first])
            found.append((out, top))
        (out_a, top_a), (out_b, top_b) = found
        total = pltpu.roll(jnp.where(low, out_b, out_a), HEAD, axis=1)
        attended[first:end, pl.ds(pl.multiple_of(head * 128, 128), 128)] = (
            jnp.where(low, out_a, out_b) / total
        ).astype(BF16)
        logs = (jnp.where(low, top_a, top_b) + jnp.log2(total)).T
        log_total[head, 0:1, first:end] = logs[0:1]
        log_total[head, 1:2, first:end] = logs[HEAD : HEAD + 1]


def gelu_and_slope(values):
    root = math.sqrt(2 / math.pi)
    cube = 0.044715
    square = values * values
    bent = jnp.tanh(values * (root + root * cube * square))
    half = 0.5 * (1 + bent)
    slope = half + 0.5 * values * (1 - bent * bent) * (root + 3 * root * cube * square)
    return values * half, slope


def norm_backward(values, gain, grad):
    scaled, inverse = row_stats(values)
    grad_scaled = grad * gain
    mean = jnp.mean(grad_scaled, axis=-1, keepdims=True)
    along = jnp.mean(grad_scaled * scaled, axis=-1, keepdims=True)
    term = inverse * (grad_scaled - mean - scaled * along)
    return term, jnp.sum(grad * scaled, axis=0, keepdims=True), jnp.sum(grad, axis=0, keepdims=True)


def attend_pair_backward(qkv, head, attended, grad, log_total, projected, turned):
    n, d = attended.shape
    low = lax.broadcasted_iota(jnp.int32, (n, 128), 1) < HEAD
    zero = jnp.zeros((), BF16)

    def columns(part):
        return pl.ds(pl.multiple_of(part * d + head * 128, 128), 128)

    query, key, value = (qkv[:, columns(part)] for part in range(3))
    grad = grad[:, columns(0)]
    product = (attended[:, columns(0)].astype(F32) * grad.astype(F32)).T
    inner = [jnp.sum(product[j * HEAD : (j + 1) * HEAD], axis=0, keepdims=True) for j in range(2)]
    logs = [log_total[head, j : j + 1, :] for j in range(2)]
    key_turned = key.T
    keys = [jnp.where(low, key, zero), jnp.where(low, zero, key)]
    values = [jnp.where(low, value, zero), jnp.where(low, zero, value)]
    low = low[:BLOCK]
    allowed = lax.broadcasted_iota(jnp.int32, (BLOCK, BLOCK), 0) <= lax.broadcasted_iota(
        jnp.int32, (BLOCK, BLOCK), 1
    )
    for i in range(n // BLOCK):
        first, end = i * BLOCK, (i + 1) * BLOCK
        found = []
        for j in range(2):
            grad_key = grad_value = 0.0
            for start, stop in ((first, end), (end, n)):
                if start == stop:
                    continue
                scores = dot_last(keys[j][first:end], query[start:stop])
                weights = jnp.exp2(scores * SCALE_LOG2 - logs[j][:, start:stop])
                if start == first:
                    weights = jnp.where(allowed, weights, 0.0)
                grad_weights = dot_last(values[j][first:end], grad[start:stop])
                grad_scores = (weights * (grad_weights - inner[j][:, start:stop])).astype(BF16)
                grad_value = grad_value + dot(weights.astype(BF16), grad[start:stop])
                grad_key = grad_key + dot(grad_scores, query[start:stop])
                part = dot(key_turned[j * HEAD : (j + 1) * HEAD, first:end], grad_scores)
                if i == 0:
                    turned[j * HEAD : (j + 1) * HEAD, start:stop] = part
                else:
                    turned[j * HEAD : (j + 1) * HEAD, start:stop] += part
            found.append((grad_key, grad_value))
        (key_a, value_a), (key_b, value_b) = found
        projected[first:end, columns(1)] = (jnp.where(low, key_a, key_b) * SCORE_SCALE).astype(BF16)
        projected[first:end, columns(2)] = jnp.where(low, value_a, value_b).astype(BF16)
    projected[:, columns(0)] = (turned[...].T * SCORE_SCALE).astype(BF16)


def block_kernel(nz, nx, tokens, cotangent, ids, small, w_qkv, w_out, in_own, hidden_own):
    n, d = tokens.shape
    heads = d // 128
    depth = w_qkv.shape[0]
    share = small[0].shape[1]
    hidden_share = hidden_own.shape[1]
    width = in_own.shape[3]
    tile = nx * hidden_share
    tiles = width // tile
    count = 2 * MOST
    cut = width // CUTS
    hidden_cut = hidden_share // CUTS
    in_tail, hidden_tail = (2, depth, cut), (hidden_cut, d)
    small_rows = 10 + EXPERTS * CHUNKS * (width // d)
    small_rows += -small_rows % 8

    def bf16(*shape):
        return jax.ShapeDtypeStruct(shape, BF16)

    def f32(*shape):
        return jax.ShapeDtypeStruct(shape, F32)

    outputs = dict(
        block_out=bf16(n, d),
        grad_res=f32(n, d),
        projected=bf16(n, 3 * d),
        qkv_terms=bf16(nz, nx, 2, depth, 3 * d),
        wo_terms=bf16(nz, nx, 2, depth, d),
        in_sum=bf16(CHUNKS, EXPERTS, depth, width),
        hidden_sum=bf16(EXPERTS, hidden_share, d),
        qkv_full=bf16(nz, nx, 2, depth, 3 * d),
        wo_full=bf16(nz, nx, 2, depth, d),
        grad_rows=bf16(2, MOST, d),
        rows=bf16(2, MOST, d),
        made_rows=bf16(2, MOST, d),
        back_rows=bf16(2, MOST, d),
        in_full=bf16(CHUNKS, nz, nx, 2, depth, width),
        hidden_full=bf16(CHUNKS, nz, nx, hidden_share, d),
        in_terms=bf16(CHUNKS, nz, nx, 2, depth, width),
        hidden_terms=bf16(CHUNKS, nz, nx, hidden_share, d),
        normed=bf16(n, d),
        qkv=bf16(n, 3 * d),
        attended=bf16(n, d),
        logs=f32(heads, 8, n),
        residual=f32(n, d),
    )
    small_outputs = dict(small_terms=f32(small_rows, d), vectors=f32(8, 3 * d), counts=f32(8, 128))

    landings = []
    for _ in range(CHUNKS):
        landings += [landing_shapes(nz, nx, in_tail, False)] * CUTS
        landings += [landing_shapes(nz, nx, hidden_tail, False)] * CUTS
    per_piece = len(landings[0])
    landing_scratch = [pltpu.VMEM(shape, BF16) for shapes in landings for shape in shapes]
    spares = [pltpu.VMEM((2,) + landings[0][0], BF16), pltpu.VMEM((2,) + landings[CUTS][0], BF16)]

    names = list(outputs) + list(small_outputs)

    def kernel(*refs):
        (
            tokens_hbm, cot_hbm, ids_ref, gain_ref, shift_ref, attn_bias_ref, out_bias_ref, in_bias_ref,
            qkv_own, wo_own, in_own, hidden_own,
        ) = refs[:12]
        out = dict(zip(names, refs[12 : 12 + len(names)]))
        rest = refs[12 + len(names) :]
        slots, small_own, small_full, in_bias, out_bias, bias_sums = rest[:6]
        spare_in, spare_hidden = rest[6:8]
        landing = rest[8 : 8 + len(landing_scratch)]
        made = Copies(*rest[8 + len(landing_scratch) :])

        place = Place(nz, nx)
        z, xy, core = place.z, place.xy, place.core
        vectors, sums = out["vectors"], out["small_terms"]

        def columns_of(ref, part):
            return lambda zs, xs: [ref.at[zs, xs, core, :, pl.ds(part * d, d)]]

        def with_small(zs, xs):
            return [out["qkv_full"].at[zs, xs, core, :, pl.ds(2 * d, d)], small_full.at[zs, xs, core]]

        regions = [columns_of(out["qkv_full"], 0), columns_of(out["qkv_full"], 1), with_small, columns_of(out["wo_full"], 0)]
        gathered = [(region, region(ALL, ALL)) for region in regions]
        for chunk in range(CHUNKS):
            for i in range(CUTS):
                gathered.append(
                    (lambda zs, xs, chunk=chunk, i=i: [out["in_full"].at[chunk, zs, xs, :, :, pl.ds(i * cut, cut)]], None)
                )
            for i in range(CUTS):
                gathered.append(
                    (
                        lambda zs, xs, chunk=chunk, i=i: [
                            out["hidden_full"].at[chunk, zs, xs, pl.ds(i * hidden_cut, hidden_cut)]
                        ],
                        None,
                    )
                )
        gather = Gather("gather", place, made, gathered)

        pieces = []
        for chunk in range(CHUNKS):
            for i in range(2 * CUTS):
                at = len(pieces)
                mine = landing[at * per_piece : (at + 1) * per_piece]
                if i < CUTS:
                    at_columns = pl.ds(i * cut, cut)
                    pieces.append(
                        (
                            lambda zs, xs, _, c=chunk, s=at_columns: out["in_terms"].at[c, zs, xs, :, :, s],
                            mine,
                            spare_in.at[at % 2],
                            lambda expert, c=chunk, s=at_columns: out["in_sum"].at[c, expert, :, s],
                            "both",
                        )
                    )
                else:
                    at_rows = pl.ds((i - CUTS) * hidden_cut, hidden_cut)
                    pieces.append(
                        (
                            lambda zs, xs, _, c=chunk, s=at_rows: out["hidden_terms"].at[c, zs, xs, s],
                            mine,
                            spare_hidden.at[at % 2],
                            lambda expert, s=at_rows: out["hidden_sum"].at[expert, s],
                            chunk,
                        )
                    )
        reduce = Reduce("reduce", place, made, pieces)

        near = [
            made.local("own qkv", qkv_own, out["qkv_full"].at[z, xy, core]),
            made.local("own wo", wo_own, out["wo_full"].at[z, xy, core]),
        ]
        late = [made.local("own hidden", hidden_own.at[core], out["hidden_full"].at[core, z, xy])]
        pair = [
            made.far("pair hidden", hidden_own.at[1 - core], out["hidden_full"].at[core, z, xy], place.sibling())
        ]
        for chunk in range(CHUNKS):
            late.append(made.local(("own in", chunk), in_own.at[chunk, core], out["in_full"].at[chunk, z, xy, core]))
            pair.append(
                made.far(
                    ("pair in", chunk), in_own.at[chunk, 1 - core], out["in_full"].at[chunk, z, xy, core], place.sibling()
                )
            )
        for copy in near + late:
            copy.start()
        place.barrier()
        for copy in near:
            copy.wait()

        def first_phase(cot, picked):
            load = made.local("cot", cot_hbm, cot)
            load.start()
            gather.tick(0)
            for copy in pair:
                copy.start()
            count_second = find_slots(slots, ids_ref, core)
            pack_small(small_own, (gain_ref, shift_ref, attn_bias_ref, out_bias_ref, in_bias_ref), count_second)
            small_full[z, xy, core] = small_own[...].astype(BF16)
            gather.tick(1)
            load.wait()
            pick_rows(picked.at[1], slots[1:2, :], cot[...])
            theirs = made.far("grad rows", picked.at[1], out["grad_rows"].at[1], place.sibling())
            theirs.start()
            gather.tick(2)
            pick_rows(picked.at[0], slots[0:1, :], cot[...])
            mine = made.local("grad rows", picked.at[0], out["grad_rows"].at[0])
            mine.start()
            for copy in late + pair:
                copy.wait()
            gather.tick(3)
            mine.wait()
            theirs.wait()

        pl.run_scoped(first_phase, pltpu.VMEM((n, d), BF16), pltpu.VMEM((2, MOST, d), BF16))

        def forward_phase(tok, w, wo, normed, qkv, attended, logs, residual, normed_two, picked):
            load = made.local("tokens", tokens_hbm, tok)
            load.start()
            loads = []
            for part in range(3):
                gather.tick(4 + part)
                gather.need(part)
                at_columns = pl.ds(part * d, d)
                loads.append(
                    made.local(
                        ("w", part), out["qkv_full"].at[:, :, :, :, at_columns], w.at[:, :, :, :, at_columns]
                    )
                )
                loads[-1].start()
            unpack_small(small_full, core, d, share, hidden_share, vectors, in_bias, out_bias, out["counts"])
            load.wait()
            for copy in loads:
                copy.wait()

            @pl.loop(0, n // BLOCK)
            def _(i):
                rows = pl.ds(pl.multiple_of(i * BLOCK, BLOCK), BLOCK)
                scaled, _ = row_stats(tok[rows].astype(F32))
                normed[rows] = (scaled * vectors[0:1, :d] + vectors[1:2, :d]).astype(BF16)
                weight = as_rows(w[...], d)
                qkv[rows] = (dot(normed[rows], weight) + vectors[2:3, :]).astype(BF16)
                ticks_at(i, {1: 7, 3: 8}, gather)

            saves = [
                made.local("save normed", normed, out["normed"]),
                made.local("save qkv", qkv, out["qkv"]),
            ]
            for save in saves:
                save.start()

            @pl.loop(0, heads)
            def _(head):
                attend_pair(qkv, head, attended, logs)
                ticks_at(head, {2: 9, 4: 10, 6: 11}, gather)

            saves += [
                made.local("save attended", attended, out["attended"]),
                made.local("save logs", logs, out["logs"]),
            ]
            for save in saves[2:]:
                save.start()
            gather.need(3)
            load_wo = made.local("wo", out["wo_full"], wo)
            load_wo.start()
            gather.tick(12)
            load_wo.wait()

            @pl.loop(0, n // BLOCK)
            def _(i):
                rows = pl.ds(pl.multiple_of(i * BLOCK, BLOCK), BLOCK)
                added = dot(attended[rows], as_rows(wo[...], d)) + vectors[0:1, 2 * d :]
                residual[rows] = tok[rows].astype(F32) + added
                scaled, _ = row_stats(residual[rows])
                normed_two[rows] = (scaled * vectors[0:1, d : 2 * d] + vectors[1:2, d : 2 * d]).astype(BF16)
                ticks_at(i, {1: 13}, gather)

            saves.append(made.local("save residual", residual, out["residual"]))
            saves[-1].start()
            pick_rows(picked.at[1], slots[1:2, :], normed_two[...])
            theirs = made.far("rows", picked.at[1], out["rows"].at[1], place.sibling())
            theirs.start()
            pick_rows(picked.at[0], slots[0:1, :], normed_two[...])
            saves.append(made.local("rows", picked.at[0], out["rows"].at[0]))
            saves[-1].start()
            gather.tick(14)
            for save in saves:
                save.wait()
            theirs.wait()

        pl.run_scoped(
            forward_phase,
            pltpu.VMEM((n, d), BF16),
            pltpu.VMEM((nz, nx, 2, depth, 3 * d), BF16),
            pltpu.VMEM((nz, nx, 2, depth, d), BF16),
            pltpu.VMEM((n, d), BF16),
            pltpu.VMEM((n, 3 * d), BF16),
            pltpu.VMEM((n, d), BF16),
            pltpu.VMEM((heads, 8, n), F32),
            pltpu.VMEM((n, d), F32),
            pltpu.VMEM((n, d), BF16),
            pltpu.VMEM((2, MOST, d), BF16),
        )

        def expert_phase(rows, grads, turned, made_total, back_total, w_in, w_hidden, grad_in, grad_hidden):
            loads = [
                made.local("load rows", out["rows"], rows),
                made.local("load grads", out["grad_rows"], grads),
            ]
            for copy in loads:
                copy.start()

            def weights(step):
                slot, chunk, t = lax.rem(step, 2), lax.div(step, tiles), lax.rem(step, tiles)
                at_columns = pl.ds(pl.multiple_of(t * tile, tile), tile)
                return [
                    made.local("w in", out["in_full"].at[chunk, :, :, :, :, at_columns], w_in.at[slot]),
                    made.local("w hidden", out["hidden_full"].at[chunk, t], w_hidden.at[slot]),
                ]

            def stores(step):
                slot, chunk, t = lax.rem(step, 2), lax.div(step, tiles), lax.rem(step, tiles)
                at_columns = pl.ds(pl.multiple_of(t * tile, tile), tile)
                return [
                    made.local("store in", grad_in.at[slot], out["in_terms"].at[chunk, :, :, :, :, at_columns], slot),
                    made.local("store hidden", grad_hidden.at[slot], out["hidden_terms"].at[chunk, t], slot),
                ]

            made_total[...] = jnp.zeros_like(made_total)
            back_total[...] = jnp.zeros_like(back_total)
            for copy in loads:
                copy.wait()
            turned[...] = as_rows(rows[...], count).T
            total = jnp.sum(as_rows(grads[...], count).astype(F32), axis=0, keepdims=True)
            sums[...] = jnp.zeros_like(sums)
            for expert in range(EXPERTS):
                sums[8 + expert : 9 + expert, :] = jnp.where(core == expert, total, 0.0)

            @pl.loop(0, CHUNKS * tiles)
            def _(step):
                slot = lax.rem(step, 2)
                for chunk in range(CHUNKS):
                    @pl.when(step == chunk * tiles)
                    def _(chunk=chunk):
                        for piece in range(2 * CUTS):
                            gather.need(4 + chunk * 2 * CUTS + piece)
                        for copy in weights(step):
                            copy.start()
                        if chunk:
                            reduce.tick(0)

                for copy in weights(step):
                    copy.wait()

                @pl.when(lax.rem(step, tiles) != tiles - 1)
                def _():
                    for copy in weights(step + 1):
                        copy.start()

                def beside(spot):
                    ticks_at(step, {k: now for (k, at), now in gather_beside.items() if at == spot}, gather)
                    ticks_at(step, {k: now for (k, at), now in reduce_beside.items() if at == spot}, reduce)

                rows_now, grads_now = as_rows(rows[...], count), as_rows(grads[...], count)
                w_in_now = as_rows(w_in[slot], d)
                w_hidden_now = as_rows(w_hidden[slot], tile)
                hidden_pre = dot(rows_now, w_in_now) + in_bias[step, 0:1, :]
                hidden, slope = gelu_and_slope(hidden_pre)
                hidden = hidden.astype(BF16)
                grad_pre = dot_last(grads_now, w_hidden_now) * slope
                bias_sums[step, 0:1, :] = jnp.sum(grad_pre, axis=0, keepdims=True)
                grad_pre = grad_pre.astype(BF16)
                beside(0)
                made_total[...] += dot(hidden, w_hidden_now)
                back_total[...] += dot_last(grad_pre, w_in_now)
                beside(1)

                @pl.when(lax.rem(step, tiles) >= 2)
                def _():
                    for copy in stores(step - 2):
                        copy.wait()

                grad_hidden[slot] = split_rows(dot(hidden.T, grads_now).astype(BF16), (nx, hidden_share, d))
                grad_in[slot] = split_rows(dot(turned[...], grad_pre).astype(BF16), (nz, nx, 2, depth, tile))
                for copy in stores(step):
                    copy.start()
                beside(2)

                @pl.when(lax.rem(step, tiles) == tiles - 1)
                def _():
                    if tiles > 1:
                        for copy in stores(step - 1):
                            copy.wait()
                    for copy in stores(step):
                        copy.wait()

            rows[...] = split_rows((made_total[...] + out_bias[0:1, :]).astype(BF16), (2, MOST, d))
            grads[...] = split_rows(back_total[...].astype(BF16), (2, MOST, d))
            results = []
            for name, source in (("made_rows", rows), ("back_rows", grads)):
                results.append(made.far(name, source.at[1], out[name].at[1], place.sibling()))
                results.append(made.local(name, source.at[0], out[name].at[0]))
            for copy in results:
                copy.start()
            reduce.tick(reduce_next[0])
            for copy in results:
                copy.wait()

        gather_beside = {(k // 2, k % 2 * 2): 15 + k for k in range(8)}
        reduce_beside = {(tiles, 2): 1, (tiles + 1, 2): 2, (tiles + 2, 2): 3, (tiles + 3, 2): 4}
        reduce_next = [5]
        pl.run_scoped(
            expert_phase,
            pltpu.VMEM((2, MOST, d), BF16),
            pltpu.VMEM((2, MOST, d), BF16),
            pltpu.VMEM((d, count), BF16),
            pltpu.VMEM((count, d), F32),
            pltpu.VMEM((count, d), F32),
            pltpu.VMEM((2, nz, nx, 2, depth, tile), BF16),
            pltpu.VMEM((2, nx, hidden_share, d), BF16),
            pltpu.VMEM((2, nz, nx, 2, depth, tile), BF16),
            pltpu.VMEM((2, nx, hidden_share, d), BF16),
        )
        reduce_next[0] += 1

        def backward_phase(
            grad_res, made_rows, back_rows, cot, wo, att, qkv, logs, normed, block, branch, grad_att, turned, projected, wide,
            slots_turned,
        ):
            def load(name, source, target):
                copy = made.local(("back", name), source, target)
                copy.start()
                return copy

            loads = [
                load("residual", out["residual"], grad_res),
                load("made", out["made_rows"], made_rows),
                load("back", out["back_rows"], back_rows),
                load("cot", cot_hbm, cot),
                load("wo", out["wo_full"], wo),
            ]
            late_loads = [
                load("att", out["attended"], att),
                load("qkv", out["qkv"], qkv),
                load("logs", out["logs"], logs),
                load("normed", out["normed"], normed),
            ]
            slots_turned[...] = slots[...].astype(F32).T
            for copy in loads:
                copy.wait()

            @pl.loop(0, n // BLOCK)
            def _(i):
                rows = pl.ds(pl.multiple_of(i * BLOCK, BLOCK), BLOCK)
                columns = lax.broadcasted_iota(jnp.int32, (BLOCK, MOST), 1).astype(F32)
                chosen = jnp.concatenate(
                    [jnp.where(columns == slots_turned[rows, k : k + 1], 1.0, 0.0).astype(BF16) for k in range(2)],
                    axis=1,
                )
                values = grad_res[rows]
                block[rows] = (values + dot(chosen, as_rows(made_rows[...], count))).astype(BF16)
                grad = dot(chosen, as_rows(back_rows[...], count))
                term, gain_sum, shift_sum = norm_backward(values, vectors[0:1, d : 2 * d], grad)
                sums[1:2, :] += gain_sum
                sums[3:4, :] += shift_sum
                total = cot[rows].astype(F32) + term
                grad_res[rows] = total
                low = total.astype(BF16)
                branch[rows] = low
                sums[6:7, :] += jnp.sum(low.astype(F32), axis=0, keepdims=True)
                grad_att[rows] = dot_last(low, as_rows(wo[...], d)).astype(BF16)
                ticks_at(i, {1: reduce_next[0], 3: reduce_next[0] + 1}, reduce)

            now = reduce_next[0] + 2
            saves = [load("block", block, out["block_out"]), load("grad_res", grad_res, out["grad_res"])]
            for copy in late_loads:
                copy.wait()

            @pl.loop(0, heads)
            def _(head):
                attend_pair_backward(qkv, head, att, grad_att, logs, projected, turned)
                spots = [heads // 8, heads // 4, heads // 2, heads * 5 // 8, heads - 1]
                ticks_at(head, {spot: now + k for k, spot in enumerate(spots)}, reduce)

            now += 5
            saves.append(load("projected", projected, out["projected"]))
            wide[0] = split_rows(dot(att[...].T, branch[...]).astype(BF16), wide.shape[1:])
            written = [load("wo terms", wide.at[0], out["wo_terms"])]
            normed_turned = normed[...].T
            for part in range(3):
                columns = slice(part * d, (part + 1) * d)
                spot = (part + 1) % 2
                if part > 0:
                    written[part - 1].wait()
                wide[spot] = split_rows(dot(normed_turned, projected[:, columns]).astype(BF16), wide.shape[1:])
                written.append(
                    load(("qkv terms", part), wide.at[spot], out["qkv_terms"].at[:, :, :, :, pl.ds(part * d, d)])
                )
                if part != 1:
                    sums[4 + part // 2 : 5 + part // 2, :] = jnp.sum(
                        projected[:, columns].astype(F32), axis=0, keepdims=True
                    )
                reduce.tick(now)
                now += 1
            lines = width // d
            for step in range(CHUNKS * tiles):
                first = (step % tiles) * tile
                for expert in range(EXPERTS):
                    row = 10 + expert * CHUNKS * lines + step // tiles * lines + first // d
                    sums[row : row + 1, first % d : first % d + tile] = jnp.where(
                        core == expert, bias_sums[step, 0:1, :], 0.0
                    )
            while now < len(pieces) + reduce.stages(pieces[0]) - 1:
                reduce.tick(now)
                now += 1
            for piece in range(len(pieces)):
                reduce.need(piece)
            for copy in saves + written[2:]:
                copy.wait()

        pl.run_scoped(
            backward_phase,
            pltpu.VMEM((n, d), F32),
            pltpu.VMEM((2, MOST, d), BF16),
            pltpu.VMEM((2, MOST, d), BF16),
            pltpu.VMEM((n, d), BF16),
            pltpu.VMEM((nz, nx, 2, depth, d), BF16),
            pltpu.VMEM((n, d), BF16),
            pltpu.VMEM((n, 3 * d), BF16),
            pltpu.VMEM((heads, 8, n), F32),
            pltpu.VMEM((n, d), BF16),
            pltpu.VMEM((n, d), BF16),
            pltpu.VMEM((n, d), BF16),
            pltpu.VMEM((n, d), BF16),
            pltpu.VMEM((128, n), F32),
            pltpu.VMEM((n, 3 * d), BF16),
            pltpu.VMEM((2, nz, nx, 2, depth, d), BF16),
            pltpu.VMEM((n, 8), F32),
        )

    exchanged = nz + nx
    results = pl.pallas_call(
        kernel,
        out_shape=list(outputs.values()) + list(small_outputs.values()),
        in_specs=[HBM, HBM] + [VMEM] * 6 + [HBM] * 4,
        out_specs=[HBM] * len(outputs) + [VMEM] * len(small_outputs),
        scratch_shapes=[
            pltpu.VMEM((8, n), jnp.int32),
            pltpu.VMEM((16, 128), F32),
            pltpu.VMEM((nz, nx, 2, 16, 128), BF16),
            pltpu.VMEM((CHUNKS * tiles, 8, tile), F32),
            pltpu.VMEM((8, d), F32),
            pltpu.VMEM((CHUNKS * tiles, 8, tile), F32),
            *spares,
            *landing_scratch,
            *semaphores(36 * exchanged + 32, 16 * (nx // 2 + 2) + 48),
        ],
        compiler_params=pltpu.CompilerParams(
            collective_id=1, has_side_effects=True, vmem_limit_bytes=64 * MIB - 64 * 1024
        ),
        name="block",
    )(tokens, cotangent, ids, *small, w_qkv, w_out, in_own, hidden_own)
    return dict(zip(names, results))


def ticks_at(step, wanted, stream):
    for k, now in wanted.items():
        @pl.when(step == k)
        def _(now=now):
            stream.tick(now)


def last_kernel(nz, nx, block, tokens):
    n, d = tokens.shape
    depth = block["wo_terms"].shape[3]
    tail = (depth, d)
    landings = [landing_shapes(nz, nx, tail, True)] * 4
    per_piece = len(landings[0])
    landing_scratch = [pltpu.VMEM(shape, BF16) for shapes in landings for shape in shapes]
    partners = nz.bit_length() - 1 + nx.bit_length() - 1 + 1
    shape = block["small_terms"].shape

    def kernel(
        projected_ref, w_ref, grad_ref, tokens_ref, vectors, small_ref, qkv_terms, wo_terms,
        input_grad, small_sum, qkv_sum, wo_sum, terms, terms_landing, spare, *scratch,
    ):
        place = Place(nz, nx)
        made = Copies(*scratch[-3:])

        def piece(at, i):
            mine = scratch[at * per_piece : (at + 1) * per_piece]
            if i == 3:
                return lambda zs, xs, core: wo_terms.at[zs, xs, core], mine, spare.at[at % 2], wo_sum, "first"
            columns = pl.ds(i * d, d)
            return (
                lambda zs, xs, core: qkv_terms.at[zs, xs, core, :, columns],
                mine, spare.at[at % 2], qkv_sum.at[:, columns], "first",
            )

        reduce = Reduce("last", place, made, [piece(at, i) for at, i in enumerate((3, 0, 1, 2))])
        total = Total(place, made, terms, terms_landing)
        place.barrier()
        reduce.tick(0)
        terms[0] = small_ref[...]

        @pl.loop(0, n // BLOCK)
        def _(i):
            rows = pl.ds(pl.multiple_of(i * BLOCK, BLOCK), BLOCK)
            grad = dot_last(projected_ref[rows], as_rows(w_ref[...], d))
            term, gain_sum, shift_sum = norm_backward(tokens_ref[rows].astype(F32), vectors[0:1, :d], grad)
            input_grad[rows] = grad_ref[rows] + term
            terms[0, 0:1, :] += gain_sum
            terms[0, 2:3, :] += shift_sum
            ticks_at(i, {1: 1, 3: 2}, reduce)

        stage = 0
        for now in range(3, 3 + reduce.stages(reduce.pieces[0])):
            if stage < total.stages:
                total.begin(stage)
            reduce.tick(now)
            if stage < total.stages:
                total.finish(stage)
                stage += 1
        for late in range(stage, total.stages):
            total.begin(late)
            total.finish(late)
        for at in range(4):
            reduce.need(at)
        small_sum[...] = terms[total.stages]

    return pl.pallas_call(
        kernel,
        out_shape=[
            jax.ShapeDtypeStruct((n, d), F32),
            jax.ShapeDtypeStruct(shape, F32),
            jax.ShapeDtypeStruct((depth, 3 * d), BF16),
            jax.ShapeDtypeStruct((depth, d), BF16),
        ],
        in_specs=[VMEM] * 6 + [HBM] * 2,
        out_specs=[VMEM] * 2 + [HBM] * 2,
        scratch_shapes=[
            pltpu.VMEM((partners + 1,) + shape, F32),
            pltpu.VMEM((partners,) + shape, F32),
            pltpu.VMEM((2,) + landings[0][0], BF16),
            *landing_scratch,
            *semaphores(4 * (2 * nx + nz) + partners, 4 * (nx + 1)),
        ],
        compiler_params=pltpu.CompilerParams(collective_id=2, has_side_effects=True, vmem_limit_bytes=60 * MIB),
        name="last_sums",
    )(
        block["projected"], block["qkv_full"], block["grad_res"], tokens, block["vectors"], block["small_terms"],
        block["qkv_terms"], block["wo_terms"],
    )


def shards(
    nz, nx, tokens, norm_gain, norm_bias, w_qkv, attn_bias, w_attn_out, expert_in, expert_in_bias, expert_out,
    expert_out_bias, expert_ids, running_load, cotangent,
):
    n, d = tokens.shape
    devices = nz * nx * 2
    chips = nz * nx
    core = lax.axis_index("core")
    me = lax.axis_index(("dp", "xy", "core"))
    share = norm_gain.shape[1]
    depth, width = expert_in.shape[1:]
    hidden_share = expert_out.shape[1]

    def columns(chip, chunk):
        first = (chip * CHUNKS + chunk) * hidden_share
        return expert_in[:, :, first : first + hidden_share]

    in_own = jnp.stack(
        [jnp.concatenate([columns(chip, chunk) for chip in range(chips)], axis=2) for chunk in range(CHUNKS)]
    )
    small = (norm_gain, norm_bias, attn_bias, expert_out_bias, expert_in_bias)
    block = block_kernel(
        nz, nx, tokens, cotangent, expert_ids.reshape(1, n), small, w_qkv, w_attn_out, in_own, expert_out
    )
    input_grad, small_sum, qkv_sum, wo_sum = last_kernel(nz, nx, block, tokens)

    mine = lax.dynamic_slice_in_dim(small_sum[:10], me * share, share, axis=1)
    lines = width // CHUNKS // d
    in_bias_sum = small_sum[10 : 10 + EXPERTS * CHUNKS * lines].reshape(EXPERTS, CHUNKS, width // CHUNKS)
    in_bias_sum = lax.dynamic_slice(
        in_bias_sum, (0, core, me // CHUNKS * hidden_share), (EXPERTS, 1, hidden_share)
    )[:, 0]
    in_sum = block["in_sum"].reshape(CHUNKS, EXPERTS, depth, chips, hidden_share)
    in_sum = in_sum.transpose(1, 2, 3, 0, 4).reshape(EXPERTS, depth, width).astype(F32)
    counts = block["counts"][0, :2]
    total_second = (counts[0] * 32 + counts[1]).astype(jnp.int32)
    expert_counts = jnp.stack([n * devices - total_second, total_second])
    expert_load = 0.9 * running_load + 0.1 * (expert_counts.astype(F32) * EXPERTS / (n * devices))
    return (
        block["block_out"],
        input_grad,
        mine[0:2],
        mine[2:4],
        qkv_sum.astype(F32),
        mine[4:7],
        wo_sum.astype(F32),
        in_sum,
        in_bias_sum,
        block["hidden_sum"].astype(F32),
        mine[8:10],
        expert_counts,
        expert_load,
    )


def solution(mesh):
    nz, nx = mesh.shape["dp"], mesh.shape["fsdp"] // 2
    fine = Mesh(mesh.devices.reshape(nz, nx, 2), ("dp", "xy", "core"))
    every = ("dp", "xy", "core")
    row, column, middle = P(every, None), P(None, every), P(None, every, None)
    return jax.shard_map(
        functools.partial(shards, nz, nx),
        mesh=fine,
        in_specs=(
            row, column, column, row, column, row, middle, column, middle, column, row, P(), row,
        ),
        out_specs=(row, row, column, column, row, column, row, middle, column, middle, column, P(), P()),
        check_vma=False,
    )
```

```python
import functools
import math

import jax
import jax.numpy as jnp
from jax import lax
from jax.experimental import pallas as pl
from jax.experimental.pallas import tpu as pltpu
from jax.sharding import Mesh, PartitionSpec as P

BF16 = jnp.bfloat16
F32 = jnp.float32
MESH_ID = pl.DeviceIdType.MESH

HEAD = 64
MOST = 640
EXPERTS = 2
CHUNKS = 2
CUTS = 4
AHEAD = 1
NORM_EPS = 1e-05
SCORE_SCALE = 0.125
SCALE_LOG2 = SCORE_SCALE * math.log2(math.e)
MASKED = -1e30
BLOCK = 256
MIB = 1 << 20
ALL = slice(None)
HBM = pl.BlockSpec(memory_space=pl.ANY)
VMEM = pl.BlockSpec(memory_space=pltpu.VMEM)


def dot(left, right):
    return lax.dot_general(left, right, (((1,), (0,)), ((), ())), preferred_element_type=F32)


def dot_last(left, right):
    return lax.dot_general(left, right, (((1,), (1,)), ((), ())), preferred_element_type=F32)


def row_stats(values):
    center = values - jnp.mean(values, axis=-1, keepdims=True)
    spread = jnp.mean(center * center, axis=-1, keepdims=True)
    inverse = lax.rsqrt(spread + NORM_EPS)
    return center * inverse, inverse


def as_rows(values, rows):
    if values.dtype == BF16 and values.shape[-2] % 16:
        return values.astype(F32).reshape(rows, values.shape[-1]).astype(BF16)
    return values.reshape(rows, values.shape[-1])


def split_rows(values, shape):
    if values.dtype == BF16 and shape[-2] % 16:
        return values.astype(F32).reshape(shape).astype(BF16)
    return values.reshape(shape)


class Place:
    def __init__(self, nz, nx):
        self.nz, self.nx = nz, nx
        self.bits_z, self.bits_x = nz.bit_length() - 1, nx.bit_length() - 1
        self.z, self.xy, self.core = lax.axis_index("dp"), lax.axis_index("xy"), lax.axis_index("core")
        self.flip_z = [(1 - 2 * lax.rem(lax.div(self.z, 2**k), 2)) * 2**k for k in range(self.bits_z)]
        self.flip_x = [(1 - 2 * lax.rem(lax.div(self.xy, 2**k), 2)) * 2**k for k in range(self.bits_x)]

    def step_x(self, k, core=None):
        core = self.core if core is None else core
        return (1 - core) * self.flip_x[k] + core * self.flip_x[self.bits_x - 1 - k]

    def span_x(self, which, core=None):
        return self.xy + sum(self.step_x(k, core) for k in range(self.bits_x) if which >> k & 1)

    def span_z(self, which):
        return self.z + sum(self.flip_z[k] for k in range(self.bits_z) if which >> k & 1)

    def partners(self):
        found = [(self.z + flip, self.xy, self.core) for flip in self.flip_z]
        found += [(self.z, self.xy + flip, self.core) for flip in self.flip_x]
        return found + [self.sibling()]

    def sibling(self):
        return (self.z, self.xy, 1 - self.core)

    def barrier(self):
        semaphore = pltpu.get_barrier_semaphore()
        partners = self.partners()
        for partner in partners:
            pl.semaphore_signal(semaphore, inc=1, device_id=partner, device_id_type=MESH_ID)
        pl.semaphore_wait(semaphore, len(partners))


class Copies:
    def __init__(self, send, recv, near):
        self.send, self.recv, self.near = send, recv, near
        self.far_names, self.near_names = {}, {}

    def far(self, name, src, dst, device):
        i = self.far_names.setdefault(name, len(self.far_names))
        return pltpu.make_async_remote_copy(
            src_ref=src, dst_ref=dst, send_sem=self.send.at[i], recv_sem=self.recv.at[i],
            device_id=device, device_id_type=MESH_ID,
        )

    def local(self, name, src, dst, slot=None):
        if slot is not None:
            self.near_names.setdefault((name, 0), len(self.near_names))
            self.near_names.setdefault((name, 1), len(self.near_names))
            return pltpu.make_async_copy(src, dst, self.near.at[self.near_names[name, 0] + slot])
        i = self.near_names.setdefault(name, len(self.near_names))
        return pltpu.make_async_copy(src, dst, self.near.at[i])


def semaphores(far, near):
    return [
        pltpu.SemaphoreType.DMA((far,)),
        pltpu.SemaphoreType.DMA((far,)),
        pltpu.SemaphoreType.DMA((near,)),
    ]


class Stream:
    def __init__(self, pieces):
        self.pieces = pieces
        self.begun = {}

    def advance(self, piece, stage):
        if stage > 0:
            self.finish(piece, stage - 1)
        self.begin(piece, stage)
        self.begun[piece] = stage

    def last(self, piece):
        return self.stages(self.pieces[piece]) - 1


class Schedule:
    def __init__(self, place):
        self.plan = PLAN if (place.nz, place.nx) == PLAN_MESH else None
        self.streams = {}

    def at(self, point):
        for item in (self.plan or {}).get(point, ()):
            self.streams[item // 1000].advance(item % 1000 // 10, item % 10)

    def in_loop(self, i, name, count):
        for k in range(count):
            if (self.plan or {}).get(f"{name}{k}"):
                @pl.when(i == k)
                def _(k=k):
                    self.at(f"{name}{k}")

    def need(self, point, stream, pieces):
        self.at(point)
        if self.plan is None:
            most = max(stream.last(piece) for piece in pieces)
            for now in range(len(pieces) + most):
                for stage in range(most, -1, -1):
                    if 0 <= now - stage < len(pieces):
                        piece = pieces[now - stage]
                        if stream.begun.get(piece, -1) < stage <= stream.last(piece):
                            stream.advance(piece, stage)
        for piece in pieces:
            stream.finish(piece, stream.last(piece))

    def force(self, stream, piece, stage):
        if self.plan is None:
            for now in range(stream.begun.get(piece, -1) + 1, stage + 1):
                stream.advance(piece, now)


class Gather(Stream):
    def __init__(self, name, place, copies, pieces):
        super().__init__(pieces)
        self.name, self.place, self.made = name, place, copies

    def stages(self, piece):
        return self.place.bits_z + self.place.bits_x + (piece[2] is not None)

    def copies(self, piece, stage):
        place = self.place
        order, region, to_sibling = self.pieces[piece]
        step_z = stage if order == "z" else stage - place.bits_x
        step_x = stage - place.bits_z if order == "z" else stage
        found = []
        if stage == place.bits_z + place.bits_x:
            found += [(ref, place.sibling()) for ref in to_sibling]
        elif 0 <= step_z < place.bits_z:
            bit = place.bits_z - 1 - step_z
            device = (place.z + place.flip_z[bit], place.xy, place.core)
            for held in range(2**step_z):
                held_xy = place.xy if order == "z" else ALL
                found += [(ref, device) for ref in region(place.span_z(held << (bit + 1)), held_xy)]
        else:
            device = (place.z, place.xy + place.step_x(step_x), place.core)
            for held in range(2**step_x):
                held_z = ALL if order == "z" else place.z
                found += [(ref, device) for ref in region(held_z, place.span_x(held))]
        return [
            self.made.far((self.name, piece, stage, i), ref, ref, device) for i, (ref, device) in enumerate(found)
        ]

    def begin(self, piece, stage):
        for copy in self.copies(piece, stage):
            copy.start()

    def finish(self, piece, stage):
        for copy in self.copies(piece, stage):
            copy.wait()


def add_up(total, landed):
    if len(total.shape) > 3:
        @pl.loop(0, total.shape[0])
        def _(i):
            add_up(total.at[i], landed.at[i])
    else:
        total[...] = (total[...].astype(F32) + landed[...].astype(F32)).astype(BF16)


class Reduce(Stream):
    def __init__(self, name, place, copies, pieces):
        super().__init__(pieces)
        self.name, self.place, self.made = name, place, copies

    def stages(self, piece):
        return self.place.bits_z + self.place.bits_x + 1

    def plan(self, piece, stage):
        place = self.place
        nx, bits_x, bits_z = place.nx, place.bits_x, place.bits_z
        pair = isinstance(self.pieces[piece], PairPiece)
        if pair:
            order, landing, acc = self.pieces[piece].order, self.pieces[piece].landing, self.pieces[piece].acc
            first, landed = False, landing[stage - 1]
            step = stage - 1
        else:
            order, landing, spare, source, _, _ = self.pieces[piece]
            acc, first, landed, step = landing[0], stage == 0, landing[stage], stage
        far, near, sums = [], [], []
        step_x = step if order == "z" else step - bits_z
        step_z = step - bits_x if order == "z" else step
        if 0 <= step_x < bits_x:
            k = bits_x - 1 - step_x
            device = (place.z, place.xy + place.step_x(k), place.core)
            for j in range(2**k):
                if first:
                    far.append((source(ALL, place.span_x(2**k + j)), acc.at[j], device))
                    near.append((source(ALL, place.span_x(j)), spare.at[j]))
                    sums.append((acc.at[j], spare.at[j]))
                elif order == "x":
                    at_z = place.z if pair else 0
                    far.append((acc.at[at_z, place.span_x(2**k + j)], landed.at[j], device))
                    sums.append((acc.at[at_z, place.span_x(j)], landed.at[j]))
                elif pair:
                    far.append((acc.at[:, place.span_x(2**k + j)], landed.at[j], device))
                    sums += [(acc.at[i, place.span_x(j)], landed.at[j, i]) for i in range(place.nz)]
                else:
                    far.append((acc.at[2**k + j], landed.at[j], device))
                    sums.append((acc.at[j], landed.at[j]))
        else:
            bit = step_z
            device = (place.z + place.flip_z[bit], place.xy, place.core)
            for s in range(2 ** (bits_z - 1 - bit)):
                upper = s << (bit + 1)
                if first:
                    far.append((source(place.span_z(upper + 1), ALL), acc.at[s], device))
                    near.append((source(place.span_z(upper), ALL), spare.at[s]))
                    sums.append((acc.at[s], spare.at[s]))
                elif order == "z":
                    at_xy = place.xy if pair else None
                    send, keep = place.span_z(upper + 2**bit), place.span_z(upper)
                    far.append((acc.at[send, at_xy] if pair else acc.at[0, send], landed.at[s], device))
                    sums.append((acc.at[keep, at_xy] if pair else acc.at[0, keep], landed.at[s]))
                else:
                    send = place.span_z(upper + 2**bit) if pair else (upper + 2**bit) // 2
                    keep = place.span_z(upper) if pair else upper // 2
                    far.append((acc.at[send], landed.at[s], device))
                    sums.append((acc.at[keep], landed.at[s]))
        return far, near, sums

    def made_copies(self, piece, stage, far, near):
        made = [
            self.made.far((self.name, piece, stage, i), src, dst, device) for i, (src, dst, device) in enumerate(far)
        ]
        return made + [self.made.local((self.name, piece, stage, i), src, dst) for i, (src, dst) in enumerate(near)]

    def deliver(self, piece, begin):
        place, core = self.place, self.place.core
        order, landing, _, _, target, owner = self.pieces[piece]
        mine = landing[0].at[0, place.z if order == "z" else place.xy]
        name = (self.name, piece, "last")

        def there(part):
            return self.made.far(name, part, target(core), place.sibling())

        def here(part):
            return self.made.local(name, part, target(core))

        if owner == "both":
            for copy in (there(mine.at[1 - core]), here(mine.at[core])):
                copy.start() if begin else copy.wait()
            return

        @pl.when(core == owner)
        def _():
            if begin:
                here(mine).start()
            else:
                here(mine).wait()
                there(mine).wait_recv()

        @pl.when(core != owner)
        def _():
            there(mine).start() if begin else there(mine).wait_send()

    def to_pair(self, piece):
        item, place = self.pieces[piece], self.place
        return self.made.far((self.name, piece, "pair"), item.source(1 - place.core), item.landed, place.sibling())

    def begin(self, piece, stage):
        pair = isinstance(self.pieces[piece], PairPiece)
        if pair and stage == 0:
            self.to_pair(piece).start()
            return
        if not pair and stage == self.stages(self.pieces[piece]) - 1:
            self.deliver(piece, True)
            return
        far, near, _ = self.plan(piece, stage)
        for copy in self.made_copies(piece, stage, far, near):
            copy.start()

    def finish(self, piece, stage):
        item, final = self.pieces[piece], stage == self.stages(self.pieces[piece]) - 1
        pair = isinstance(item, PairPiece)
        if pair and stage == 0:
            self.to_pair(piece).wait()
            here = self.made.local((self.name, piece, "pair"), item.landed, item.acc)
            here.start()
            here.wait()
            add_up(item.acc, item.source(self.place.core))
            return
        if final and not pair:
            self.deliver(piece, False)
            return
        far, near, sums = self.plan(piece, stage)
        for copy in self.made_copies(piece, stage, far, near):
            copy.wait()
        for total, landed in sums:
            add_up(total, landed)
        if final:
            here = self.made.local((self.name, piece, "last"), item.acc.at[self.place.z, self.place.xy], item.target)
            here.start()
            here.wait()


class PairPiece:
    def __init__(self, order, source, landed, acc, landing, target):
        self.order, self.source, self.landed, self.acc = order, source, landed, acc
        self.landing, self.target = landing, target


def landing_shapes(nz, nx, tail, order):
    bits_z, bits_x = nz.bit_length() - 1, nx.bit_length() - 1
    if order == "z":
        return [(2**k, nz) + tail for k in reversed(range(bits_x))] + [
            (2 ** (bits_z - 1 - bit),) + tail for bit in range(bits_z)
        ]
    return [(2 ** (bits_z - 1 - bit), nx) + tail for bit in range(bits_z)] + [
        (2**k,) + tail for k in reversed(range(bits_x))
    ]


class Total:
    def __init__(self, place, copies, terms, landing):
        self.place, self.made, self.terms, self.landing = place, copies, terms, landing
        self.stages = len(place.partners())

    def copy(self, stage):
        device = self.place.partners()[stage]
        return self.made.far(("total", stage), self.terms.at[stage % 2], self.landing.at[stage], device)

    def begin(self, stage):
        self.copy(stage).start()

    def finish(self, stage):
        self.copy(stage).wait()
        self.terms[(stage + 1) % 2] = self.terms[stage % 2] + self.landing[stage]


def one_hot(slots, count):
    rows = lax.broadcasted_iota(jnp.int32, (count, slots.shape[1]), 0)
    return jnp.where(rows == slots, 1.0, 0.0).astype(BF16)


def pick_rows(picked, slots, values):
    picked[...] = dot(one_hot(slots, picked.shape[0]), values).astype(BF16)


def find_slots(slots, ids_ref, core):
    n = ids_ref.shape[1]
    ids = ids_ref[...]
    second = jnp.where(ids == 1, 1.0, 0.0)
    earlier = lax.broadcasted_iota(jnp.int32, (n, n), 0) <= lax.broadcasted_iota(jnp.int32, (n, n), 1)
    before = dot(
        jnp.broadcast_to(second, (16, n)).astype(BF16), jnp.where(earlier, 1.0, 0.0).astype(BF16)
    )[0:1].astype(jnp.int32)
    rank = jnp.where(ids == 1, before - 1, lax.broadcasted_iota(jnp.int32, (1, n), 1) - before)
    own = ids == core
    slots[0:1, :] = jnp.where(own, rank, -1)
    slots[1:2, :] = jnp.where(own, -1, rank)
    slots[2:8, :] = jnp.full((6, n), -1, jnp.int32)
    return jnp.sum(second, axis=1, keepdims=True)


GAIN, SHIFT, ATTN_BIAS, OUT_BIAS, IN_BIAS, DIGITS = 0, 2, 4, 7, 9, 11


def pack_small(small, refs, count_second):
    small[...] = jnp.zeros_like(small)
    for row, ref in zip((GAIN, SHIFT, ATTN_BIAS, OUT_BIAS, IN_BIAS), refs):
        count, share = ref.shape
        small[row : row + count, :share] = ref[...].astype(F32)
    high = jnp.floor(count_second * (1 / 32))
    lane = lax.broadcasted_iota(jnp.int32, (1, 128), 1)
    small[DIGITS : DIGITS + 1, :] = jnp.where(lane == 0, high, jnp.where(lane == 1, count_second - 32 * high, 0.0))


def spread(shares, length, share, place_of):
    devices = shares.shape[0]
    lanes = lax.broadcasted_iota(jnp.int32, (128, length), 1)
    repeat = jnp.where(lax.rem(lanes, share) == lax.broadcasted_iota(jnp.int32, (128, length), 0), 1.0, 0.0)
    copies = dot(shares, repeat.astype(BF16))
    lanes = lax.broadcasted_iota(jnp.int32, (devices, length), 1)
    device = lax.broadcasted_iota(jnp.int32, (devices, length), 0)
    return jnp.sum(jnp.where(lax.div(lanes, share) == place_of(device), copies, 0.0), axis=0, keepdims=True)


def unpack_small(small_full, core, d, share, hidden_share, vectors, in_bias, out_bias, counts):
    nz, nx = small_full.shape[:2]
    devices = nz * nx * 2
    found = small_full[...].astype(F32).reshape(devices, 16, 128)

    def rows(row):
        return found[:, row, :].astype(BF16)

    def vector(shares):
        return spread(shares, d, share, lambda device: device)

    vectors[...] = jnp.zeros_like(vectors)
    for line, row, part in (
        (0, GAIN, 0), (0, GAIN + 1, 1), (0, ATTN_BIAS + 2, 2), (1, SHIFT, 0), (1, SHIFT + 1, 1),
        (2, ATTN_BIAS, 0), (2, ATTN_BIAS + 1, 2),
    ):
        vectors[line : line + 1, part * d : (part + 1) * d] = vector(rows(row))

    def of_expert(row):
        return jnp.where(core == 0, rows(row), rows(row + 1))

    out_bias[0:1, :] = vector(of_expert(OUT_BIAS))
    width = hidden_share * devices // CHUNKS
    tile = in_bias.shape[2]
    for chunk in range(CHUNKS):
        line = spread(
            of_expert(IN_BIAS), width, hidden_share,
            lambda device: jnp.where(lax.rem(device, 2) == chunk, lax.div(device, 2), -1),
        )
        for i in range(width // tile):
            in_bias[chunk * (width // tile) + i, 0:1, :] = line[:, i * tile : (i + 1) * tile]
    counts[...] = jnp.broadcast_to(jnp.sum(found[:, DIGITS, :], axis=0, keepdims=True), counts.shape)


def attend_pair(qkv, head, attended, log_total):
    n, d = attended.shape
    low = lax.broadcasted_iota(jnp.int32, (n, 128), 1) < HEAD
    one, zero = jnp.ones((), BF16), jnp.zeros((), BF16)
    query = qkv[:, pl.ds(pl.multiple_of(head * 128, 128), 128)]
    key = qkv[:, pl.ds(pl.multiple_of(d + head * 128, 128), 128)]
    value = qkv[:, pl.ds(pl.multiple_of(2 * d + head * 128, 128), 128)]
    values = [jnp.where(low, value, one), jnp.where(low, one, value)]
    queries = [jnp.where(low, query, zero), jnp.where(low, zero, query)]
    low = low[:BLOCK]
    allowed = lax.broadcasted_iota(jnp.int32, (BLOCK, BLOCK), 1) <= lax.broadcasted_iota(
        jnp.int32, (BLOCK, BLOCK), 0
    )
    for i in range(n // BLOCK):
        first, end = i * BLOCK, (i + 1) * BLOCK
        found = []
        for j in range(2):
            near = jnp.where(allowed, dot_last(queries[j][first:end], key[first:end]), MASKED)
            top = jnp.max(near, axis=-1, keepdims=True)
            if i:
                far = dot_last(queries[j][first:end], key[:first])
                top = jnp.maximum(top, jnp.max(far, axis=-1, keepdims=True))
            top = top * SCALE_LOG2
            out = dot(jnp.exp2(near * SCALE_LOG2 - top).astype(BF16), values[j][first:end])
            if i:
                out = out + dot(jnp.exp2(far * SCALE_LOG2 - top).astype(BF16), values[j][:first])
            found.append((out, top))
        (out_a, top_a), (out_b, top_b) = found
        total = pltpu.roll(jnp.where(low, out_b, out_a), HEAD, axis=1)
        attended[first:end, pl.ds(pl.multiple_of(head * 128, 128), 128)] = (
            jnp.where(low, out_a, out_b) / total
        ).astype(BF16)
        logs = (jnp.where(low, top_a, top_b) + jnp.log2(total)).T
        log_total[head, 0:1, first:end] = logs[0:1]
        log_total[head, 1:2, first:end] = logs[HEAD : HEAD + 1]


def gelu_and_slope(values):
    root = math.sqrt(2 / math.pi)
    cube = 0.044715
    square = values * values
    bent = jnp.tanh(values * (root + root * cube * square))
    half = 0.5 * (1 + bent)
    slope = half + 0.5 * values * (1 - bent * bent) * (root + 3 * root * cube * square)
    return values * half, slope


def norm_backward(values, gain, grad):
    scaled, inverse = row_stats(values)
    grad_scaled = grad * gain
    mean = jnp.mean(grad_scaled, axis=-1, keepdims=True)
    along = jnp.mean(grad_scaled * scaled, axis=-1, keepdims=True)
    term = inverse * (grad_scaled - mean - scaled * along)
    return term, jnp.sum(grad * scaled, axis=0, keepdims=True), jnp.sum(grad, axis=0, keepdims=True)


def attend_pair_backward(qkv, head, attended, grad, log_total, projected, turned):
    n, d = attended.shape
    low = lax.broadcasted_iota(jnp.int32, (n, 128), 1) < HEAD
    zero = jnp.zeros((), BF16)

    def columns(part):
        return pl.ds(pl.multiple_of(part * d + head * 128, 128), 128)

    query, key, value = (qkv[:, columns(part)] for part in range(3))
    grad = grad[:, columns(0)]
    product = (attended[:, columns(0)].astype(F32) * grad.astype(F32)).T
    inner = [jnp.sum(product[j * HEAD : (j + 1) * HEAD], axis=0, keepdims=True) for j in range(2)]
    logs = [log_total[head, j : j + 1, :] for j in range(2)]
    key_turned = key.T
    keys = [jnp.where(low, key, zero), jnp.where(low, zero, key)]
    values = [jnp.where(low, value, zero), jnp.where(low, zero, value)]
    low = low[:BLOCK]
    allowed = lax.broadcasted_iota(jnp.int32, (BLOCK, BLOCK), 0) <= lax.broadcasted_iota(
        jnp.int32, (BLOCK, BLOCK), 1
    )
    for i in range(n // BLOCK):
        first, end = i * BLOCK, (i + 1) * BLOCK
        found = []
        for j in range(2):
            grad_key = grad_value = 0.0
            for start, stop in ((first, end), (end, n)):
                if start == stop:
                    continue
                scores = dot_last(keys[j][first:end], query[start:stop])
                weights = jnp.exp2(scores * SCALE_LOG2 - logs[j][:, start:stop])
                if start == first:
                    weights = jnp.where(allowed, weights, 0.0)
                grad_weights = dot_last(values[j][first:end], grad[start:stop])
                grad_scores = (weights * (grad_weights - inner[j][:, start:stop])).astype(BF16)
                grad_value = grad_value + dot(weights.astype(BF16), grad[start:stop])
                grad_key = grad_key + dot(grad_scores, query[start:stop])
                part = dot(key_turned[j * HEAD : (j + 1) * HEAD, first:end], grad_scores)
                if i == 0:
                    turned[j * HEAD : (j + 1) * HEAD, start:stop] = part
                else:
                    turned[j * HEAD : (j + 1) * HEAD, start:stop] += part
            found.append((grad_key, grad_value))
        (key_a, value_a), (key_b, value_b) = found
        projected[first:end, columns(1)] = (jnp.where(low, key_a, key_b) * SCORE_SCALE).astype(BF16)
        projected[first:end, columns(2)] = jnp.where(low, value_a, value_b).astype(BF16)
    projected[:, columns(0)] = (turned[...].T * SCORE_SCALE).astype(BF16)


PLAN_MESH = (4, 4)
GATHER_ACROSS = (11, 15, 19)
REDUCE_ACROSS = (3, 7, 15, 19)
PLAN = {
    "s0": (0, 10,),
    "s1": (110, 20, 150, 190,),
    "s3": (40, 111, 151, 191,),
    "w0": (1, 11, 21, 2, 41, 3, 80, 50, 12, 30, 4, 22, 42, 81, 51, 13,),
    "w1": (31, 82, 90, 23, 60, 100, 14, 91, 43, 70, 112,),
    "w2": (83, 24, 52,),
    "q0": (32, 92, 61, 101,),
    "q1": (53, 71,),
    "q2": (113,),
    "q3": (33,),
    "h0": (93,),
    "h2": (62, 120, 160,),
    "h3": (102, 34, 130,),
    "h4": (72, 170,),
    "h5": (121,),
    "h6": (63, 161, 131,),
    "h7": (103, 171,),
    "o0": (140,),
    "o1": (73, 180,),
    "o2": (152,),
    "o3": (122,),
    "d1": (162,),
    "e0": (132,),
    "t0.0": (123, 141, 181,),
    "t1.0": (163, 153,),
    "t0.1": (133,),
    "t2.1": (172, 192,),
    "t0.2": (142,),
    "t1.2": (182,),
    "t0.3": (173,),
    "t1.3": (143, 193,),
    "e1": (183,),
    "e1r": (1000, 1030,),
    "t0.4": (1040,),
    "t2.4": (1070,),
    "t0.5": (1001, 1010,),
    "t2.5": (1041,),
    "t0.6": (1031, 1050,),
    "t2.6": (1011,),
    "t0.7": (1002, 1020,),
    "t1.7": (1042, 1051, 1012,),
    "t2.7": (1003, 1032, 1060, 1071,),
    "b0": (1004, 1033, 1021, 1061, 1043,),
    "b1": (1013, 1034, 1080,),
    "b2": (1052, 1022, 1044, 1072, 1120,),
    "b3": (1014, 1062, 1150,),
    "wo2": (1073, 1190, 1081, 1090,),
    "a0": (1074, 1121,),
    "a1": (1053, 1023, 1130,),
    "a2": (1063, 1091, 1151, 1100,),
    "a3": (1054, 1024,),
    "a4": (1064, 1131, 1140,),
    "a5": (1082, 1122, 1152, 1101,),
    "a6": (1092, 1110, 1083,),
    "a7": (1153, 1123, 1093, 1141, 1084,),
    "p0": (1154, 1132, 1102, 1111, 1160,),
    "p1": (1191, 1124, 1094, 1161, 1170,),
    "p2": (1180,),
    "i0": (1171, 1133, 1103,),
    "i1": (1142, 1162,),
    "i2": (1192, 1181, 1134, 1104,),
    "i3": (1172,),
    "m0": (1143,),
    "m1": (1112, 1182,),
    "m2": (1193, 1144, 1163, 1173,),
    "m3": (1194, 1113, 1183,),
    "m4": (1164,),
    "end": (1114, 1174, 1184,),
}


def aligned(hidden_share):
    return hidden_share % 128 == 0


def split_columns(whole, parts, hidden_share):
    width = parts.shape[-1]
    for chunk in range(CHUNKS):
        if not aligned(hidden_share):
            parts[chunk] = whole[:, :, chunk * width : (chunk + 1) * width]
            continue
        for chip in range(width // hidden_share):
            first = (chip * CHUNKS + chunk) * hidden_share
            parts[chunk, :, :, chip * hidden_share : (chip + 1) * hidden_share] = whole[
                :, :, first : first + hidden_share
            ]


def join_columns(parts, whole, hidden_share):
    width = parts.shape[-1]
    for chunk in range(CHUNKS):
        if not aligned(hidden_share):
            whole[:, :, chunk * width : (chunk + 1) * width] = parts[chunk].astype(F32)
            continue
        for chip in range(width // hidden_share):
            first = (chip * CHUNKS + chunk) * hidden_share
            whole[:, :, first : first + hidden_share] = parts[
                chunk, :, :, chip * hidden_share : (chip + 1) * hidden_share
            ].astype(F32)


def block_kernel(nz, nx, tokens, cotangent, ids, small, w_qkv, w_out, in_shard, hidden_own):
    n, d = tokens.shape
    heads = d // 128
    depth = w_qkv.shape[0]
    share = small[0].shape[1]
    hidden_share = hidden_own.shape[1]
    width = in_shard.shape[2] // CHUNKS
    tile = nx * hidden_share
    tiles = width // tile
    count = 2 * MOST
    cut = width // CUTS
    hidden_cut = hidden_share // CUTS
    in_tail, hidden_tail = (2, depth, cut), (hidden_cut, d)
    small_rows = 10 + EXPERTS * CHUNKS * (width // d)
    small_rows += -small_rows % 8

    def bf16(*shape):
        return jax.ShapeDtypeStruct(shape, BF16)

    def f32(*shape):
        return jax.ShapeDtypeStruct(shape, F32)

    outputs = dict(
        block_out=bf16(n, d),
        input_grad=f32(n, d),
        qkv_sum=bf16(depth, 3 * d),
        wo_sum=bf16(depth, d),
        in_sum=bf16(CHUNKS, EXPERTS, depth, width),
        hidden_sum=bf16(EXPERTS, hidden_share, d),
        pair_terms=bf16(4, nz, nx, depth, d),
        qkv_full=bf16(nz, nx, 2, depth, 3 * d),
        wo_full=bf16(nz, nx, 2, depth, d),
        grad_rows=bf16(2, MOST, d),
        rows=bf16(2, MOST, d),
        made_rows=bf16(2, MOST, d),
        back_rows=bf16(2, MOST, d),
        in_full=bf16(CHUNKS, nz, nx, 2, depth, width),
        hidden_full=bf16(CHUNKS, nz, nx, hidden_share, d),
        in_terms=bf16(CHUNKS, nz, nx, 2, depth, width),
        hidden_terms=bf16(CHUNKS, nz, nx, hidden_share, d),
        normed=bf16(n, d),
        qkv=bf16(n, 3 * d),
        attended=bf16(n, d),
        logs=f32(heads, 8, n),
        residual=f32(n, d),
    )
    small_outputs = dict(small_sum=f32(small_rows, d), counts=f32(8, 128))

    gather_order = ["x" if piece in GATHER_ACROSS and nz == nx else "z" for piece in range(20)]
    reduce_order = ["x" if piece in REDUCE_ACROSS and nz == nx else "z" for piece in range(20)]
    landings = []
    for chunk in range(CHUNKS):
        for i in range(2 * CUTS):
            tail = in_tail if i < CUTS else hidden_tail
            landings.append(landing_shapes(nz, nx, tail, reduce_order[chunk * 2 * CUTS + i]))
    per_piece = len(landings[0])
    landing_scratch = [pltpu.VMEM(shape, BF16) for shapes in landings for shape in shapes]
    spares = [
        pltpu.VMEM(landing_shapes(nz, nx, tail, order)[0], BF16) for tail in (in_tail, hidden_tail) for order in "zx"
    ]
    partners = nz.bit_length() - 1 + nx.bit_length() - 1 + 1

    names = list(outputs) + list(small_outputs)

    def kernel(*refs):
        (
            tokens_hbm, cot_hbm, ids_ref, gain_ref, shift_ref, attn_bias_ref, out_bias_ref, in_bias_ref,
            qkv_own, wo_own, in_shard, hidden_own,
        ) = refs[:12]
        out = dict(zip(names, refs[12 : 12 + len(names)]))
        rest = refs[12 + len(names) :]
        slots, small_own, small_full, in_bias, out_bias, bias_sums, vectors, terms, terms_landing, free = rest[:10]
        spare = rest[10:14]
        landing = rest[14 : 14 + len(landing_scratch)]
        made = Copies(*rest[14 + len(landing_scratch) :])

        place = Place(nz, nx)
        z, xy, core = place.z, place.xy, place.core
        sums = terms.at[0]
        total = Total(place, made, terms, terms_landing)

        def columns_of(ref, part):
            return lambda zs, xs: [ref.at[zs, xs, core, :, pl.ds(part * d, d)]]

        def with_small(zs, xs):
            return [out["qkv_full"].at[zs, xs, core, :, pl.ds(2 * d, d)], small_full.at[zs, xs, core]]

        regions = [columns_of(out["qkv_full"], 0), columns_of(out["qkv_full"], 1), with_small, columns_of(out["wo_full"], 0)]
        gathered = [(order, region, region(ALL, ALL)) for order, region in zip(gather_order, regions)]
        for chunk in range(CHUNKS):
            for i in range(CUTS):
                at_columns = pl.ds(i * cut, cut)
                gathered.append(
                    (gather_order[len(gathered)], lambda zs, xs, c=chunk, s=at_columns: [out["in_full"].at[c, zs, xs, :, :, s]], None)
                )
            for i in range(CUTS):
                at_rows = pl.ds(i * hidden_cut, hidden_cut)
                gathered.append(
                    (gather_order[len(gathered)], lambda zs, xs, c=chunk, s=at_rows: [out["hidden_full"].at[c, zs, xs, s]], None)
                )
        gather = Gather("gather", place, made, gathered)

        pieces = []
        for chunk in range(CHUNKS):
            for i in range(2 * CUTS):
                at = len(pieces)
                order = reduce_order[at]
                mine = landing[at * per_piece : (at + 1) * per_piece]
                spare_now = spare[i // CUTS * 2 + (order == "x")]
                if i < CUTS:
                    at_columns = pl.ds(i * cut, cut)
                    pieces.append(
                        (
                            order, mine, spare_now,
                            lambda zs, xs, c=chunk, s=at_columns: out["in_terms"].at[c, zs, xs, :, :, s],
                            lambda expert, c=chunk, s=at_columns: out["in_sum"].at[c, expert, :, s],
                            "both",
                        )
                    )
                else:
                    at_rows = pl.ds((i - CUTS) * hidden_cut, hidden_cut)
                    pieces.append(
                        (
                            order, mine, spare_now,
                            lambda zs, xs, c=chunk, s=at_rows: out["hidden_terms"].at[c, zs, xs, s],
                            lambda expert, s=at_rows: out["hidden_sum"].at[expert, s],
                            chunk,
                        )
                    )
        reduce = Reduce("reduce", place, made, pieces)
        schedule = Schedule(place)
        schedule.streams.update({0: gather, 1: reduce})

        def first_phase(cot, picked, shard, in_own, qkv, wo, hidden):
            def load(name, source, target):
                copy = made.local(("first", name), source, target)
                copy.start()
                return copy

            loads = [load("qkv", qkv_own, qkv), load("wo", wo_own, wo), load("hidden", hidden_own, hidden)]
            load_shard = load("shard", in_shard, shard)
            load_cot = load("cot", cot_hbm, cot)
            place.barrier()
            loads[0].wait()
            near = [load("own qkv", qkv, out["qkv_full"].at[z, xy, core])]
            loads[1].wait()
            near.append(load("own wo", wo, out["wo_full"].at[z, xy, core]))
            for copy in near:
                copy.wait()
            schedule.at("s0")
            loads[2].wait()
            late = [load("own hidden", hidden.at[core], out["hidden_full"].at[core, z, xy])]
            pair = [made.far("pair hidden", hidden.at[1 - core], out["hidden_full"].at[core, z, xy], place.sibling())]
            load_shard.wait()
            split_columns(shard, in_own, hidden_share)
            for chunk in range(CHUNKS):
                target = out["in_full"].at[chunk, z, xy, core]
                late.append(load(("own in", chunk), in_own.at[chunk, core], target))
                pair.append(made.far(("pair in", chunk), in_own.at[chunk, 1 - core], target, place.sibling()))
            for copy in pair:
                copy.start()
            count_second = find_slots(slots, ids_ref, core)
            pack_small(small_own, (gain_ref, shift_ref, attn_bias_ref, out_bias_ref, in_bias_ref), count_second)
            small_full[z, xy, core] = small_own[...].astype(BF16)
            for copy in late + pair:
                copy.wait()
            schedule.at("s1")
            load_cot.wait()
            pick_rows(picked.at[1], slots[1:2, :], cot[...])
            theirs = made.far("grad rows", picked.at[1], out["grad_rows"].at[1], place.sibling())
            theirs.start()
            schedule.at("s2")
            pick_rows(picked.at[0], slots[0:1, :], cot[...])
            mine = made.local("grad rows", picked.at[0], out["grad_rows"].at[0])
            mine.start()
            schedule.at("s3")
            mine.wait()
            theirs.wait()

        pl.run_scoped(
            first_phase,
            pltpu.VMEM((n, d), BF16),
            pltpu.VMEM((2, MOST, d), BF16),
            pltpu.VMEM((EXPERTS, depth, CHUNKS * width), BF16),
            pltpu.VMEM((CHUNKS, EXPERTS, depth, width), BF16),
            pltpu.VMEM((depth, 3 * d), BF16),
            pltpu.VMEM((depth, d), BF16),
            pltpu.VMEM((EXPERTS, hidden_share, d), BF16),
        )

        def forward_phase(tok, w, wo, normed, qkv, attended, logs, residual, normed_two, picked):
            load = made.local("tokens", tokens_hbm, tok)
            load.start()
            loads = []
            for part in range(3):
                schedule.need(f"w{part}", gather, [part])
                at_columns = pl.ds(part * d, d)
                loads.append(
                    made.local(
                        ("w", part), out["qkv_full"].at[:, :, :, :, at_columns], w.at[:, :, :, :, at_columns]
                    )
                )
                loads[-1].start()
            unpack_small(small_full, core, d, share, hidden_share, vectors, in_bias, out_bias, out["counts"])
            load.wait()
            for copy in loads:
                copy.wait()

            @pl.loop(0, n // BLOCK)
            def _(i):
                rows = pl.ds(pl.multiple_of(i * BLOCK, BLOCK), BLOCK)
                scaled, _ = row_stats(tok[rows].astype(F32))
                normed[rows] = (scaled * vectors[0:1, :d] + vectors[1:2, :d]).astype(BF16)
                weight = as_rows(w[...], d)
                qkv[rows] = (dot(normed[rows], weight) + vectors[2:3, :]).astype(BF16)
                schedule.in_loop(i, "q", n // BLOCK)

            saves = [
                made.local("save normed", normed, out["normed"]),
                made.local("save qkv", qkv, out["qkv"]),
            ]
            for save in saves:
                save.start()

            @pl.loop(0, heads)
            def _(head):
                attend_pair(qkv, head, attended, logs)
                schedule.in_loop(head, "h", heads)

            saves += [
                made.local("save attended", attended, out["attended"]),
                made.local("save logs", logs, out["logs"]),
            ]
            for save in saves[2:]:
                save.start()
            schedule.need("wo", gather, [3])
            load_wo = made.local("wo", out["wo_full"], wo)
            load_wo.start()
            load_wo.wait()

            @pl.loop(0, n // BLOCK)
            def _(i):
                rows = pl.ds(pl.multiple_of(i * BLOCK, BLOCK), BLOCK)
                added = dot(attended[rows], as_rows(wo[...], d)) + vectors[0:1, 2 * d :]
                residual[rows] = tok[rows].astype(F32) + added
                scaled, _ = row_stats(residual[rows])
                normed_two[rows] = (scaled * vectors[0:1, d : 2 * d] + vectors[1:2, d : 2 * d]).astype(BF16)
                schedule.in_loop(i, "o", n // BLOCK)


            saves.append(made.local("save residual", residual, out["residual"]))
            saves[-1].start()
            pick_rows(picked.at[1], slots[1:2, :], normed_two[...])
            theirs = made.far("rows", picked.at[1], out["rows"].at[1], place.sibling())
            theirs.start()
            schedule.at("d0")
            pick_rows(picked.at[0], slots[0:1, :], normed_two[...])
            saves.append(made.local("rows", picked.at[0], out["rows"].at[0]))
            saves[-1].start()
            schedule.at("d1")
            for save in saves:
                save.wait()
            theirs.wait()

        pl.run_scoped(
            forward_phase,
            pltpu.VMEM((n, d), BF16),
            pltpu.VMEM((nz, nx, 2, depth, 3 * d), BF16),
            pltpu.VMEM((nz, nx, 2, depth, d), BF16),
            pltpu.VMEM((n, d), BF16),
            pltpu.VMEM((n, 3 * d), BF16),
            pltpu.VMEM((n, d), BF16),
            pltpu.VMEM((heads, 8, n), F32),
            pltpu.VMEM((n, d), F32),
            pltpu.VMEM((n, d), BF16),
            pltpu.VMEM((2, MOST, d), BF16),
        )

        def expert_phase(rows, grads, turned, made_total, back_total, w_in, w_hidden, grad_in, grad_hidden):
            loads = [
                made.local("load rows", out["rows"], rows),
                made.local("load grads", out["grad_rows"], grads),
            ]
            for copy in loads:
                copy.start()

            def weights(step):
                slot, chunk, t = lax.rem(step, 2), lax.div(step, tiles), lax.rem(step, tiles)
                at_columns = pl.ds(pl.multiple_of(t * tile, tile), tile)
                return [
                    made.local("w in", out["in_full"].at[chunk, :, :, :, :, at_columns], w_in.at[slot]),
                    made.local("w hidden", out["hidden_full"].at[chunk, t], w_hidden.at[slot]),
                ]

            def stores(step):
                chunk, t = lax.div(step, tiles), lax.rem(step, tiles)
                at_columns = pl.ds(pl.multiple_of(t * tile, tile), tile)
                return [
                    made.local("store in", grad_in, out["in_terms"].at[chunk, :, :, :, :, at_columns]),
                    made.local("store hidden", grad_hidden, out["hidden_terms"].at[chunk, t]),
                ]

            terms[0] = jnp.zeros(terms.shape[1:], F32)
            made_total[...] = jnp.zeros_like(made_total)
            back_total[...] = jnp.zeros_like(back_total)
            for copy in loads:
                copy.wait()
            turned[...] = as_rows(rows[...], count).T
            line = jnp.sum(as_rows(grads[...], count).astype(F32), axis=0, keepdims=True)
            for expert in range(EXPERTS):
                sums[8 + expert : 9 + expert, :] = jnp.where(core == expert, line, 0.0)

            @pl.loop(0, CHUNKS * tiles)
            def _(step):
                slot = lax.rem(step, 2)
                for chunk in range(CHUNKS):
                    @pl.when(step == chunk * tiles)
                    def _(chunk=chunk):
                        schedule.need(f"e{chunk}", gather, range(4 + chunk * 2 * CUTS, 4 + (chunk + 1) * 2 * CUTS))
                        for copy in weights(step):
                            copy.start()
                        if chunk:
                            schedule.at("e1r")

                for copy in weights(step):
                    copy.wait()

                @pl.when(lax.rem(step, tiles) != tiles - 1)
                def _():
                    for copy in weights(step + 1):
                        copy.start()

                def beside(spot):
                    schedule.in_loop(step, f"t{spot}.", CHUNKS * tiles)

                rows_now, grads_now = as_rows(rows[...], count), as_rows(grads[...], count)
                w_in_now = as_rows(w_in[slot], d)
                w_hidden_now = as_rows(w_hidden[slot], tile)
                hidden_pre = dot(rows_now, w_in_now) + in_bias[step, 0:1, :]
                hidden, slope = gelu_and_slope(hidden_pre)
                hidden = hidden.astype(BF16)
                grad_pre = dot_last(grads_now, w_hidden_now) * slope
                bias_sums[step, 0:1, :] = jnp.sum(grad_pre, axis=0, keepdims=True)
                grad_pre = grad_pre.astype(BF16)
                beside(0)
                made_total[...] += dot(hidden, w_hidden_now)
                back_total[...] += dot_last(grad_pre, w_in_now)
                beside(1)

                @pl.when(lax.rem(step, tiles) >= 1)
                def _():
                    for copy in stores(step - 1):
                        copy.wait()

                grad_hidden[...] = split_rows(dot(hidden.T, grads_now).astype(BF16), (nx, hidden_share, d))
                grad_in[...] = split_rows(dot(turned[...], grad_pre).astype(BF16), (nz, nx, 2, depth, tile))
                for copy in stores(step):
                    copy.start()
                beside(2)

                @pl.when(lax.rem(step, tiles) == tiles - 1)
                def _():
                    for copy in stores(step):
                        copy.wait()

            rows[...] = split_rows((made_total[...] + out_bias[0:1, :]).astype(BF16), (2, MOST, d))
            grads[...] = split_rows(back_total[...].astype(BF16), (2, MOST, d))
            results = []
            for name, source in (("made_rows", rows), ("back_rows", grads)):
                results.append(made.far(name, source.at[1], out[name].at[1], place.sibling()))
                results.append(made.local(name, source.at[0], out[name].at[0]))
            for copy in results:
                copy.start()
            schedule.at("x")
            for copy in results:
                copy.wait()

        pl.run_scoped(
            expert_phase,
            pltpu.VMEM((2, MOST, d), BF16),
            pltpu.VMEM((2, MOST, d), BF16),
            pltpu.VMEM((d, count), BF16),
            pltpu.VMEM((count, d), F32),
            pltpu.VMEM((count, d), F32),
            pltpu.VMEM((2, nz, nx, 2, depth, tile), BF16),
            pltpu.VMEM((2, nx, hidden_share, d), BF16),
            pltpu.VMEM((nz, nx, 2, depth, tile), BF16),
            pltpu.VMEM((nx, hidden_share, d), BF16),
        )

        def backward_phase(grad_res, branch, grad_att, att, projected, normed, wide, acc):
            def load(name, source, target):
                copy = made.local(("back", name), source, target)
                copy.start()
                return copy

            late_loads = [load("att", out["attended"], att), load("normed", out["normed"], normed)]

            for i in range(4):
                at = CUTS + i
                columns = pl.ds(i * d, d)
                pieces.append(
                    PairPiece(
                        reduce_order[len(pieces)],
                        lambda which, spot=(1, 2, 0, 0)[i]: wide.at[spot, :, :, which],
                        out["pair_terms"].at[i],
                        acc.at[i],
                        landing[at * per_piece : (at + 1) * per_piece],
                        out["wo_sum"] if i == 3 else out["qkv_sum"].at[:, columns],
                    )
                )

            def residual_phase(made_rows, back_rows, cot, wo, block, slots_turned):
                loads = [
                    load("residual", out["residual"], grad_res),
                    load("made", out["made_rows"], made_rows),
                    load("back", out["back_rows"], back_rows),
                    load("cot", cot_hbm, cot),
                    load("wo", out["wo_full"], wo),
                ]
                slots_turned[...] = slots[...].astype(F32).T
                for copy in loads:
                    copy.wait()

                @pl.loop(0, n // BLOCK)
                def _(i):
                    rows = pl.ds(pl.multiple_of(i * BLOCK, BLOCK), BLOCK)
                    columns = lax.broadcasted_iota(jnp.int32, (BLOCK, MOST), 1).astype(F32)
                    chosen = jnp.concatenate(
                        [
                            jnp.where(columns == slots_turned[rows, k : k + 1], 1.0, 0.0).astype(BF16)
                            for k in range(2)
                        ],
                        axis=1,
                    )
                    values = grad_res[rows]
                    block[rows] = (values + dot(chosen, as_rows(made_rows[...], count))).astype(BF16)
                    grad = dot(chosen, as_rows(back_rows[...], count))
                    term, gain_sum, shift_sum = norm_backward(values, vectors[0:1, d : 2 * d], grad)
                    sums[1:2, :] += gain_sum
                    sums[3:4, :] += shift_sum
                    now = cot[rows].astype(F32) + term
                    grad_res[rows] = now
                    low = now.astype(BF16)
                    branch[rows] = low
                    sums[6:7, :] += jnp.sum(low.astype(F32), axis=0, keepdims=True)
                    grad_att[rows] = dot_last(low, as_rows(wo[...], d)).astype(BF16)
                    schedule.in_loop(i, "b", n // BLOCK)

                load("block", block, out["block_out"]).wait()

            pl.run_scoped(
                residual_phase,
                pltpu.VMEM((2, MOST, d), BF16),
                pltpu.VMEM((2, MOST, d), BF16),
                pltpu.VMEM((n, d), BF16),
                pltpu.VMEM((nz, nx, 2, depth, d), BF16),
                pltpu.VMEM((n, d), BF16),
                pltpu.VMEM((n, 8), F32),
            )
            for copy in late_loads:
                copy.wait()
            wide[0] = split_rows(dot(att[...].T, branch[...]).astype(BF16), wide.shape[1:])
            schedule.at("wo2")

            def attend_phase(qkv, logs, turned):
                loads = [load("qkv", out["qkv"], qkv), load("logs", out["logs"], logs)]
                for copy in loads:
                    copy.wait()

                @pl.loop(0, heads)
                def _(head):
                    attend_pair_backward(qkv, head, att, grad_att, logs, projected, turned)
                    schedule.in_loop(head, "a", heads)

            pl.run_scoped(
                attend_phase,
                pltpu.VMEM((n, 3 * d), BF16),
                pltpu.VMEM((heads, 8, n), F32),
                pltpu.VMEM((128, n), F32),
            )

            schedule.need("free", reduce, range(2 * CUTS))
            senders = place.partners()[:-1]
            for device in senders:
                pl.semaphore_signal(free, inc=1, device_id=device, device_id_type=MESH_ID)

            def input_phase(w, tok):
                loads = [load("w", out["qkv_full"], w), load("tok", tokens_hbm, tok)]
                normed_turned = normed[...].T
                for part in range(3):
                    columns = slice(part * d, (part + 1) * d)
                    wide[(1, 2, 0)[part]] = split_rows(
                        dot(normed_turned, projected[:, columns]).astype(BF16), wide.shape[1:]
                    )
                    if part == 1:
                        pl.semaphore_wait(free, len(senders))
                    schedule.at(f"p{part}")
                    if part == 1:
                        schedule.force(reduce, 19, 1)
                    if part != 1:
                        sums[4 + part // 2 : 5 + part // 2, :] = jnp.sum(
                            projected[:, columns].astype(F32), axis=0, keepdims=True
                        )
                for copy in loads:
                    copy.wait()

                @pl.loop(0, n // BLOCK)
                def _(i):
                    rows = pl.ds(pl.multiple_of(i * BLOCK, BLOCK), BLOCK)
                    grad = dot_last(projected[rows], as_rows(w[...], d))
                    term, gain_sum, shift_sum = norm_backward(tok[rows].astype(F32), vectors[0:1, :d], grad)
                    grad_res[rows] += term
                    sums[0:1, :] += gain_sum
                    sums[2:3, :] += shift_sum
                    schedule.in_loop(i, "i", n // BLOCK)

                save = load("input_grad", grad_res, out["input_grad"])
                lines = width // d
                for step in range(CHUNKS * tiles):
                    first = (step % tiles) * tile
                    for expert in range(EXPERTS):
                        row = 10 + expert * CHUNKS * lines + step // tiles * lines + first // d
                        sums[row : row + 1, first % d : first % d + tile] = jnp.where(
                            core == expert, bias_sums[step, 0:1, :], 0.0
                        )
                for stage in range(total.stages):
                    total.begin(stage)
                    schedule.at(f"m{stage}")
                    total.finish(stage)
                out["small_sum"][...] = terms[total.stages % 2]
                schedule.need("end", reduce, range(2 * CUTS, len(pieces)))
                save.wait()

            pl.run_scoped(
                input_phase, pltpu.VMEM((nz, nx, 2, depth, 3 * d), BF16), pltpu.VMEM((n, d), BF16)
            )

        pl.run_scoped(
            backward_phase,
            pltpu.VMEM((n, d), F32),
            pltpu.VMEM((n, d), BF16),
            pltpu.VMEM((n, d), BF16),
            pltpu.VMEM((n, d), BF16),
            pltpu.VMEM((n, 3 * d), BF16),
            pltpu.VMEM((n, d), BF16),
            pltpu.VMEM((3, nz, nx, 2, depth, d), BF16),
            pltpu.VMEM((4, nz, nx, depth, d), BF16),
        )

    exchanged = nz + nx
    results = pl.pallas_call(
        kernel,
        out_shape=list(outputs.values()) + list(small_outputs.values()),
        in_specs=[HBM, HBM] + [VMEM] * 6 + [HBM] * 4,
        out_specs=[HBM] * len(outputs) + [VMEM] * len(small_outputs),
        scratch_shapes=[
            pltpu.VMEM((8, n), jnp.int32),
            pltpu.VMEM((16, 128), F32),
            pltpu.VMEM((nz, nx, 2, 16, 128), BF16),
            pltpu.VMEM((CHUNKS * tiles, 8, tile), F32),
            pltpu.VMEM((8, d), F32),
            pltpu.VMEM((CHUNKS * tiles, 8, tile), F32),
            pltpu.VMEM((8, 3 * d), F32),
            pltpu.VMEM((2, small_rows, d), F32),
            pltpu.VMEM((partners, small_rows, d), F32),
            pltpu.SemaphoreType.REGULAR,
            *spares,
            *landing_scratch,
            *semaphores(40 * exchanged + 48, 16 * (max(nx, nz) // 2 + 2) + 56),
        ],
        compiler_params=pltpu.CompilerParams(
            collective_id=1, has_side_effects=True, vmem_limit_bytes=64 * MIB - 64 * 1024
        ),
        name="block",
    )(tokens, cotangent, ids, *small, w_qkv, w_out, in_shard, hidden_own)
    return dict(zip(names, results))


PARTS = 4


def result_kernel(nz, nx, block, running_load, share, hidden_share):
    devices = nz * nx * 2
    n, d = block["block_out"].shape
    depth, width = block["in_sum"].shape[2:]
    lines = width // d

    def kernel(
        block_hbm, input_hbm, qkv_ref, wo_ref, in_ref, hidden_ref, small_ref, counts_ref, load_ref,
        block_out, input_grad, gain, shift, qkv, attn_bias, wo, in_grad, in_bias, hidden, out_bias, counts, loads,
        block_buffer, input_buffer, here,
    ):
        copies = []
        for i in range(2 * PARTS):
            source, buffer, target = ((block_hbm, block_buffer, block_out), (input_hbm, input_buffer, input_grad))[i % 2]
            rows = pl.ds(i // 2 * (n // PARTS), n // PARTS)
            copies.append(
                (
                    pltpu.make_async_copy(source.at[rows], buffer.at[rows], here.at[2 * i]),
                    pltpu.make_async_copy(buffer.at[rows], target.at[rows], here.at[2 * i + 1]),
                )
            )
        for copy in copies:
            copy[0].start()
        for copy in copies:
            copy[0].wait()
            copy[1].start()
        core = lax.axis_index("core")
        chip = lax.axis_index("dp") * nx + lax.axis_index("xy")
        first = (chip * 2 + core) * share
        own = pltpu.roll(small_ref[...], lax.rem(d - first, d), axis=1)
        gain[...] = own[0:2, :share]
        shift[...] = own[2:4, :share]
        attn_bias[...] = own[4:7, :share]
        out_bias[...] = own[8:10, :share]
        first = chip * hidden_share
        rows = lax.broadcasted_iota(jnp.int32, small_ref.shape, 0)
        for expert in range(EXPERTS):
            row = 10 + (expert * CHUNKS + core) * lines + lax.div(first, d)
            line = jnp.sum(jnp.where(rows == row, small_ref[...], 0.0), axis=0, keepdims=True)
            line = pltpu.roll(jnp.broadcast_to(line, (8, d)), lax.rem(d - lax.rem(first, d), d), axis=1)
            in_bias[expert : expert + 1, :] = line[0:1, :hidden_share]
        qkv[...] = qkv_ref[...].astype(F32)
        wo[...] = wo_ref[...].astype(F32)
        hidden[...] = hidden_ref[...].astype(F32)
        join_columns(in_ref, in_grad, hidden_share)
        lane = lax.broadcasted_iota(jnp.int32, (1, 128), 1)
        digits = counts_ref[0:1, :]
        second = jnp.sum(jnp.where(lane == 0, digits * 32, jnp.where(lane == 1, digits, 0.0)))
        for expert, count in enumerate((n * devices - second, second)):
            counts[expert] = count.astype(jnp.int32)
            loads[expert] = 0.9 * load_ref[expert] + 0.1 * (count * (EXPERTS / (n * devices)))
        for copy in copies:
            copy[1].wait()

    def f32(*shape):
        return jax.ShapeDtypeStruct(shape, F32)

    scalars = pl.BlockSpec(memory_space=pltpu.SMEM)
    return pl.pallas_call(
        kernel,
        out_shape=[
            jax.ShapeDtypeStruct((n, d), BF16),
            f32(n, d),
            f32(2, share),
            f32(2, share),
            f32(depth, 3 * d),
            f32(3, share),
            f32(depth, d),
            f32(EXPERTS, depth, CHUNKS * width),
            f32(EXPERTS, hidden_share),
            f32(EXPERTS, hidden_share, d),
            f32(EXPERTS, share),
            jax.ShapeDtypeStruct((EXPERTS,), jnp.int32),
            f32(EXPERTS),
        ],
        in_specs=[HBM] * 2 + [VMEM] * 6 + [scalars],
        out_specs=[HBM] * 2 + [VMEM] * 9 + [scalars] * 2,
        scratch_shapes=[
            pltpu.VMEM((n, d), BF16),
            pltpu.VMEM((n, d), F32),
            pltpu.SemaphoreType.DMA((4 * PARTS,)),
        ],
        compiler_params=pltpu.CompilerParams(vmem_limit_bytes=60 * MIB),
        name="results",
    )(
        block["block_out"], block["input_grad"], block["qkv_sum"], block["wo_sum"], block["in_sum"], block["hidden_sum"],
        block["small_sum"], block["counts"], running_load,
    )


def shards(
    nz, nx, tokens, norm_gain, norm_bias, w_qkv, attn_bias, w_attn_out, expert_in, expert_in_bias, expert_out,
    expert_out_bias, expert_ids, running_load, cotangent,
):
    chips = nz * nx
    depth, width = expert_in.shape[1:]
    share, hidden_share = norm_gain.shape[1], expert_out.shape[1]

    if not aligned(hidden_share):
        expert_in = expert_in.reshape(EXPERTS, depth, chips, CHUNKS, hidden_share).swapaxes(2, 3)
        expert_in = expert_in.reshape(EXPERTS, depth, width)
    small = (norm_gain, norm_bias, attn_bias, expert_out_bias, expert_in_bias)
    ids = expert_ids.reshape(1, tokens.shape[0])
    block = block_kernel(nz, nx, tokens, cotangent, ids, small, w_qkv, w_attn_out, expert_in, expert_out)
    results = list(result_kernel(nz, nx, block, running_load, share, hidden_share))
    if not aligned(hidden_share):
        in_grad = results[7].reshape(EXPERTS, depth, CHUNKS, chips, hidden_share).swapaxes(2, 3)
        results[7] = in_grad.reshape(EXPERTS, depth, width)
    return tuple(results)


def solution(mesh):
    nz, nx = mesh.shape["dp"], mesh.shape["fsdp"] // 2
    fine = Mesh(mesh.devices.reshape(nz, nx, 2), ("dp", "xy", "core"))
    every = ("dp", "xy", "core")
    row, column, middle = P(every, None), P(None, every), P(None, every, None)
    return jax.shard_map(
        functools.partial(shards, nz, nx),
        mesh=fine,
        in_specs=(
            row, column, column, row, column, row, middle, column, middle, column, row, P(), row,
        ),
        out_specs=(row, row, column, column, row, column, row, middle, column, middle, column, P(), P()),
        check_vma=False,
    )
```

```python
import functools
import math

import jax
import jax.numpy as jnp
from jax import lax
from jax.experimental import pallas as pl
from jax.experimental.pallas import tpu as pltpu
from jax.sharding import Mesh, PartitionSpec as P

BF16 = jnp.bfloat16
F32 = jnp.float32
MESH_ID = pl.DeviceIdType.MESH

HEAD = 64
MOST = 640
EXPERTS = 2
CHUNKS = 2
CUTS = 4
AHEAD = 1
NORM_EPS = 1e-05
SCORE_SCALE = 0.125
SCALE_LOG2 = SCORE_SCALE * math.log2(math.e)
MASKED = -1e30
BLOCK = 256
MIB = 1 << 20
ALL = slice(None)
HBM = pl.BlockSpec(memory_space=pl.ANY)
VMEM = pl.BlockSpec(memory_space=pltpu.VMEM)


def dot(left, right):
    return lax.dot_general(left, right, (((1,), (0,)), ((), ())), preferred_element_type=F32)


def dot_last(left, right):
    return lax.dot_general(left, right, (((1,), (1,)), ((), ())), preferred_element_type=F32)


def row_stats(values):
    center = values - jnp.mean(values, axis=-1, keepdims=True)
    spread = jnp.mean(center * center, axis=-1, keepdims=True)
    inverse = lax.rsqrt(spread + NORM_EPS)
    return center * inverse, inverse


def as_rows(values, rows):
    if values.dtype == BF16 and values.shape[-2] % 16:
        return values.astype(F32).reshape(rows, values.shape[-1]).astype(BF16)
    return values.reshape(rows, values.shape[-1])


def split_rows(values, shape):
    if values.dtype == BF16 and shape[-2] % 16:
        return values.astype(F32).reshape(shape).astype(BF16)
    return values.reshape(shape)


class Place:
    def __init__(self, nz, nx):
        self.nz, self.nx = nz, nx
        self.bits_z, self.bits_x = nz.bit_length() - 1, nx.bit_length() - 1
        self.z, self.xy, self.core = lax.axis_index("dp"), lax.axis_index("xy"), lax.axis_index("core")
        self.flip_z = [(1 - 2 * lax.rem(lax.div(self.z, 2**k), 2)) * 2**k for k in range(self.bits_z)]
        self.flip_x = [(1 - 2 * lax.rem(lax.div(self.xy, 2**k), 2)) * 2**k for k in range(self.bits_x)]

    def step_x(self, k, core=None):
        core = self.core if core is None else core
        return (1 - core) * self.flip_x[k] + core * self.flip_x[self.bits_x - 1 - k]

    def span_x(self, which, core=None):
        return self.xy + sum(self.step_x(k, core) for k in range(self.bits_x) if which >> k & 1)

    def span_z(self, which):
        return self.z + sum(self.flip_z[k] for k in range(self.bits_z) if which >> k & 1)

    def partners(self):
        found = [(self.z + flip, self.xy, self.core) for flip in self.flip_z]
        found += [(self.z, self.xy + flip, self.core) for flip in self.flip_x]
        return found + [self.sibling()]

    def sibling(self):
        return (self.z, self.xy, 1 - self.core)

    def barrier(self):
        semaphore = pltpu.get_barrier_semaphore()
        partners = self.partners()
        for partner in partners:
            pl.semaphore_signal(semaphore, inc=1, device_id=partner, device_id_type=MESH_ID)
        pl.semaphore_wait(semaphore, len(partners))


class Copies:
    def __init__(self, send, recv, near):
        self.send, self.recv, self.near = send, recv, near
        self.far_names, self.near_names = {}, {}

    def far(self, name, src, dst, device):
        i = self.far_names.setdefault(name, len(self.far_names))
        return pltpu.make_async_remote_copy(
            src_ref=src, dst_ref=dst, send_sem=self.send.at[i], recv_sem=self.recv.at[i],
            device_id=device, device_id_type=MESH_ID,
        )

    def local(self, name, src, dst, slot=None):
        if slot is not None:
            self.near_names.setdefault((name, 0), len(self.near_names))
            self.near_names.setdefault((name, 1), len(self.near_names))
            return pltpu.make_async_copy(src, dst, self.near.at[self.near_names[name, 0] + slot])
        i = self.near_names.setdefault(name, len(self.near_names))
        return pltpu.make_async_copy(src, dst, self.near.at[i])


def semaphores(far, near):
    return [
        pltpu.SemaphoreType.DMA((far,)),
        pltpu.SemaphoreType.DMA((far,)),
        pltpu.SemaphoreType.DMA((near,)),
    ]


class Stream:
    def __init__(self, pieces):
        self.pieces = pieces
        self.begun = {}

    def advance(self, piece, stage):
        if stage > 0:
            self.finish(piece, stage - 1)
        self.begin(piece, stage)
        self.begun[piece] = stage

    def last(self, piece):
        return self.stages(self.pieces[piece]) - 1


class Schedule:
    def __init__(self, place):
        self.plan = PLAN if (place.nz, place.nx) == PLAN_MESH else None
        self.streams = {}

    def at(self, point):
        for item in (self.plan or {}).get(point, ()):
            self.streams[item // 1000].advance(item % 1000 // 10, item % 10)

    def in_loop(self, i, name, count):
        for k in range(count):
            if (self.plan or {}).get(f"{name}{k}"):
                @pl.when(i == k)
                def _(k=k):
                    self.at(f"{name}{k}")

    def need(self, point, stream, pieces):
        self.at(point)
        if self.plan is None:
            most = max(stream.last(piece) for piece in pieces)
            for now in range(len(pieces) + most):
                for stage in range(most, -1, -1):
                    if 0 <= now - stage < len(pieces):
                        piece = pieces[now - stage]
                        if stream.begun.get(piece, -1) < stage <= stream.last(piece):
                            stream.advance(piece, stage)
        for piece in pieces:
            stream.finish(piece, stream.last(piece))

    def force(self, stream, piece, stage):
        if self.plan is None:
            for now in range(stream.begun.get(piece, -1) + 1, stage + 1):
                stream.advance(piece, now)


class Gather(Stream):
    def __init__(self, name, place, copies, pieces):
        super().__init__(pieces)
        self.name, self.place, self.made = name, place, copies

    def stages(self, piece):
        return self.place.bits_z + self.place.bits_x + (piece[2] is not None)

    def copies(self, piece, stage):
        place = self.place
        order, region, to_sibling = self.pieces[piece]
        step_z = stage if order == "z" else stage - place.bits_x
        step_x = stage - place.bits_z if order == "z" else stage
        found = []
        if stage == place.bits_z + place.bits_x:
            found += [(ref, place.sibling()) for ref in to_sibling]
        elif 0 <= step_z < place.bits_z:
            bit = place.bits_z - 1 - step_z
            device = (place.z + place.flip_z[bit], place.xy, place.core)
            for held in range(2**step_z):
                held_xy = place.xy if order == "z" else ALL
                found += [(ref, device) for ref in region(place.span_z(held << (bit + 1)), held_xy)]
        else:
            device = (place.z, place.xy + place.step_x(step_x), place.core)
            for held in range(2**step_x):
                held_z = ALL if order == "z" else place.z
                found += [(ref, device) for ref in region(held_z, place.span_x(held))]
        return [
            self.made.far((self.name, piece, stage, i), ref, ref, device) for i, (ref, device) in enumerate(found)
        ]

    def begin(self, piece, stage):
        for copy in self.copies(piece, stage):
            copy.start()

    def finish(self, piece, stage):
        for copy in self.copies(piece, stage):
            copy.wait()


def add_up(total, landed):
    if len(total.shape) > 3:
        @pl.loop(0, total.shape[0])
        def _(i):
            add_up(total.at[i], landed.at[i])
    else:
        total[...] = (total[...].astype(F32) + landed[...].astype(F32)).astype(BF16)


class Reduce(Stream):
    def __init__(self, name, place, copies, pieces):
        super().__init__(pieces)
        self.name, self.place, self.made = name, place, copies

    def stages(self, piece):
        return self.place.bits_z + self.place.bits_x + 1

    def plan(self, piece, stage):
        place = self.place
        nx, bits_x, bits_z = place.nx, place.bits_x, place.bits_z
        pair = isinstance(self.pieces[piece], PairPiece)
        if pair:
            order, landing, acc = self.pieces[piece].order, self.pieces[piece].landing, self.pieces[piece].acc
            first, landed = False, landing[stage - 1]
            step = stage - 1
        else:
            order, landing, spare, source, _, _ = self.pieces[piece]
            acc, first, landed, step = landing[0], stage == 0, landing[stage], stage
        far, near, sums = [], [], []
        step_x = step if order == "z" else step - bits_z
        step_z = step - bits_x if order == "z" else step
        if 0 <= step_x < bits_x:
            k = bits_x - 1 - step_x
            device = (place.z, place.xy + place.step_x(k), place.core)
            for j in range(2**k):
                if first:
                    far.append((source(ALL, place.span_x(2**k + j)), acc.at[j], device))
                    near.append((source(ALL, place.span_x(j)), spare.at[j]))
                    sums.append((acc.at[j], spare.at[j]))
                elif order == "x":
                    at_z = place.z if pair else 0
                    far.append((acc.at[at_z, place.span_x(2**k + j)], landed.at[j], device))
                    sums.append((acc.at[at_z, place.span_x(j)], landed.at[j]))
                elif pair:
                    far.append((acc.at[:, place.span_x(2**k + j)], landed.at[j], device))
                    sums += [(acc.at[i, place.span_x(j)], landed.at[j, i]) for i in range(place.nz)]
                else:
                    far.append((acc.at[2**k + j], landed.at[j], device))
                    sums.append((acc.at[j], landed.at[j]))
        else:
            bit = step_z
            device = (place.z + place.flip_z[bit], place.xy, place.core)
            for s in range(2 ** (bits_z - 1 - bit)):
                upper = s << (bit + 1)
                if first:
                    far.append((source(place.span_z(upper + 1), ALL), acc.at[s], device))
                    near.append((source(place.span_z(upper), ALL), spare.at[s]))
                    sums.append((acc.at[s], spare.at[s]))
                elif order == "z":
                    at_xy = place.xy if pair else None
                    send, keep = place.span_z(upper + 2**bit), place.span_z(upper)
                    far.append((acc.at[send, at_xy] if pair else acc.at[0, send], landed.at[s], device))
                    sums.append((acc.at[keep, at_xy] if pair else acc.at[0, keep], landed.at[s]))
                else:
                    send = place.span_z(upper + 2**bit) if pair else (upper + 2**bit) // 2
                    keep = place.span_z(upper) if pair else upper // 2
                    far.append((acc.at[send], landed.at[s], device))
                    sums.append((acc.at[keep], landed.at[s]))
        return far, near, sums

    def made_copies(self, piece, stage, far, near):
        made = [
            self.made.far((self.name, piece, stage, i), src, dst, device) for i, (src, dst, device) in enumerate(far)
        ]
        return made + [self.made.local((self.name, piece, stage, i), src, dst) for i, (src, dst) in enumerate(near)]

    def deliver(self, piece, begin):
        place, core = self.place, self.place.core
        order, landing, _, _, target, owner = self.pieces[piece]
        mine = landing[0].at[0, place.z if order == "z" else place.xy]
        name = (self.name, piece, "last")

        def there(part):
            return self.made.far(name, part, target(core), place.sibling())

        def here(part):
            return self.made.local(name, part, target(core))

        if owner == "both":
            for copy in (there(mine.at[1 - core]), here(mine.at[core])):
                copy.start() if begin else copy.wait()
            return

        @pl.when(core == owner)
        def _():
            if begin:
                here(mine).start()
            else:
                here(mine).wait()
                there(mine).wait_recv()

        @pl.when(core != owner)
        def _():
            there(mine).start() if begin else there(mine).wait_send()

    def to_pair(self, piece):
        item, place = self.pieces[piece], self.place
        return self.made.far((self.name, piece, "pair"), item.source(1 - place.core), item.landed, place.sibling())

    def begin(self, piece, stage):
        pair = isinstance(self.pieces[piece], PairPiece)
        if pair and stage == 0:
            self.to_pair(piece).start()
            return
        if not pair and stage == self.stages(self.pieces[piece]) - 1:
            self.deliver(piece, True)
            return
        far, near, _ = self.plan(piece, stage)
        for copy in self.made_copies(piece, stage, far, near):
            copy.start()

    def finish(self, piece, stage):
        item, final = self.pieces[piece], stage == self.stages(self.pieces[piece]) - 1
        pair = isinstance(item, PairPiece)
        if pair and stage == 0:
            self.to_pair(piece).wait()
            here = self.made.local((self.name, piece, "pair"), item.landed, item.acc)
            here.start()
            here.wait()
            add_up(item.acc, item.source(self.place.core))
            return
        if final and not pair:
            self.deliver(piece, False)
            return
        far, near, sums = self.plan(piece, stage)
        for copy in self.made_copies(piece, stage, far, near):
            copy.wait()
        for total, landed in sums:
            add_up(total, landed)
        if final:
            here = self.made.local((self.name, piece, "last"), item.acc.at[self.place.z, self.place.xy], item.target)
            here.start()
            here.wait()


class PairPiece:
    def __init__(self, order, source, landed, acc, landing, target):
        self.order, self.source, self.landed, self.acc = order, source, landed, acc
        self.landing, self.target = landing, target


def landing_shapes(nz, nx, tail, order):
    bits_z, bits_x = nz.bit_length() - 1, nx.bit_length() - 1
    if order == "z":
        return [(2**k, nz) + tail for k in reversed(range(bits_x))] + [
            (2 ** (bits_z - 1 - bit),) + tail for bit in range(bits_z)
        ]
    return [(2 ** (bits_z - 1 - bit), nx) + tail for bit in range(bits_z)] + [
        (2**k,) + tail for k in reversed(range(bits_x))
    ]


class Total:
    def __init__(self, place, copies, terms, landing):
        self.place, self.made, self.terms, self.landing = place, copies, terms, landing
        self.stages = len(place.partners())

    def copy(self, stage):
        device = self.place.partners()[stage]
        return self.made.far(("total", stage), self.terms.at[stage % 2], self.landing.at[stage], device)

    def begin(self, stage):
        self.copy(stage).start()

    def finish(self, stage):
        self.copy(stage).wait()
        self.terms[(stage + 1) % 2] = self.terms[stage % 2] + self.landing[stage]


def one_hot(slots, count):
    rows = lax.broadcasted_iota(jnp.int32, (count, slots.shape[1]), 0)
    return jnp.where(rows == slots, 1.0, 0.0).astype(BF16)


def pick_rows(picked, slots, values):
    picked[...] = dot(one_hot(slots, picked.shape[0]), values).astype(BF16)


def find_slots(slots, ids_ref, core):
    n = ids_ref.shape[1]
    ids = ids_ref[...]
    second = jnp.where(ids == 1, 1.0, 0.0)
    earlier = lax.broadcasted_iota(jnp.int32, (n, n), 0) <= lax.broadcasted_iota(jnp.int32, (n, n), 1)
    before = dot(
        jnp.broadcast_to(second, (16, n)).astype(BF16), jnp.where(earlier, 1.0, 0.0).astype(BF16)
    )[0:1].astype(jnp.int32)
    rank = jnp.where(ids == 1, before - 1, lax.broadcasted_iota(jnp.int32, (1, n), 1) - before)
    own = ids == core
    slots[0:1, :] = jnp.where(own, rank, -1)
    slots[1:2, :] = jnp.where(own, -1, rank)
    slots[2:8, :] = jnp.full((6, n), -1, jnp.int32)
    return jnp.sum(second, axis=1, keepdims=True)


GAIN, SHIFT, ATTN_BIAS, OUT_BIAS, IN_BIAS, DIGITS = 0, 2, 4, 7, 9, 11


def pack_small(small, refs, count_second):
    small[...] = jnp.zeros_like(small)
    for row, ref in zip((GAIN, SHIFT, ATTN_BIAS, OUT_BIAS, IN_BIAS), refs):
        count, share = ref.shape
        small[row : row + count, :share] = ref[...].astype(F32)
    high = jnp.floor(count_second * (1 / 32))
    lane = lax.broadcasted_iota(jnp.int32, (1, 128), 1)
    small[DIGITS : DIGITS + 1, :] = jnp.where(lane == 0, high, jnp.where(lane == 1, count_second - 32 * high, 0.0))


def spread(shares, length, share, place_of, first=0):
    devices = shares.shape[0]
    lanes = lax.broadcasted_iota(jnp.int32, (128, length), 1)
    chosen = lax.rem(lanes, share) + first == lax.broadcasted_iota(jnp.int32, (128, length), 0)
    repeat = jnp.where(chosen, 1.0, 0.0)
    copies = dot(shares, repeat.astype(BF16))
    lanes = lax.broadcasted_iota(jnp.int32, (devices, length), 1)
    device = lax.broadcasted_iota(jnp.int32, (devices, length), 0)
    return jnp.sum(jnp.where(lax.div(lanes, share) == place_of(device), copies, 0.0), axis=0, keepdims=True)


def unpack_small(small_full, core, d, share, hidden_share, vectors, in_bias, out_bias, counts):
    nz, nx = small_full.shape[:2]
    devices = nz * nx * 2
    found = small_full[...].astype(F32).reshape(devices, 16, 128)

    def rows(row):
        return found[:, row, :].astype(BF16)

    def vector(shares):
        return spread(shares, d, share, lambda device: device)

    vectors[...] = jnp.zeros_like(vectors)
    for line, row, part in (
        (0, GAIN, 0), (0, GAIN + 1, 1), (0, ATTN_BIAS + 2, 2), (1, SHIFT, 0), (1, SHIFT + 1, 1),
        (2, ATTN_BIAS, 0), (2, ATTN_BIAS + 1, 2),
    ):
        vectors[line : line + 1, part * d : (part + 1) * d] = vector(rows(row))

    def of_expert(row):
        return jnp.where(core == 0, rows(row), rows(row + 1))

    out_bias[0:1, :] = vector(of_expert(OUT_BIAS))
    cut = hidden_share // CUTS
    for chunk in range(CHUNKS):
        for i in range(CUTS):
            in_bias[chunk * CUTS + i, 0:1, :] = spread(
                of_expert(IN_BIAS), in_bias.shape[2], cut,
                lambda device: jnp.where(lax.rem(device, 2) == chunk, lax.div(device, 2), -1), i * cut,
            )
    counts[...] = jnp.broadcast_to(jnp.sum(found[:, DIGITS, :], axis=0, keepdims=True), counts.shape)


def attend_pair(qkv, head, attended, log_total):
    n, d = attended.shape
    low = lax.broadcasted_iota(jnp.int32, (n, 128), 1) < HEAD
    one, zero = jnp.ones((), BF16), jnp.zeros((), BF16)
    query = qkv[:, pl.ds(pl.multiple_of(head * 128, 128), 128)]
    key = qkv[:, pl.ds(pl.multiple_of(d + head * 128, 128), 128)]
    value = qkv[:, pl.ds(pl.multiple_of(2 * d + head * 128, 128), 128)]
    values = [jnp.where(low, value, one), jnp.where(low, one, value)]
    queries = [jnp.where(low, query, zero), jnp.where(low, zero, query)]
    low = low[:BLOCK]
    allowed = lax.broadcasted_iota(jnp.int32, (BLOCK, BLOCK), 1) <= lax.broadcasted_iota(
        jnp.int32, (BLOCK, BLOCK), 0
    )
    for i in range(n // BLOCK):
        first, end = i * BLOCK, (i + 1) * BLOCK
        found = []
        for j in range(2):
            near = jnp.where(allowed, dot_last(queries[j][first:end], key[first:end]), MASKED)
            top = jnp.max(near, axis=-1, keepdims=True)
            if i:
                far = dot_last(queries[j][first:end], key[:first])
                top = jnp.maximum(top, jnp.max(far, axis=-1, keepdims=True))
            top = top * SCALE_LOG2
            out = dot(jnp.exp2(near * SCALE_LOG2 - top).astype(BF16), values[j][first:end])
            if i:
                out = out + dot(jnp.exp2(far * SCALE_LOG2 - top).astype(BF16), values[j][:first])
            found.append((out, top))
        (out_a, top_a), (out_b, top_b) = found
        total = pltpu.roll(jnp.where(low, out_b, out_a), HEAD, axis=1)
        attended[first:end, pl.ds(pl.multiple_of(head * 128, 128), 128)] = (
            jnp.where(low, out_a, out_b) / total
        ).astype(BF16)
        logs = (jnp.where(low, top_a, top_b) + jnp.log2(total)).T
        log_total[head, 0:1, first:end] = logs[0:1]
        log_total[head, 1:2, first:end] = logs[HEAD : HEAD + 1]


def gelu_and_slope(values):
    root = math.sqrt(2 / math.pi)
    cube = 0.044715
    square = values * values
    bent = jnp.tanh(values * (root + root * cube * square))
    half = 0.5 * (1 + bent)
    slope = half + 0.5 * values * (1 - bent * bent) * (root + 3 * root * cube * square)
    return values * half, slope


def norm_backward(values, gain, grad):
    scaled, inverse = row_stats(values)
    grad_scaled = grad * gain
    mean = jnp.mean(grad_scaled, axis=-1, keepdims=True)
    along = jnp.mean(grad_scaled * scaled, axis=-1, keepdims=True)
    term = inverse * (grad_scaled - mean - scaled * along)
    return term, jnp.sum(grad * scaled, axis=0, keepdims=True), jnp.sum(grad, axis=0, keepdims=True)


def attend_pair_backward(qkv, head, attended, grad, log_total, projected, turned):
    n, d = attended.shape
    low = lax.broadcasted_iota(jnp.int32, (n, 128), 1) < HEAD
    zero = jnp.zeros((), BF16)

    def columns(part):
        return pl.ds(pl.multiple_of(part * d + head * 128, 128), 128)

    query, key, value = (qkv[:, columns(part)] for part in range(3))
    grad = grad[:, columns(0)]
    product = (attended[:, columns(0)].astype(F32) * grad.astype(F32)).T
    inner = [jnp.sum(product[j * HEAD : (j + 1) * HEAD], axis=0, keepdims=True) for j in range(2)]
    logs = [log_total[head, j : j + 1, :] for j in range(2)]
    key_turned = key.T
    keys = [jnp.where(low, key, zero), jnp.where(low, zero, key)]
    values = [jnp.where(low, value, zero), jnp.where(low, zero, value)]
    low = low[:BLOCK]
    allowed = lax.broadcasted_iota(jnp.int32, (BLOCK, BLOCK), 0) <= lax.broadcasted_iota(
        jnp.int32, (BLOCK, BLOCK), 1
    )
    for i in range(n // BLOCK):
        first, end = i * BLOCK, (i + 1) * BLOCK
        found = []
        for j in range(2):
            grad_key = grad_value = 0.0
            for start, stop in ((first, end), (end, n)):
                if start == stop:
                    continue
                scores = dot_last(keys[j][first:end], query[start:stop])
                weights = jnp.exp2(scores * SCALE_LOG2 - logs[j][:, start:stop])
                if start == first:
                    weights = jnp.where(allowed, weights, 0.0)
                grad_weights = dot_last(values[j][first:end], grad[start:stop])
                grad_scores = (weights * (grad_weights - inner[j][:, start:stop])).astype(BF16)
                grad_value = grad_value + dot(weights.astype(BF16), grad[start:stop])
                grad_key = grad_key + dot(grad_scores, query[start:stop])
                part = dot(key_turned[j * HEAD : (j + 1) * HEAD, first:end], grad_scores)
                if i == 0:
                    turned[j * HEAD : (j + 1) * HEAD, start:stop] = part
                else:
                    turned[j * HEAD : (j + 1) * HEAD, start:stop] += part
            found.append((grad_key, grad_value))
        (key_a, value_a), (key_b, value_b) = found
        projected[first:end, columns(1)] = (jnp.where(low, key_a, key_b) * SCORE_SCALE).astype(BF16)
        projected[first:end, columns(2)] = jnp.where(low, value_a, value_b).astype(BF16)
    projected[:, columns(0)] = (turned[...].T * SCORE_SCALE).astype(BF16)


PLAN_MESH = (4, 4)
GATHER_ACROSS = (7, 11, 15, 17)
REDUCE_ACROSS = (7, 8, 14)
PLAN = {
    "s0": (0,),
    "s1": (10, 70, 110, 170, 150,),
    "s2": (1,),
    "s3": (20, 71,),
    "w0": (111, 171, 2, 11, 21, 151, 40, 12, 80, 3, 30, 41, 22, 81, 13, 31, 4, 50, 42, 90,),
    "w1": (82, 60, 51, 23, 14, 91, 100,),
    "w2": (43, 61, 120, 83, 101, 24, 72, 32,),
    "q0": (52, 121, 92,),
    "q1": (33, 112,),
    "q3": (53,),
    "h0": (73,),
    "h1": (34, 93,),
    "h2": (62,),
    "h3": (102, 113,),
    "h4": (122,),
    "h5": (63,),
    "h6": (103, 160,),
    "h7": (130,),
    "o0": (123, 161,),
    "o1": (131,),
    "o2": (140,),
    "o3": (162, 180,),
    "d0": (132, 172,),
    "e0": (163,),
    "t0.0": (133,),
    "t1.0": (141,),
    "t2.0": (181,),
    "t0.1": (142, 173,),
    "t1.1": (182,),
    "t2.1": (143,),
    "t0.2": (183, 190,),
    "t1.2": (152,),
    "t2.2": (1000,),
    "t1.3": (1040,),
    "t2.3": (191,),
    "t0.4": (153, 1001,),
    "t1.4": (192,),
    "t2.4": (1041,),
    "t0.5": (193, 1002,),
    "t1.5": (1042, 1010,),
    "t2.5": (1070,),
    "t0.6": (1050,),
    "t2.6": (1003, 1011,),
    "t0.7": (1043, 1051,),
    "t1.7": (1004, 1012, 1020,),
    "t2.7": (1044, 1052, 1060,),
    "x": (1071,),
    "b0": (1021,),
    "b1": (1013, 1061,),
    "b2": (1053, 1030,),
    "b3": (1014, 1022, 1072, 1120, 1062,),
    "wo2": (1054, 1190, 1080,),
    "a0": (1031,),
    "a1": (1023, 1073, 1121,),
    "a2": (1063, 1074, 1090,),
    "a3": (1024, 1032, 1064, 1130,),
    "a4": (1081, 1091,),
    "a5": (1131,),
    "a6": (1033, 1100,),
    "a7": (1122, 1150,),
    "free": (1034, 1092, 1082, 1132,),
    "p0": (1123, 1101, 1160, 1110, 1140,),
    "p1": (1170, 1191,),
    "p2": (1124, 1180,),
    "i0": (1093,),
    "i1": (1083, 1133, 1111,),
    "i2": (1192, 1102, 1084, 1094, 1151, 1141,),
    "i3": (1134, 1161,),
    "m0": (1171,),
    "m1": (1193,),
    "m2": (1103, 1142, 1162, 1112,),
    "m3": (1194, 1172,),
    "m4": (1104, 1143, 1113, 1181, 1152,),
    "end": (1144, 1163, 1114, 1173, 1153, 1182, 1164, 1174, 1154, 1183, 1184,),
}


def gathered_columns(pieces):
    found, at = None, 0
    for values, first, lanes in pieces:
        moved = pltpu.roll(values, (at - first) % 128, axis=values.ndim - 1) if at != first else values
        lane = lax.broadcasted_iota(jnp.int32, values.shape, values.ndim - 1)
        found = moved if found is None else jnp.where(lane >= at, moved, found)
        at += lanes
    return found


def whole_tiles(hidden_share):
    return hidden_share % 128 == 0


def split_columns(whole, parts, hidden_share):
    width = parts.shape[-1]
    cut = hidden_share // CUTS
    if not whole_tiles(hidden_share):
        for chunk in range(CHUNKS):
            parts[chunk] = whole[:, :, chunk * width : (chunk + 1) * width]
        return
    for expert in range(whole.shape[0]):
        for at in range(0, CHUNKS * width, 128):
            chunk, k, chip = at // width, at % width // (width // CUTS), at % (width // CUTS) // cut
            pieces = []
            for i in range(128 // cut):
                first = ((chip + i) * CHUNKS + chunk) * hidden_share + k * cut
                block = whole[expert, :, first // 128 * 128 : first // 128 * 128 + 128].astype(F32)
                pieces.append((block, first % 128, cut))
            parts[chunk, expert, :, at % width : at % width + 128] = gathered_columns(pieces).astype(BF16)


def join_columns(parts, whole, hidden_share):
    width = parts.shape[-1]
    cut = hidden_share // CUTS
    if not whole_tiles(hidden_share):
        for chunk in range(CHUNKS):
            whole[:, :, chunk * width : (chunk + 1) * width] = parts[chunk].astype(F32)
        return
    for expert in range(whole.shape[0]):
        for at in range(0, CHUNKS * width, 128):
            chip, chunk = at // hidden_share // CHUNKS, at // hidden_share % CHUNKS
            pieces = []
            for k in range(at % hidden_share // cut, at % hidden_share // cut + 128 // cut):
                first = k * (width // CUTS) + chip * cut
                block = parts[chunk, expert, :, first // 128 * 128 : first // 128 * 128 + 128].astype(F32)
                pieces.append((block, first % 128, cut))
            whole[expert, :, at : at + 128] = gathered_columns(pieces)


def block_kernel(nz, nx, tokens, cotangent, ids, small, w_qkv, w_out, in_shard, hidden_own):
    n, d = tokens.shape
    heads = d // 128
    depth = w_qkv.shape[0]
    share = small[0].shape[1]
    hidden_share = hidden_own.shape[1]
    width = in_shard.shape[2] // CHUNKS
    tile = width // CUTS
    tiles = CUTS
    count = 2 * MOST
    cut = width // CUTS
    hidden_cut = hidden_share // CUTS
    in_tail, hidden_tail = (2, depth, cut), (hidden_cut, d)
    small_rows = 10 + EXPERTS * CHUNKS * (width // d)
    small_rows += -small_rows % 8

    def bf16(*shape):
        return jax.ShapeDtypeStruct(shape, BF16)

    def f32(*shape):
        return jax.ShapeDtypeStruct(shape, F32)

    outputs = dict(
        block_out=bf16(n, d),
        input_grad=f32(n, d),
        qkv_sum=bf16(depth, 3 * d),
        wo_sum=bf16(depth, d),
        in_sum=bf16(CHUNKS, EXPERTS, depth, width),
        hidden_sum=bf16(EXPERTS, hidden_share, d),
        pair_terms=bf16(4, nz, nx, depth, d),
        qkv_full=bf16(nz, nx, 2, depth, 3 * d),
        wo_full=bf16(nz, nx, 2, depth, d),
        grad_rows=bf16(2, MOST, d),
        rows=bf16(2, MOST, d),
        made_rows=bf16(2, MOST, d),
        back_rows=bf16(2, MOST, d),
        in_full=bf16(CHUNKS, nz, nx, 2, depth, width),
        hidden_full=bf16(CHUNKS, nz, nx, hidden_share, d),
        in_terms=bf16(CHUNKS, nz, nx, 2, depth, width),
        hidden_terms=bf16(CHUNKS, nz, nx, hidden_share, d),
        normed=bf16(n, d),
        qkv=bf16(n, 3 * d),
        attended=bf16(n, d),
        logs=f32(heads, 8, n),
        residual=f32(n, d),
    )
    small_outputs = dict(small_sum=f32(small_rows, d), counts=f32(8, 128))

    gather_order = ["x" if piece in GATHER_ACROSS and nz == nx else "z" for piece in range(20)]
    reduce_order = ["x" if piece in REDUCE_ACROSS and nz == nx else "z" for piece in range(20)]
    landings = []
    for chunk in range(CHUNKS):
        for i in range(2 * CUTS):
            tail = in_tail if i < CUTS else hidden_tail
            landings.append(landing_shapes(nz, nx, tail, reduce_order[chunk * 2 * CUTS + i]))
    per_piece = len(landings[0])
    landing_scratch = [pltpu.VMEM(shape, BF16) for shapes in landings for shape in shapes]
    spares = [
        pltpu.VMEM(landing_shapes(nz, nx, tail, order)[0], BF16) for tail in (in_tail, hidden_tail) for order in "zx"
    ]
    partners = nz.bit_length() - 1 + nx.bit_length() - 1 + 1

    names = list(outputs) + list(small_outputs)

    def kernel(*refs):
        (
            tokens_hbm, cot_hbm, ids_ref, gain_ref, shift_ref, attn_bias_ref, out_bias_ref, in_bias_ref,
            qkv_own, wo_own, in_shard, hidden_own,
        ) = refs[:12]
        out = dict(zip(names, refs[12 : 12 + len(names)]))
        rest = refs[12 + len(names) :]
        slots, small_own, small_full, in_bias, out_bias, bias_sums, vectors, terms, terms_landing, free = rest[:10]
        spare = rest[10:14]
        landing = rest[14 : 14 + len(landing_scratch)]
        made = Copies(*rest[14 + len(landing_scratch) :])

        place = Place(nz, nx)
        z, xy, core = place.z, place.xy, place.core
        sums = terms.at[0]
        total = Total(place, made, terms, terms_landing)

        def columns_of(ref, part):
            return lambda zs, xs: [ref.at[zs, xs, core, :, pl.ds(part * d, d)]]

        def with_small(zs, xs):
            return [out["qkv_full"].at[zs, xs, core, :, pl.ds(2 * d, d)], small_full.at[zs, xs, core]]

        regions = [columns_of(out["qkv_full"], 0), columns_of(out["qkv_full"], 1), with_small, columns_of(out["wo_full"], 0)]
        gathered = [(order, region, region(ALL, ALL)) for order, region in zip(gather_order, regions)]
        for chunk in range(CHUNKS):
            for i in range(CUTS):
                at_columns = pl.ds(i * cut, cut)
                gathered.append(
                    (gather_order[len(gathered)], lambda zs, xs, c=chunk, s=at_columns: [out["in_full"].at[c, zs, xs, :, :, s]], None)
                )
            for i in range(CUTS):
                at_rows = pl.ds(i * hidden_cut, hidden_cut)
                gathered.append(
                    (gather_order[len(gathered)], lambda zs, xs, c=chunk, s=at_rows: [out["hidden_full"].at[c, zs, xs, s]], None)
                )
        gather = Gather("gather", place, made, gathered)

        pieces = []
        for chunk in range(CHUNKS):
            for i in range(2 * CUTS):
                at = len(pieces)
                order = reduce_order[at]
                mine = landing[at * per_piece : (at + 1) * per_piece]
                spare_now = spare[i // CUTS * 2 + (order == "x")]
                if i < CUTS:
                    at_columns = pl.ds(i * cut, cut)
                    pieces.append(
                        (
                            order, mine, spare_now,
                            lambda zs, xs, c=chunk, s=at_columns: out["in_terms"].at[c, zs, xs, :, :, s],
                            lambda expert, c=chunk, s=at_columns: out["in_sum"].at[c, expert, :, s],
                            "both",
                        )
                    )
                else:
                    at_rows = pl.ds((i - CUTS) * hidden_cut, hidden_cut)
                    pieces.append(
                        (
                            order, mine, spare_now,
                            lambda zs, xs, c=chunk, s=at_rows: out["hidden_terms"].at[c, zs, xs, s],
                            lambda expert, s=at_rows: out["hidden_sum"].at[expert, s],
                            chunk,
                        )
                    )
        reduce = Reduce("reduce", place, made, pieces)
        schedule = Schedule(place)
        schedule.streams.update({0: gather, 1: reduce})

        def first_phase(cot, picked, shard, in_own, qkv, wo, hidden):
            def load(name, source, target):
                copy = made.local(("first", name), source, target)
                copy.start()
                return copy

            loads = [load("qkv", qkv_own, qkv), load("wo", wo_own, wo), load("hidden", hidden_own, hidden)]
            load_shard = load("shard", in_shard, shard)
            load_cot = load("cot", cot_hbm, cot)
            place.barrier()
            loads[0].wait()
            near = [load("own qkv", qkv, out["qkv_full"].at[z, xy, core])]
            loads[1].wait()
            near.append(load("own wo", wo, out["wo_full"].at[z, xy, core]))
            for copy in near:
                copy.wait()
            schedule.at("s0")
            loads[2].wait()
            late = [load("own hidden", hidden.at[core], out["hidden_full"].at[core, z, xy])]
            pair = [made.far("pair hidden", hidden.at[1 - core], out["hidden_full"].at[core, z, xy], place.sibling())]
            load_shard.wait()
            split_columns(shard, in_own, hidden_share)
            for chunk in range(CHUNKS):
                target = out["in_full"].at[chunk, z, xy, core]
                late.append(load(("own in", chunk), in_own.at[chunk, core], target))
                pair.append(made.far(("pair in", chunk), in_own.at[chunk, 1 - core], target, place.sibling()))
            for copy in pair:
                copy.start()
            count_second = find_slots(slots, ids_ref, core)
            pack_small(small_own, (gain_ref, shift_ref, attn_bias_ref, out_bias_ref, in_bias_ref), count_second)
            small_full[z, xy, core] = small_own[...].astype(BF16)
            for copy in late + pair:
                copy.wait()
            schedule.at("s1")
            load_cot.wait()
            pick_rows(picked.at[1], slots[1:2, :], cot[...])
            theirs = made.far("grad rows", picked.at[1], out["grad_rows"].at[1], place.sibling())
            theirs.start()
            schedule.at("s2")
            pick_rows(picked.at[0], slots[0:1, :], cot[...])
            mine = made.local("grad rows", picked.at[0], out["grad_rows"].at[0])
            mine.start()
            schedule.at("s3")
            mine.wait()
            theirs.wait()

        pl.run_scoped(
            first_phase,
            pltpu.VMEM((n, d), BF16),
            pltpu.VMEM((2, MOST, d), BF16),
            pltpu.VMEM((EXPERTS, depth, CHUNKS * width), BF16),
            pltpu.VMEM((CHUNKS, EXPERTS, depth, width), BF16),
            pltpu.VMEM((depth, 3 * d), BF16),
            pltpu.VMEM((depth, d), BF16),
            pltpu.VMEM((EXPERTS, hidden_share, d), BF16),
        )

        def forward_phase(tok, w, wo, normed, qkv, attended, logs, residual, normed_two, picked):
            load = made.local("tokens", tokens_hbm, tok)
            load.start()
            loads = []
            for part in range(3):
                schedule.need(f"w{part}", gather, [part])
                at_columns = pl.ds(part * d, d)
                loads.append(
                    made.local(
                        ("w", part), out["qkv_full"].at[:, :, :, :, at_columns], w.at[:, :, :, :, at_columns]
                    )
                )
                loads[-1].start()
            unpack_small(small_full, core, d, share, hidden_share, vectors, in_bias, out_bias, out["counts"])
            load.wait()
            for copy in loads:
                copy.wait()

            @pl.loop(0, n // BLOCK)
            def _(i):
                rows = pl.ds(pl.multiple_of(i * BLOCK, BLOCK), BLOCK)
                scaled, _ = row_stats(tok[rows].astype(F32))
                normed[rows] = (scaled * vectors[0:1, :d] + vectors[1:2, :d]).astype(BF16)
                weight = as_rows(w[...], d)
                qkv[rows] = (dot(normed[rows], weight) + vectors[2:3, :]).astype(BF16)
                schedule.in_loop(i, "q", n // BLOCK)

            saves = [
                made.local("save normed", normed, out["normed"]),
                made.local("save qkv", qkv, out["qkv"]),
            ]
            for save in saves:
                save.start()

            @pl.loop(0, heads)
            def _(head):
                attend_pair(qkv, head, attended, logs)
                schedule.in_loop(head, "h", heads)

            saves += [
                made.local("save attended", attended, out["attended"]),
                made.local("save logs", logs, out["logs"]),
            ]
            for save in saves[2:]:
                save.start()
            schedule.need("wo", gather, [3])
            load_wo = made.local("wo", out["wo_full"], wo)
            load_wo.start()
            load_wo.wait()

            @pl.loop(0, n // BLOCK)
            def _(i):
                rows = pl.ds(pl.multiple_of(i * BLOCK, BLOCK), BLOCK)
                added = dot(attended[rows], as_rows(wo[...], d)) + vectors[0:1, 2 * d :]
                residual[rows] = tok[rows].astype(F32) + added
                scaled, _ = row_stats(residual[rows])
                normed_two[rows] = (scaled * vectors[0:1, d : 2 * d] + vectors[1:2, d : 2 * d]).astype(BF16)
                schedule.in_loop(i, "o", n // BLOCK)


            saves.append(made.local("save residual", residual, out["residual"]))
            saves[-1].start()
            pick_rows(picked.at[1], slots[1:2, :], normed_two[...])
            theirs = made.far("rows", picked.at[1], out["rows"].at[1], place.sibling())
            theirs.start()
            schedule.at("d0")
            pick_rows(picked.at[0], slots[0:1, :], normed_two[...])
            saves.append(made.local("rows", picked.at[0], out["rows"].at[0]))
            saves[-1].start()
            schedule.at("d1")
            for save in saves:
                save.wait()
            theirs.wait()

        pl.run_scoped(
            forward_phase,
            pltpu.VMEM((n, d), BF16),
            pltpu.VMEM((nz, nx, 2, depth, 3 * d), BF16),
            pltpu.VMEM((nz, nx, 2, depth, d), BF16),
            pltpu.VMEM((n, d), BF16),
            pltpu.VMEM((n, 3 * d), BF16),
            pltpu.VMEM((n, d), BF16),
            pltpu.VMEM((heads, 8, n), F32),
            pltpu.VMEM((n, d), F32),
            pltpu.VMEM((n, d), BF16),
            pltpu.VMEM((2, MOST, d), BF16),
        )

        def expert_phase(rows, grads, turned, made_total, back_total, w_in, w_hidden, grad_in, grad_hidden):
            loads = [
                made.local("load rows", out["rows"], rows),
                made.local("load grads", out["grad_rows"], grads),
            ]
            for copy in loads:
                copy.start()

            def cut_rows(t):
                return pl.ds(pl.multiple_of(t * hidden_cut, hidden_cut), hidden_cut)

            def weights(step):
                slot, chunk, t = lax.rem(step, 2), lax.div(step, tiles), lax.rem(step, tiles)
                at_columns = pl.ds(pl.multiple_of(t * tile, tile), tile)
                return [
                    made.local("w in", out["in_full"].at[chunk, :, :, :, :, at_columns], w_in.at[slot]),
                    made.local("w hidden", out["hidden_full"].at[chunk, :, :, cut_rows(t)], w_hidden.at[slot]),
                ]

            def stores(step):
                chunk, t = lax.div(step, tiles), lax.rem(step, tiles)
                at_columns = pl.ds(pl.multiple_of(t * tile, tile), tile)
                return [
                    made.local("store in", grad_in, out["in_terms"].at[chunk, :, :, :, :, at_columns]),
                    made.local("store hidden", grad_hidden, out["hidden_terms"].at[chunk, :, :, cut_rows(t)]),
                ]

            terms[0] = jnp.zeros(terms.shape[1:], F32)
            made_total[...] = jnp.zeros_like(made_total)
            back_total[...] = jnp.zeros_like(back_total)
            for copy in loads:
                copy.wait()
            turned[...] = as_rows(rows[...], count).T
            line = jnp.sum(as_rows(grads[...], count).astype(F32), axis=0, keepdims=True)
            for expert in range(EXPERTS):
                sums[8 + expert : 9 + expert, :] = jnp.where(core == expert, line, 0.0)

            def arrive(step):
                chunk, t = step // tiles, step % tiles
                first = 4 + chunk * 2 * CUTS + t
                schedule.need(f"e{step}", gather, [first, first + CUTS])
                for copy in weights(step):
                    copy.start()

            arrive(0)

            @pl.loop(0, CHUNKS * tiles)
            def _(step):
                slot = lax.rem(step, 2)
                for copy in weights(step):
                    copy.wait()

                def beside(spot):
                    schedule.in_loop(step, f"t{spot}.", CHUNKS * tiles)

                rows_now, grads_now = as_rows(rows[...], count), as_rows(grads[...], count)
                w_in_now = as_rows(w_in[slot], d)
                w_hidden_now = as_rows(w_hidden[slot], tile)
                hidden_pre = dot(rows_now, w_in_now) + in_bias[step, 0:1, :]
                hidden, slope = gelu_and_slope(hidden_pre)
                hidden = hidden.astype(BF16)
                grad_pre = dot_last(grads_now, w_hidden_now) * slope
                bias_sums[step, 0:1, :] = jnp.sum(grad_pre, axis=0, keepdims=True)
                grad_pre = grad_pre.astype(BF16)
                beside(0)
                made_total[...] += dot(hidden, w_hidden_now)
                back_total[...] += dot_last(grad_pre, w_in_now)

                @pl.when(step >= 1)
                def _():
                    for copy in stores(step - 1):
                        copy.wait()

                beside(1)
                for k in range(1, CHUNKS * tiles):
                    @pl.when(step == k - 1)
                    def _(k=k):
                        arrive(k)

                grad_hidden[...] = split_rows(dot(hidden.T, grads_now).astype(BF16), (nz, nx, hidden_cut, d))
                grad_in[...] = split_rows(dot(turned[...], grad_pre).astype(BF16), (nz, nx, 2, depth, tile))
                for copy in stores(step):
                    copy.start()
                beside(2)

            for copy in stores(CHUNKS * tiles - 1):
                copy.wait()

            rows[...] = split_rows((made_total[...] + out_bias[0:1, :]).astype(BF16), (2, MOST, d))
            grads[...] = split_rows(back_total[...].astype(BF16), (2, MOST, d))
            results = []
            for name, source in (("made_rows", rows), ("back_rows", grads)):
                results.append(made.far(name, source.at[1], out[name].at[1], place.sibling()))
                results.append(made.local(name, source.at[0], out[name].at[0]))
            for copy in results:
                copy.start()
            schedule.at("x")
            for copy in results:
                copy.wait()

        pl.run_scoped(
            expert_phase,
            pltpu.VMEM((2, MOST, d), BF16),
            pltpu.VMEM((2, MOST, d), BF16),
            pltpu.VMEM((d, count), BF16),
            pltpu.VMEM((count, d), F32),
            pltpu.VMEM((count, d), F32),
            pltpu.VMEM((2, nz, nx, 2, depth, tile), BF16),
            pltpu.VMEM((2, nz, nx, hidden_cut, d), BF16),
            pltpu.VMEM((nz, nx, 2, depth, tile), BF16),
            pltpu.VMEM((nz, nx, hidden_cut, d), BF16),
        )

        def backward_phase(grad_res, branch, grad_att, att, projected, normed, wide, acc):
            def load(name, source, target):
                copy = made.local(("back", name), source, target)
                copy.start()
                return copy

            late_loads = [load("att", out["attended"], att), load("normed", out["normed"], normed)]

            for i in range(4):
                at = CUTS + i
                columns = pl.ds(i * d, d)
                pieces.append(
                    PairPiece(
                        reduce_order[len(pieces)],
                        lambda which, spot=(1, 2, 0, 0)[i]: wide.at[spot, :, :, which],
                        out["pair_terms"].at[i],
                        acc.at[i],
                        landing[at * per_piece : (at + 1) * per_piece],
                        out["wo_sum"] if i == 3 else out["qkv_sum"].at[:, columns],
                    )
                )

            def residual_phase(made_rows, back_rows, cot, wo, block, slots_turned):
                loads = [
                    load("residual", out["residual"], grad_res),
                    load("made", out["made_rows"], made_rows),
                    load("back", out["back_rows"], back_rows),
                    load("cot", cot_hbm, cot),
                    load("wo", out["wo_full"], wo),
                ]
                slots_turned[...] = slots[...].astype(F32).T
                for copy in loads:
                    copy.wait()

                @pl.loop(0, n // BLOCK)
                def _(i):
                    rows = pl.ds(pl.multiple_of(i * BLOCK, BLOCK), BLOCK)
                    columns = lax.broadcasted_iota(jnp.int32, (BLOCK, MOST), 1).astype(F32)
                    chosen = jnp.concatenate(
                        [
                            jnp.where(columns == slots_turned[rows, k : k + 1], 1.0, 0.0).astype(BF16)
                            for k in range(2)
                        ],
                        axis=1,
                    )
                    values = grad_res[rows]
                    block[rows] = (values + dot(chosen, as_rows(made_rows[...], count))).astype(BF16)
                    grad = dot(chosen, as_rows(back_rows[...], count))
                    term, gain_sum, shift_sum = norm_backward(values, vectors[0:1, d : 2 * d], grad)
                    sums[1:2, :] += gain_sum
                    sums[3:4, :] += shift_sum
                    now = cot[rows].astype(F32) + term
                    grad_res[rows] = now
                    low = now.astype(BF16)
                    branch[rows] = low
                    sums[6:7, :] += jnp.sum(low.astype(F32), axis=0, keepdims=True)
                    grad_att[rows] = dot_last(low, as_rows(wo[...], d)).astype(BF16)
                    schedule.in_loop(i, "b", n // BLOCK)

                load("block", block, out["block_out"]).wait()

            pl.run_scoped(
                residual_phase,
                pltpu.VMEM((2, MOST, d), BF16),
                pltpu.VMEM((2, MOST, d), BF16),
                pltpu.VMEM((n, d), BF16),
                pltpu.VMEM((nz, nx, 2, depth, d), BF16),
                pltpu.VMEM((n, d), BF16),
                pltpu.VMEM((n, 8), F32),
            )
            for copy in late_loads:
                copy.wait()
            wide[0] = split_rows(dot(att[...].T, branch[...]).astype(BF16), wide.shape[1:])
            schedule.at("wo2")

            def attend_phase(qkv, logs, turned):
                loads = [load("qkv", out["qkv"], qkv), load("logs", out["logs"], logs)]
                for copy in loads:
                    copy.wait()

                @pl.loop(0, heads)
                def _(head):
                    attend_pair_backward(qkv, head, att, grad_att, logs, projected, turned)
                    schedule.in_loop(head, "a", heads)

            pl.run_scoped(
                attend_phase,
                pltpu.VMEM((n, 3 * d), BF16),
                pltpu.VMEM((heads, 8, n), F32),
                pltpu.VMEM((128, n), F32),
            )

            schedule.need("free", reduce, range(2 * CUTS))
            senders = place.partners()[:-1]
            for device in senders:
                pl.semaphore_signal(free, inc=1, device_id=device, device_id_type=MESH_ID)

            def input_phase(w, tok):
                loads = [load("w", out["qkv_full"], w), load("tok", tokens_hbm, tok)]
                normed_turned = normed[...].T
                for part in range(3):
                    columns = slice(part * d, (part + 1) * d)
                    wide[(1, 2, 0)[part]] = split_rows(
                        dot(normed_turned, projected[:, columns]).astype(BF16), wide.shape[1:]
                    )
                    if part == 1:
                        pl.semaphore_wait(free, len(senders))
                    schedule.at(f"p{part}")
                    if part == 1:
                        schedule.force(reduce, 19, 1)
                    if part != 1:
                        sums[4 + part // 2 : 5 + part // 2, :] = jnp.sum(
                            projected[:, columns].astype(F32), axis=0, keepdims=True
                        )
                for copy in loads:
                    copy.wait()

                @pl.loop(0, n // BLOCK)
                def _(i):
                    rows = pl.ds(pl.multiple_of(i * BLOCK, BLOCK), BLOCK)
                    grad = dot_last(projected[rows], as_rows(w[...], d))
                    term, gain_sum, shift_sum = norm_backward(tok[rows].astype(F32), vectors[0:1, :d], grad)
                    grad_res[rows] += term
                    sums[0:1, :] += gain_sum
                    sums[2:3, :] += shift_sum
                    schedule.in_loop(i, "i", n // BLOCK)

                save = load("input_grad", grad_res, out["input_grad"])
                lines = width // d
                for step in range(CHUNKS * tiles):
                    first = (step % tiles) * tile
                    for expert in range(EXPERTS):
                        row = 10 + expert * CHUNKS * lines + step // tiles * lines + first // d
                        sums[row : row + 1, first % d : first % d + tile] = jnp.where(
                            core == expert, bias_sums[step, 0:1, :], 0.0
                        )
                for stage in range(total.stages):
                    total.begin(stage)
                    schedule.at(f"m{stage}")
                    total.finish(stage)
                out["small_sum"][...] = terms[total.stages % 2]
                schedule.need("end", reduce, range(2 * CUTS, len(pieces)))
                save.wait()

            pl.run_scoped(
                input_phase, pltpu.VMEM((nz, nx, 2, depth, 3 * d), BF16), pltpu.VMEM((n, d), BF16)
            )

        pl.run_scoped(
            backward_phase,
            pltpu.VMEM((n, d), F32),
            pltpu.VMEM((n, d), BF16),
            pltpu.VMEM((n, d), BF16),
            pltpu.VMEM((n, d), BF16),
            pltpu.VMEM((n, 3 * d), BF16),
            pltpu.VMEM((n, d), BF16),
            pltpu.VMEM((3, nz, nx, 2, depth, d), BF16),
            pltpu.VMEM((4, nz, nx, depth, d), BF16),
        )

    exchanged = nz + nx
    results = pl.pallas_call(
        kernel,
        out_shape=list(outputs.values()) + list(small_outputs.values()),
        in_specs=[HBM, HBM] + [VMEM] * 6 + [HBM] * 4,
        out_specs=[HBM] * len(outputs) + [VMEM] * len(small_outputs),
        scratch_shapes=[
            pltpu.VMEM((8, n), jnp.int32),
            pltpu.VMEM((16, 128), F32),
            pltpu.VMEM((nz, nx, 2, 16, 128), BF16),
            pltpu.VMEM((CHUNKS * tiles, 8, tile), F32),
            pltpu.VMEM((8, d), F32),
            pltpu.VMEM((CHUNKS * tiles, 8, tile), F32),
            pltpu.VMEM((8, 3 * d), F32),
            pltpu.VMEM((2, small_rows, d), F32),
            pltpu.VMEM((partners, small_rows, d), F32),
            pltpu.SemaphoreType.REGULAR,
            *spares,
            *landing_scratch,
            *semaphores(40 * exchanged + 48, 16 * (max(nx, nz) // 2 + 2) + 56),
        ],
        compiler_params=pltpu.CompilerParams(
            collective_id=1, has_side_effects=True, vmem_limit_bytes=64 * MIB - 64 * 1024
        ),
        name="block",
    )(tokens, cotangent, ids, *small, w_qkv, w_out, in_shard, hidden_own)
    return dict(zip(names, results))


PARTS = 4


def result_kernel(nz, nx, block, running_load, share, hidden_share):
    devices = nz * nx * 2
    n, d = block["block_out"].shape
    depth, width = block["in_sum"].shape[2:]
    lines = width // d

    def kernel(
        block_hbm, input_hbm, qkv_ref, wo_ref, in_ref, hidden_ref, small_ref, counts_ref, load_ref,
        block_out, input_grad, gain, shift, qkv, attn_bias, wo, in_grad, in_bias, hidden, out_bias, counts, loads,
        block_buffer, input_buffer, here,
    ):
        copies = []
        for i in range(2 * PARTS):
            source, buffer, target = ((block_hbm, block_buffer, block_out), (input_hbm, input_buffer, input_grad))[i % 2]
            rows = pl.ds(i // 2 * (n // PARTS), n // PARTS)
            copies.append(
                (
                    pltpu.make_async_copy(source.at[rows], buffer.at[rows], here.at[2 * i]),
                    pltpu.make_async_copy(buffer.at[rows], target.at[rows], here.at[2 * i + 1]),
                )
            )
        for copy in copies:
            copy[0].start()
        for copy in copies:
            copy[0].wait()
            copy[1].start()
        core = lax.axis_index("core")
        chip = lax.axis_index("dp") * nx + lax.axis_index("xy")
        first = (chip * 2 + core) * share
        own = pltpu.roll(small_ref[...], lax.rem(d - first, d), axis=1)
        gain[...] = own[0:2, :share]
        shift[...] = own[2:4, :share]
        attn_bias[...] = own[4:7, :share]
        out_bias[...] = own[8:10, :share]
        cut = hidden_share // CUTS
        first = chip * cut
        rows = lax.broadcasted_iota(jnp.int32, small_ref.shape, 0)
        for expert in range(EXPERTS):
            for k in range(CUTS):
                start = k * (width // CUTS)
                row = 10 + (expert * CHUNKS + core) * lines + start // d
                line = jnp.sum(jnp.where(rows == row, small_ref[...], 0.0), axis=0, keepdims=True)
                line = pltpu.roll(jnp.broadcast_to(line, (8, d)), lax.rem(2 * d - start % d - first, d), axis=1)
                in_bias[expert : expert + 1, k * cut : (k + 1) * cut] = line[0:1, :cut]
        qkv[...] = qkv_ref[...].astype(F32)
        wo[...] = wo_ref[...].astype(F32)
        hidden[...] = hidden_ref[...].astype(F32)
        join_columns(in_ref, in_grad, hidden_share)
        lane = lax.broadcasted_iota(jnp.int32, (1, 128), 1)
        digits = counts_ref[0:1, :]
        second = jnp.sum(jnp.where(lane == 0, digits * 32, jnp.where(lane == 1, digits, 0.0)))
        for expert, count in enumerate((n * devices - second, second)):
            counts[expert] = count.astype(jnp.int32)
            loads[expert] = 0.9 * load_ref[expert] + 0.1 * (count * (EXPERTS / (n * devices)))
        for copy in copies:
            copy[1].wait()

    def f32(*shape):
        return jax.ShapeDtypeStruct(shape, F32)

    scalars = pl.BlockSpec(memory_space=pltpu.SMEM)
    return pl.pallas_call(
        kernel,
        out_shape=[
            jax.ShapeDtypeStruct((n, d), BF16),
            f32(n, d),
            f32(2, share),
            f32(2, share),
            f32(depth, 3 * d),
            f32(3, share),
            f32(depth, d),
            f32(EXPERTS, depth, CHUNKS * width),
            f32(EXPERTS, hidden_share),
            f32(EXPERTS, hidden_share, d),
            f32(EXPERTS, share),
            jax.ShapeDtypeStruct((EXPERTS,), jnp.int32),
            f32(EXPERTS),
        ],
        in_specs=[HBM] * 2 + [VMEM] * 6 + [scalars],
        out_specs=[HBM] * 2 + [VMEM] * 9 + [scalars] * 2,
        scratch_shapes=[
            pltpu.VMEM((n, d), BF16),
            pltpu.VMEM((n, d), F32),
            pltpu.SemaphoreType.DMA((4 * PARTS,)),
        ],
        compiler_params=pltpu.CompilerParams(vmem_limit_bytes=60 * MIB),
        name="results",
    )(
        block["block_out"], block["input_grad"], block["qkv_sum"], block["wo_sum"], block["in_sum"], block["hidden_sum"],
        block["small_sum"], block["counts"], running_load,
    )


def shards(
    nz, nx, tokens, norm_gain, norm_bias, w_qkv, attn_bias, w_attn_out, expert_in, expert_in_bias, expert_out,
    expert_out_bias, expert_ids, running_load, cotangent,
):
    chips = nz * nx
    depth, width = expert_in.shape[1:]
    share, hidden_share = norm_gain.shape[1], expert_out.shape[1]

    tiled = (EXPERTS, depth, CHUNKS, CUTS, chips, hidden_share // CUTS)
    if not whole_tiles(hidden_share):
        expert_in = expert_in.reshape(EXPERTS, depth, chips, CHUNKS, CUTS, -1).transpose(0, 1, 3, 4, 2, 5)
        expert_in = expert_in.reshape(EXPERTS, depth, width)
    small = (norm_gain, norm_bias, attn_bias, expert_out_bias, expert_in_bias)
    ids = expert_ids.reshape(1, tokens.shape[0])
    block = block_kernel(nz, nx, tokens, cotangent, ids, small, w_qkv, w_attn_out, expert_in, expert_out)
    results = list(result_kernel(nz, nx, block, running_load, share, hidden_share))
    if not whole_tiles(hidden_share):
        in_grad = results[7].reshape(tiled).transpose(0, 1, 4, 2, 3, 5)
        results[7] = in_grad.reshape(EXPERTS, depth, width)
    return tuple(results)


def solution(mesh):
    nz, nx = mesh.shape["dp"], mesh.shape["fsdp"] // 2
    fine = Mesh(mesh.devices.reshape(nz, nx, 2), ("dp", "xy", "core"))
    every = ("dp", "xy", "core")
    row, column, middle = P(every, None), P(None, every), P(None, every, None)
    return jax.shard_map(
        functools.partial(shards, nz, nx),
        mesh=fine,
        in_specs=(
            row, column, column, row, column, row, middle, column, middle, column, row, P(), row,
        ),
        out_specs=(row, row, column, column, row, column, row, middle, column, middle, column, P(), P()),
        check_vma=False,
    )
```

```python
import functools
import math

import jax
import jax.numpy as jnp
from jax import lax
from jax.experimental import pallas as pl
from jax.experimental.pallas import tpu as pltpu
from jax.sharding import Mesh, PartitionSpec as P

BF16 = jnp.bfloat16
F32 = jnp.float32
MESH_ID = pl.DeviceIdType.MESH

HEAD = 64
MOST = 640
EXPERTS = 2
CHUNKS = 2
CUTS = 4
AHEAD = 1
NORM_EPS = 1e-05
SCORE_SCALE = 0.125
SCALE_LOG2 = SCORE_SCALE * math.log2(math.e)
MASKED = -1e30
BLOCK = 256
MIB = 1 << 20
ALL = slice(None)
HBM = pl.BlockSpec(memory_space=pl.ANY)
VMEM = pl.BlockSpec(memory_space=pltpu.VMEM)


def dot(left, right):
    return lax.dot_general(left, right, (((1,), (0,)), ((), ())), preferred_element_type=F32)


def dot_last(left, right):
    return lax.dot_general(left, right, (((1,), (1,)), ((), ())), preferred_element_type=F32)


def row_stats(values):
    center = values - jnp.mean(values, axis=-1, keepdims=True)
    spread = jnp.mean(center * center, axis=-1, keepdims=True)
    inverse = lax.rsqrt(spread + NORM_EPS)
    return center * inverse, inverse


def as_rows(values, rows):
    if values.dtype == BF16 and values.shape[-2] % 16:
        return values.astype(F32).reshape(rows, values.shape[-1]).astype(BF16)
    return values.reshape(rows, values.shape[-1])


def split_rows(values, shape):
    if values.dtype == BF16 and shape[-2] % 16:
        return values.astype(F32).reshape(shape).astype(BF16)
    return values.reshape(shape)


class Place:
    def __init__(self, nz, nx):
        self.nz, self.nx = nz, nx
        self.bits_z, self.bits_x = nz.bit_length() - 1, nx.bit_length() - 1
        self.z, self.xy, self.core = lax.axis_index("dp"), lax.axis_index("xy"), lax.axis_index("core")
        self.flip_z = [(1 - 2 * lax.rem(lax.div(self.z, 2**k), 2)) * 2**k for k in range(self.bits_z)]
        self.flip_x = [(1 - 2 * lax.rem(lax.div(self.xy, 2**k), 2)) * 2**k for k in range(self.bits_x)]

    def step_x(self, k, core=None):
        core = self.core if core is None else core
        return (1 - core) * self.flip_x[k] + core * self.flip_x[self.bits_x - 1 - k]

    def span_x(self, which, core=None):
        return self.xy + sum(self.step_x(k, core) for k in range(self.bits_x) if which >> k & 1)

    def span_z(self, which):
        return self.z + sum(self.flip_z[k] for k in range(self.bits_z) if which >> k & 1)

    def partners(self):
        found = [(self.z + flip, self.xy, self.core) for flip in self.flip_z]
        found += [(self.z, self.xy + flip, self.core) for flip in self.flip_x]
        return found + [self.sibling()]

    def sibling(self):
        return (self.z, self.xy, 1 - self.core)

    def barrier(self):
        semaphore = pltpu.get_barrier_semaphore()
        partners = self.partners()
        for partner in partners:
            pl.semaphore_signal(semaphore, inc=1, device_id=partner, device_id_type=MESH_ID)
        pl.semaphore_wait(semaphore, len(partners))


class Copies:
    def __init__(self, send, recv, near):
        self.send, self.recv, self.near = send, recv, near
        self.far_names, self.near_names = {}, {}

    def far(self, name, src, dst, device):
        i = self.far_names.setdefault(name, len(self.far_names))
        return pltpu.make_async_remote_copy(
            src_ref=src, dst_ref=dst, send_sem=self.send.at[i], recv_sem=self.recv.at[i],
            device_id=device, device_id_type=MESH_ID,
        )

    def local(self, name, src, dst, slot=None):
        if slot is not None:
            self.near_names.setdefault((name, 0), len(self.near_names))
            self.near_names.setdefault((name, 1), len(self.near_names))
            return pltpu.make_async_copy(src, dst, self.near.at[self.near_names[name, 0] + slot])
        i = self.near_names.setdefault(name, len(self.near_names))
        return pltpu.make_async_copy(src, dst, self.near.at[i])


def semaphores(far, near):
    return [
        pltpu.SemaphoreType.DMA((far,)),
        pltpu.SemaphoreType.DMA((far,)),
        pltpu.SemaphoreType.DMA((near,)),
    ]


class Stream:
    def __init__(self, pieces):
        self.pieces = pieces
        self.begun = {}

    def advance(self, piece, stage):
        if stage > 0:
            self.finish(piece, stage - 1)
        self.begin(piece, stage)
        self.begun[piece] = stage

    def last(self, piece):
        return self.stages(self.pieces[piece]) - 1


class Schedule:
    def __init__(self, place):
        self.plan = PLAN if (place.nz, place.nx) == PLAN_MESH else None
        self.streams = {}

    def at(self, point):
        for item in (self.plan or {}).get(point, ()):
            self.streams[item // 1000].advance(item % 1000 // 10, item % 10)

    def in_loop(self, i, name, count):
        for k in range(count):
            if (self.plan or {}).get(f"{name}{k}"):
                @pl.when(i == k)
                def _(k=k):
                    self.at(f"{name}{k}")

    def need(self, point, stream, pieces):
        self.at(point)
        if self.plan is None:
            most = max(stream.last(piece) for piece in pieces)
            for now in range(len(pieces) + most):
                for stage in range(most, -1, -1):
                    if 0 <= now - stage < len(pieces):
                        piece = pieces[now - stage]
                        if stream.begun.get(piece, -1) < stage <= stream.last(piece):
                            stream.advance(piece, stage)
        for piece in pieces:
            stream.finish(piece, stream.last(piece))

    def force(self, stream, piece, stage):
        if self.plan is None:
            for now in range(stream.begun.get(piece, -1) + 1, stage + 1):
                stream.advance(piece, now)


class Gather(Stream):
    def __init__(self, name, place, copies, pieces):
        super().__init__(pieces)
        self.name, self.place, self.made = name, place, copies

    def stages(self, piece):
        return self.place.bits_z + self.place.bits_x + (piece[2] is not None)

    def copies(self, piece, stage):
        place = self.place
        order, region, to_sibling = self.pieces[piece]
        step_z = stage if order == "z" else stage - place.bits_x
        step_x = stage - place.bits_z if order == "z" else stage
        found = []
        if stage == place.bits_z + place.bits_x:
            found += [(ref, place.sibling()) for ref in to_sibling]
        elif 0 <= step_z < place.bits_z:
            bit = place.bits_z - 1 - step_z
            device = (place.z + place.flip_z[bit], place.xy, place.core)
            for held in range(2**step_z):
                held_xy = place.xy if order == "z" else ALL
                found += [(ref, device) for ref in region(place.span_z(held << (bit + 1)), held_xy)]
        else:
            device = (place.z, place.xy + place.step_x(step_x), place.core)
            for held in range(2**step_x):
                held_z = ALL if order == "z" else place.z
                found += [(ref, device) for ref in region(held_z, place.span_x(held))]
        return [
            self.made.far((self.name, piece, stage, i), ref, ref, device) for i, (ref, device) in enumerate(found)
        ]

    def begin(self, piece, stage):
        for copy in self.copies(piece, stage):
            copy.start()

    def finish(self, piece, stage):
        for copy in self.copies(piece, stage):
            copy.wait()


def add_up(total, landed):
    if len(total.shape) > 3:
        @pl.loop(0, total.shape[0])
        def _(i):
            add_up(total.at[i], landed.at[i])
    else:
        total[...] = (total[...].astype(F32) + landed[...].astype(F32)).astype(BF16)


class Reduce(Stream):
    def __init__(self, name, place, copies, pieces):
        super().__init__(pieces)
        self.name, self.place, self.made = name, place, copies

    def stages(self, piece):
        return self.place.bits_z + self.place.bits_x + 1

    def plan(self, piece, stage):
        place = self.place
        nx, bits_x, bits_z = place.nx, place.bits_x, place.bits_z
        pair = isinstance(self.pieces[piece], PairPiece)
        if pair:
            order, landing, acc = self.pieces[piece].order, self.pieces[piece].landing, self.pieces[piece].acc
            first, landed = False, landing[stage - 1]
            step = stage - 1
        else:
            order, landing, spare, source, _, _ = self.pieces[piece]
            acc, first, landed, step = landing[0], stage == 0, landing[stage], stage
        far, near, sums = [], [], []
        step_x = step if order == "z" else step - bits_z
        step_z = step - bits_x if order == "z" else step
        if 0 <= step_x < bits_x:
            k = bits_x - 1 - step_x
            device = (place.z, place.xy + place.step_x(k), place.core)
            for j in range(2**k):
                if first:
                    far.append((source(ALL, place.span_x(2**k + j)), acc.at[j], device))
                    near.append((source(ALL, place.span_x(j)), spare.at[j]))
                    sums.append((acc.at[j], spare.at[j]))
                elif order == "x":
                    at_z = place.z if pair else 0
                    far.append((acc.at[at_z, place.span_x(2**k + j)], landed.at[j], device))
                    sums.append((acc.at[at_z, place.span_x(j)], landed.at[j]))
                elif pair:
                    far.append((acc.at[:, place.span_x(2**k + j)], landed.at[j], device))
                    sums += [(acc.at[i, place.span_x(j)], landed.at[j, i]) for i in range(place.nz)]
                else:
                    far.append((acc.at[2**k + j], landed.at[j], device))
                    sums.append((acc.at[j], landed.at[j]))
        else:
            bit = step_z
            device = (place.z + place.flip_z[bit], place.xy, place.core)
            for s in range(2 ** (bits_z - 1 - bit)):
                upper = s << (bit + 1)
                if first:
                    far.append((source(place.span_z(upper + 1), ALL), acc.at[s], device))
                    near.append((source(place.span_z(upper), ALL), spare.at[s]))
                    sums.append((acc.at[s], spare.at[s]))
                elif order == "z":
                    at_xy = place.xy if pair else None
                    send, keep = place.span_z(upper + 2**bit), place.span_z(upper)
                    far.append((acc.at[send, at_xy] if pair else acc.at[0, send], landed.at[s], device))
                    sums.append((acc.at[keep, at_xy] if pair else acc.at[0, keep], landed.at[s]))
                else:
                    send = place.span_z(upper + 2**bit) if pair else (upper + 2**bit) // 2
                    keep = place.span_z(upper) if pair else upper // 2
                    far.append((acc.at[send], landed.at[s], device))
                    sums.append((acc.at[keep], landed.at[s]))
        return far, near, sums

    def made_copies(self, piece, stage, far, near):
        made = [
            self.made.far((self.name, piece, stage, i), src, dst, device) for i, (src, dst, device) in enumerate(far)
        ]
        return made + [self.made.local((self.name, piece, stage, i), src, dst) for i, (src, dst) in enumerate(near)]

    def deliver(self, piece, begin):
        place, core = self.place, self.place.core
        order, landing, _, _, target, owner = self.pieces[piece]
        mine = landing[0].at[0, place.z if order == "z" else place.xy]
        name = (self.name, piece, "last")

        def there(part):
            return self.made.far(name, part, target(core), place.sibling())

        def here(part):
            return self.made.local(name, part, target(core))

        if owner == "both":
            for copy in (there(mine.at[1 - core]), here(mine.at[core])):
                copy.start() if begin else copy.wait()
            return

        @pl.when(core == owner)
        def _():
            if begin:
                here(mine).start()
            else:
                here(mine).wait()
                there(mine).wait_recv()

        @pl.when(core != owner)
        def _():
            there(mine).start() if begin else there(mine).wait_send()

    def to_pair(self, piece):
        item, place = self.pieces[piece], self.place
        return self.made.far((self.name, piece, "pair"), item.source(1 - place.core), item.landed, place.sibling())

    def begin(self, piece, stage):
        pair = isinstance(self.pieces[piece], PairPiece)
        if pair and stage == 0:
            self.to_pair(piece).start()
            return
        if not pair and stage == self.stages(self.pieces[piece]) - 1:
            self.deliver(piece, True)
            return
        far, near, _ = self.plan(piece, stage)
        for copy in self.made_copies(piece, stage, far, near):
            copy.start()

    def finish(self, piece, stage):
        item, final = self.pieces[piece], stage == self.stages(self.pieces[piece]) - 1
        pair = isinstance(item, PairPiece)
        if pair and stage == 0:
            self.to_pair(piece).wait()
            here = self.made.local((self.name, piece, "pair"), item.landed, item.acc)
            here.start()
            here.wait()
            add_up(item.acc, item.source(self.place.core))
            return
        if final and not pair:
            self.deliver(piece, False)
            return
        far, near, sums = self.plan(piece, stage)
        for copy in self.made_copies(piece, stage, far, near):
            copy.wait()
        for total, landed in sums:
            add_up(total, landed)
        if final:
            here = self.made.local((self.name, piece, "last"), item.acc.at[self.place.z, self.place.xy], item.target)
            here.start()
            here.wait()


class PairPiece:
    def __init__(self, order, source, landed, acc, landing, target):
        self.order, self.source, self.landed, self.acc = order, source, landed, acc
        self.landing, self.target = landing, target


def landing_shapes(nz, nx, tail, order):
    bits_z, bits_x = nz.bit_length() - 1, nx.bit_length() - 1
    if order == "z":
        return [(2**k, nz) + tail for k in reversed(range(bits_x))] + [
            (2 ** (bits_z - 1 - bit),) + tail for bit in range(bits_z)
        ]
    return [(2 ** (bits_z - 1 - bit), nx) + tail for bit in range(bits_z)] + [
        (2**k,) + tail for k in reversed(range(bits_x))
    ]


class Total:
    def __init__(self, place, copies, terms, landing):
        self.place, self.made, self.terms, self.landing = place, copies, terms, landing
        self.stages = len(place.partners())

    def copy(self, stage):
        device = self.place.partners()[stage]
        return self.made.far(("total", stage), self.terms.at[stage % 2], self.landing.at[stage], device)

    def begin(self, stage):
        self.copy(stage).start()

    def finish(self, stage):
        self.copy(stage).wait()
        self.terms[(stage + 1) % 2] = self.terms[stage % 2] + self.landing[stage]


def one_hot(slots, count):
    rows = lax.broadcasted_iota(jnp.int32, (count, slots.shape[1]), 0)
    return jnp.where(rows == slots, 1.0, 0.0).astype(BF16)


def pick_rows(picked, slots, values):
    picked[...] = dot(one_hot(slots, picked.shape[0]), values).astype(BF16)


def find_slots(slots, ids_ref, core):
    n = ids_ref.shape[1]
    ids = ids_ref[...]
    second = jnp.where(ids == 1, 1.0, 0.0)
    earlier = lax.broadcasted_iota(jnp.int32, (n, n), 0) <= lax.broadcasted_iota(jnp.int32, (n, n), 1)
    before = dot(
        jnp.broadcast_to(second, (16, n)).astype(BF16), jnp.where(earlier, 1.0, 0.0).astype(BF16)
    )[0:1].astype(jnp.int32)
    rank = jnp.where(ids == 1, before - 1, lax.broadcasted_iota(jnp.int32, (1, n), 1) - before)
    own = ids == core
    slots[0:1, :] = jnp.where(own, rank, -1)
    slots[1:2, :] = jnp.where(own, -1, rank)
    slots[2:8, :] = jnp.full((6, n), -1, jnp.int32)
    return jnp.sum(second, axis=1, keepdims=True)


GAIN, SHIFT, ATTN_BIAS, OUT_BIAS, IN_BIAS, DIGITS = 0, 2, 4, 7, 9, 11


def pack_small(small, refs, count_second):
    small[...] = jnp.zeros_like(small)
    for row, ref in zip((GAIN, SHIFT, ATTN_BIAS, OUT_BIAS, IN_BIAS), refs):
        count, share = ref.shape
        small[row : row + count, :share] = ref[...].astype(F32)
    high = jnp.floor(count_second * (1 / 32))
    lane = lax.broadcasted_iota(jnp.int32, (1, 128), 1)
    small[DIGITS : DIGITS + 1, :] = jnp.where(lane == 0, high, jnp.where(lane == 1, count_second - 32 * high, 0.0))


def spread(shares, length, share, place_of, first=0):
    devices = shares.shape[0]
    lanes = lax.broadcasted_iota(jnp.int32, (128, length), 1)
    chosen = lax.rem(lanes, share) + first == lax.broadcasted_iota(jnp.int32, (128, length), 0)
    repeat = jnp.where(chosen, 1.0, 0.0)
    copies = dot(shares, repeat.astype(BF16))
    lanes = lax.broadcasted_iota(jnp.int32, (devices, length), 1)
    device = lax.broadcasted_iota(jnp.int32, (devices, length), 0)
    return jnp.sum(jnp.where(lax.div(lanes, share) == place_of(device), copies, 0.0), axis=0, keepdims=True)


def unpack_small(small_full, core, d, share, hidden_share, vectors, in_bias, out_bias, counts):
    nz, nx = small_full.shape[:2]
    devices = nz * nx * 2
    found = small_full[...].astype(F32).reshape(devices, 16, 128)

    def rows(row):
        return found[:, row, :].astype(BF16)

    def vector(shares):
        return spread(shares, d, share, lambda device: device)

    vectors[...] = jnp.zeros_like(vectors)
    for line, row, part in (
        (0, GAIN, 0), (0, GAIN + 1, 1), (0, ATTN_BIAS + 2, 2), (1, SHIFT, 0), (1, SHIFT + 1, 1),
        (2, ATTN_BIAS, 0), (2, ATTN_BIAS + 1, 2),
    ):
        vectors[line : line + 1, part * d : (part + 1) * d] = vector(rows(row))

    def of_expert(row):
        return jnp.where(core == 0, rows(row), rows(row + 1))

    out_bias[0:1, :] = vector(of_expert(OUT_BIAS))
    cut = hidden_share // CUTS
    for chunk in range(CHUNKS):
        for i in range(CUTS):
            in_bias[chunk * CUTS + i, 0:1, :] = spread(
                of_expert(IN_BIAS), in_bias.shape[2], cut,
                lambda device: jnp.where(lax.rem(device, 2) == chunk, lax.div(device, 2), -1), i * cut,
            )
    counts[...] = jnp.broadcast_to(jnp.sum(found[:, DIGITS, :], axis=0, keepdims=True), counts.shape)


def attend_pair(qkv, head, attended, log_total):
    n, d = attended.shape
    low = lax.broadcasted_iota(jnp.int32, (n, 128), 1) < HEAD
    one, zero = jnp.ones((), BF16), jnp.zeros((), BF16)
    query = qkv[:, pl.ds(pl.multiple_of(head * 128, 128), 128)]
    key = qkv[:, pl.ds(pl.multiple_of(d + head * 128, 128), 128)]
    value = qkv[:, pl.ds(pl.multiple_of(2 * d + head * 128, 128), 128)]
    values = [jnp.where(low, value, one), jnp.where(low, one, value)]
    queries = [jnp.where(low, query, zero), jnp.where(low, zero, query)]
    low = low[:BLOCK]
    allowed = lax.broadcasted_iota(jnp.int32, (BLOCK, BLOCK), 1) <= lax.broadcasted_iota(
        jnp.int32, (BLOCK, BLOCK), 0
    )
    for i in range(n // BLOCK):
        first, end = i * BLOCK, (i + 1) * BLOCK
        found = []
        for j in range(2):
            near = jnp.where(allowed, dot_last(queries[j][first:end], key[first:end]), MASKED)
            top = jnp.max(near, axis=-1, keepdims=True)
            if i:
                far = dot_last(queries[j][first:end], key[:first])
                top = jnp.maximum(top, jnp.max(far, axis=-1, keepdims=True))
            top = top * SCALE_LOG2
            out = dot(jnp.exp2(near * SCALE_LOG2 - top).astype(BF16), values[j][first:end])
            if i:
                out = out + dot(jnp.exp2(far * SCALE_LOG2 - top).astype(BF16), values[j][:first])
            found.append((out, top))
        (out_a, top_a), (out_b, top_b) = found
        total = pltpu.roll(jnp.where(low, out_b, out_a), HEAD, axis=1)
        attended[first:end, pl.ds(pl.multiple_of(head * 128, 128), 128)] = (
            jnp.where(low, out_a, out_b) / total
        ).astype(BF16)
        logs = (jnp.where(low, top_a, top_b) + jnp.log2(total)).T
        log_total[head, 0:1, first:end] = logs[0:1]
        log_total[head, 1:2, first:end] = logs[HEAD : HEAD + 1]


def gelu_and_slope(values):
    root = math.sqrt(2 / math.pi)
    cube = 0.044715
    square = values * values
    bent = jnp.tanh(values * (root + root * cube * square))
    half = 0.5 * (1 + bent)
    slope = half + 0.5 * values * (1 - bent * bent) * (root + 3 * root * cube * square)
    return values * half, slope


def norm_backward(values, gain, grad):
    scaled, inverse = row_stats(values)
    grad_scaled = grad * gain
    mean = jnp.mean(grad_scaled, axis=-1, keepdims=True)
    along = jnp.mean(grad_scaled * scaled, axis=-1, keepdims=True)
    term = inverse * (grad_scaled - mean - scaled * along)
    return term, jnp.sum(grad * scaled, axis=0, keepdims=True), jnp.sum(grad, axis=0, keepdims=True)


def attend_pair_backward(qkv, head, attended, grad, log_total, projected, turned):
    n, d = attended.shape
    low = lax.broadcasted_iota(jnp.int32, (n, 128), 1) < HEAD
    zero = jnp.zeros((), BF16)

    def columns(part):
        return pl.ds(pl.multiple_of(part * d + head * 128, 128), 128)

    query, key, value = (qkv[:, columns(part)] for part in range(3))
    grad = grad[:, columns(0)]
    product = (attended[:, columns(0)].astype(F32) * grad.astype(F32)).T
    inner = [jnp.sum(product[j * HEAD : (j + 1) * HEAD], axis=0, keepdims=True) for j in range(2)]
    logs = [log_total[head, j : j + 1, :] for j in range(2)]
    key_turned = key.T
    keys = [jnp.where(low, key, zero), jnp.where(low, zero, key)]
    values = [jnp.where(low, value, zero), jnp.where(low, zero, value)]
    low = low[:BLOCK]
    allowed = lax.broadcasted_iota(jnp.int32, (BLOCK, BLOCK), 0) <= lax.broadcasted_iota(
        jnp.int32, (BLOCK, BLOCK), 1
    )
    for i in range(n // BLOCK):
        first, end = i * BLOCK, (i + 1) * BLOCK
        found = []
        for j in range(2):
            grad_key = grad_value = 0.0
            for start, stop in ((first, end), (end, n)):
                if start == stop:
                    continue
                scores = dot_last(keys[j][first:end], query[start:stop])
                weights = jnp.exp2(scores * SCALE_LOG2 - logs[j][:, start:stop])
                if start == first:
                    weights = jnp.where(allowed, weights, 0.0)
                grad_weights = dot_last(values[j][first:end], grad[start:stop])
                grad_scores = (weights * (grad_weights - inner[j][:, start:stop])).astype(BF16)
                grad_value = grad_value + dot(weights.astype(BF16), grad[start:stop])
                grad_key = grad_key + dot(grad_scores, query[start:stop])
                part = dot(key_turned[j * HEAD : (j + 1) * HEAD, first:end], grad_scores)
                if i == 0:
                    turned[j * HEAD : (j + 1) * HEAD, start:stop] = part
                else:
                    turned[j * HEAD : (j + 1) * HEAD, start:stop] += part
            found.append((grad_key, grad_value))
        (key_a, value_a), (key_b, value_b) = found
        projected[first:end, columns(1)] = (jnp.where(low, key_a, key_b) * SCORE_SCALE).astype(BF16)
        projected[first:end, columns(2)] = jnp.where(low, value_a, value_b).astype(BF16)
    projected[:, columns(0)] = (turned[...].T * SCORE_SCALE).astype(BF16)


PLAN_MESH = (4, 4)
GATHER_ACROSS = (7, 9, 15, 17)
REDUCE_ACROSS = (7, 8, 14, 16)
PLAN = {
    "s0": (0, 10,),
    "s1": (20, 90, 70, 170, 150,),
    "s2": (30,),
    "s3": (40,),
    "w0": (91, 71, 171, 151, 1, 80, 11, 21, 31, 2, 41, 12, 81, 3, 50, 60, 22, 100, 32, 42, 92, 82, 4, 13, 23, 51, 61,),
    "q0.0": (33, 101, 93,),
    "q0.3": (43,),
    "w1": (14, 24, 83, 110, 120,),
    "q1.0": (72,),
    "q1.1": (52,),
    "q1.3": (34, 62,),
    "q2.1": (102,),
    "h0": (111, 121,),
    "h1": (160,),
    "h2": (53, 63, 130, 140,),
    "h3": (73,),
    "h4": (103,),
    "h5": (112,),
    "h6": (122, 161,),
    "h7": (131, 141,),
    "o0": (180,),
    "o1": (172,),
    "o2": (113, 123,),
    "d1": (162, 181,),
    "e0": (132, 142, 190, 152,),
    "t0.0": (182,),
    "t0.1": (163, 133, 173,),
    "t2.1": (143,),
    "t0.2": (191,),
    "t1.2": (183, 153,),
    "t2.2": (1000,),
    "t1.3": (192,),
    "t2.3": (1040,),
    "t1.4": (1070,),
    "t2.4": (1001, 1010,),
    "t0.5": (193,),
    "t1.5": (1080,),
    "t2.5": (1041,),
    "t0.6": (1050,),
    "t1.6": (1002, 1011,),
    "e7": (1020, 1071,),
    "t1.7": (1003,),
    "t2.7": (1042, 1012, 1051, 1021, 1060,),
    "x": (1081,),
    "b0": (1004, 1030, 1072, 1043,),
    "b1": (1013, 1061, 1120,),
    "b2": (1052, 1022, 1073,),
    "b3": (1044, 1031, 1082, 1090, 1014, 1140,),
    "wo2": (1074, 1190,),
    "a0": (1053, 1023, 1083, 1121, 1130,),
    "a1": (1062, 1032, 1091, 1084, 1100, 1141,),
    "a2": (1054, 1024,),
    "a3": (1131, 1063, 1150,),
    "a4": (1033, 1101, 1122, 1110,),
    "a5": (1064, 1092,),
    "a6": (1034, 1123, 1132, 1142, 1093, 1151,),
    "a7": (1102, 1143, 1111,),
    "p0": (1160, 1124, 1094, 1133, 1144, 1152,),
    "p1": (1170, 1161, 1191,),
    "p2": (1171, 1180, 1134,),
    "i0": (1103,),
    "i1": (1181, 1192, 1112, 1153,),
    "i2": (1104, 1162, 1172,),
    "m0": (1154,),
    "m1": (1182, 1193, 1173,),
    "m2": (1113,),
    "m3": (1163, 1183,),
    "m4": (1174, 1194,),
    "end": (1164, 1114, 1184,),
}


def gathered_columns(pieces):
    found, at = None, 0
    for values, first, lanes in pieces:
        moved = pltpu.roll(values, (at - first) % 128, axis=values.ndim - 1) if at != first else values
        lane = lax.broadcasted_iota(jnp.int32, values.shape, values.ndim - 1)
        found = moved if found is None else jnp.where(lane >= at, moved, found)
        at += lanes
    return found


def whole_tiles(hidden_share):
    return hidden_share % 128 == 0


def split_columns(whole, parts, hidden_share):
    width = parts.shape[-1]
    cut = hidden_share // CUTS
    if not whole_tiles(hidden_share):
        for chunk in range(CHUNKS):
            parts[chunk] = whole[:, :, chunk * width : (chunk + 1) * width]
        return
    for expert in range(whole.shape[0]):
        for at in range(0, CHUNKS * width, 128):
            chunk, k, chip = at // width, at % width // (width // CUTS), at % (width // CUTS) // cut
            pieces = []
            for i in range(128 // cut):
                first = ((chip + i) * CHUNKS + chunk) * hidden_share + k * cut
                block = whole[expert, :, first // 128 * 128 : first // 128 * 128 + 128].astype(F32)
                pieces.append((block, first % 128, cut))
            parts[chunk, expert, :, at % width : at % width + 128] = gathered_columns(pieces).astype(BF16)


def join_columns(parts, whole, hidden_share):
    width = parts.shape[-1]
    cut = hidden_share // CUTS
    if not whole_tiles(hidden_share):
        for chunk in range(CHUNKS):
            whole[:, :, chunk * width : (chunk + 1) * width] = parts[chunk].astype(F32)
        return
    for expert in range(whole.shape[0]):
        for at in range(0, CHUNKS * width, 128):
            chip, chunk = at // hidden_share // CHUNKS, at // hidden_share % CHUNKS
            pieces = []
            for k in range(at % hidden_share // cut, at % hidden_share // cut + 128 // cut):
                first = k * (width // CUTS) + chip * cut
                block = parts[chunk, expert, :, first // 128 * 128 : first // 128 * 128 + 128].astype(F32)
                pieces.append((block, first % 128, cut))
            whole[expert, :, at : at + 128] = gathered_columns(pieces)


def block_kernel(nz, nx, tokens, cotangent, ids, small, w_qkv, w_out, in_shard, hidden_own):
    n, d = tokens.shape
    heads = d // 128
    depth = w_qkv.shape[0]
    share = small[0].shape[1]
    hidden_share = hidden_own.shape[1]
    width = in_shard.shape[2] // CHUNKS
    tile = width // CUTS
    tiles = CUTS
    count = 2 * MOST
    cut = width // CUTS
    hidden_cut = hidden_share // CUTS
    in_tail, hidden_tail = (2, depth, cut), (hidden_cut, d)
    small_rows = 10 + EXPERTS * CHUNKS * (width // d)
    small_rows += -small_rows % 8

    def bf16(*shape):
        return jax.ShapeDtypeStruct(shape, BF16)

    def f32(*shape):
        return jax.ShapeDtypeStruct(shape, F32)

    outputs = dict(
        block_out=bf16(n, d),
        input_grad=f32(n, d),
        qkv_sum=bf16(depth, 3 * d),
        wo_sum=bf16(depth, d),
        in_sum=bf16(CHUNKS, EXPERTS, depth, width),
        hidden_sum=bf16(EXPERTS, hidden_share, d),
        pair_terms=bf16(4, nz, nx, depth, d),
        qkv_full=bf16(nz, nx, 2, depth, 3 * d),
        wo_full=bf16(nz, nx, 2, depth, d),
        grad_rows=bf16(2, MOST, d),
        rows=bf16(2, MOST, d),
        made_rows=bf16(2, MOST, d),
        back_rows=bf16(2, MOST, d),
        in_full=bf16(CHUNKS, nz, nx, 2, depth, width),
        hidden_full=bf16(CHUNKS, nz, nx, hidden_share, d),
        in_terms=bf16(CHUNKS, nz, nx, 2, depth, width),
        hidden_terms=bf16(CHUNKS, nz, nx, hidden_share, d),
        normed=bf16(n, d),
        qkv=bf16(n, 3 * d),
        attended=bf16(n, d),
        logs=f32(heads, 8, n),
        residual=f32(n, d),
    )
    small_outputs = dict(small_sum=f32(small_rows, d), counts=f32(8, 128))

    gather_order = ["x" if piece in GATHER_ACROSS and nz == nx else "z" for piece in range(20)]
    reduce_order = ["x" if piece in REDUCE_ACROSS and nz == nx else "z" for piece in range(20)]
    landings = []
    for chunk in range(CHUNKS):
        for i in range(2 * CUTS):
            tail = in_tail if i < CUTS else hidden_tail
            landings.append(landing_shapes(nz, nx, tail, reduce_order[chunk * 2 * CUTS + i]))
    per_piece = len(landings[0])
    landing_scratch = [pltpu.VMEM(shape, BF16) for shapes in landings for shape in shapes]
    spares = [
        pltpu.VMEM(landing_shapes(nz, nx, tail, order)[0], BF16) for tail in (in_tail, hidden_tail) for order in "zx"
    ]
    partners = nz.bit_length() - 1 + nx.bit_length() - 1 + 1

    names = list(outputs) + list(small_outputs)

    def kernel(*refs):
        (
            tokens_hbm, cot_hbm, ids_ref, gain_ref, shift_ref, attn_bias_ref, out_bias_ref, in_bias_ref,
            qkv_own, wo_own, in_shard, hidden_own,
        ) = refs[:12]
        out = dict(zip(names, refs[12 : 12 + len(names)]))
        rest = refs[12 + len(names) :]
        slots, small_own, small_full, in_bias, out_bias, bias_sums, vectors, terms, terms_landing, free = rest[:10]
        spare = rest[10:14]
        landing = rest[14 : 14 + len(landing_scratch)]
        made = Copies(*rest[14 + len(landing_scratch) :])

        place = Place(nz, nx)
        z, xy, core = place.z, place.xy, place.core
        sums = terms.at[0]
        total = Total(place, made, terms, terms_landing)

        def columns_of(ref, part):
            return lambda zs, xs: [ref.at[zs, xs, core, :, pl.ds(part * d, d)]]

        def with_small(zs, xs):
            return [out["qkv_full"].at[zs, xs, core, :, pl.ds(0, d)], small_full.at[zs, xs, core]]

        regions = [with_small, columns_of(out["qkv_full"], 1), columns_of(out["qkv_full"], 2), columns_of(out["wo_full"], 0)]
        gathered = [(order, region, region(ALL, ALL)) for order, region in zip(gather_order, regions)]
        for chunk in range(CHUNKS):
            for i in range(CUTS):
                at_columns = pl.ds(i * cut, cut)
                gathered.append(
                    (gather_order[len(gathered)], lambda zs, xs, c=chunk, s=at_columns: [out["in_full"].at[c, zs, xs, :, :, s]], None)
                )
            for i in range(CUTS):
                at_rows = pl.ds(i * hidden_cut, hidden_cut)
                gathered.append(
                    (gather_order[len(gathered)], lambda zs, xs, c=chunk, s=at_rows: [out["hidden_full"].at[c, zs, xs, s]], None)
                )
        gather = Gather("gather", place, made, gathered)

        pieces = []
        for chunk in range(CHUNKS):
            for i in range(2 * CUTS):
                at = len(pieces)
                order = reduce_order[at]
                mine = landing[at * per_piece : (at + 1) * per_piece]
                spare_now = spare[i // CUTS * 2 + (order == "x")]
                if i < CUTS:
                    at_columns = pl.ds(i * cut, cut)
                    pieces.append(
                        (
                            order, mine, spare_now,
                            lambda zs, xs, c=chunk, s=at_columns: out["in_terms"].at[c, zs, xs, :, :, s],
                            lambda expert, c=chunk, s=at_columns: out["in_sum"].at[c, expert, :, s],
                            "both",
                        )
                    )
                else:
                    at_rows = pl.ds((i - CUTS) * hidden_cut, hidden_cut)
                    pieces.append(
                        (
                            order, mine, spare_now,
                            lambda zs, xs, c=chunk, s=at_rows: out["hidden_terms"].at[c, zs, xs, s],
                            lambda expert, s=at_rows: out["hidden_sum"].at[expert, s],
                            chunk,
                        )
                    )
        reduce = Reduce("reduce", place, made, pieces)
        schedule = Schedule(place)
        schedule.streams.update({0: gather, 1: reduce})

        def first_phase(cot, picked, shard, in_own, qkv, wo, hidden):
            def load(name, source, target):
                copy = made.local(("first", name), source, target)
                copy.start()
                return copy

            loads = [load("qkv", qkv_own, qkv), load("wo", wo_own, wo), load("hidden", hidden_own, hidden)]
            load_shard = load("shard", in_shard, shard)
            load_cot = load("cot", cot_hbm, cot)
            count_second = find_slots(slots, ids_ref, core)
            pack_small(small_own, (gain_ref, shift_ref, attn_bias_ref, out_bias_ref, in_bias_ref), count_second)
            small_full[z, xy, core] = small_own[...].astype(BF16)
            place.barrier()
            loads[0].wait()
            near = [load("own qkv", qkv, out["qkv_full"].at[z, xy, core])]
            loads[1].wait()
            near.append(load("own wo", wo, out["wo_full"].at[z, xy, core]))
            for copy in near:
                copy.wait()
            schedule.at("s0")
            loads[2].wait()
            late = [load("own hidden", hidden.at[core], out["hidden_full"].at[core, z, xy])]
            pair = [made.far("pair hidden", hidden.at[1 - core], out["hidden_full"].at[core, z, xy], place.sibling())]
            load_shard.wait()
            split_columns(shard, in_own, hidden_share)
            for chunk in range(CHUNKS):
                target = out["in_full"].at[chunk, z, xy, core]
                late.append(load(("own in", chunk), in_own.at[chunk, core], target))
                pair.append(made.far(("pair in", chunk), in_own.at[chunk, 1 - core], target, place.sibling()))
            for copy in pair:
                copy.start()
            for copy in late + pair:
                copy.wait()
            schedule.at("s1")
            load_cot.wait()
            pick_rows(picked.at[1], slots[1:2, :], cot[...])
            theirs = made.far("grad rows", picked.at[1], out["grad_rows"].at[1], place.sibling())
            theirs.start()
            schedule.at("s2")
            pick_rows(picked.at[0], slots[0:1, :], cot[...])
            mine = made.local("grad rows", picked.at[0], out["grad_rows"].at[0])
            mine.start()
            schedule.at("s3")
            mine.wait()
            theirs.wait()

        pl.run_scoped(
            first_phase,
            pltpu.VMEM((n, d), BF16),
            pltpu.VMEM((2, MOST, d), BF16),
            pltpu.VMEM((EXPERTS, depth, CHUNKS * width), BF16),
            pltpu.VMEM((CHUNKS, EXPERTS, depth, width), BF16),
            pltpu.VMEM((depth, 3 * d), BF16),
            pltpu.VMEM((depth, d), BF16),
            pltpu.VMEM((EXPERTS, hidden_share, d), BF16),
        )

        def forward_phase(tok, w, wo, normed, qkv, attended, logs, residual, normed_two, picked):
            load = made.local("tokens", tokens_hbm, tok)
            load.start()
            for part in range(3):
                schedule.need(f"w{part}", gather, [part])
                at_columns = pl.ds(part * d, d)
                load_w = made.local(
                    ("w", part), out["qkv_full"].at[:, :, :, :, at_columns], w.at[:, :, :, :, at_columns]
                )
                load_w.start()
                if part == 0:
                    unpack_small(
                        small_full, core, d, share, hidden_share, vectors, in_bias, out_bias, out["counts"]
                    )
                    load.wait()
                load_w.wait()

                @pl.loop(0, n // BLOCK)
                def _(i, part=part):
                    rows = pl.ds(pl.multiple_of(i * BLOCK, BLOCK), BLOCK)
                    if part == 0:
                        scaled, _ = row_stats(tok[rows].astype(F32))
                        normed[rows] = (scaled * vectors[0:1, :d] + vectors[1:2, :d]).astype(BF16)
                    columns = slice(part * d, (part + 1) * d)
                    weight = as_rows(w[:, :, :, :, columns], d)
                    qkv[rows, columns] = (dot(normed[rows], weight) + vectors[2:3, columns]).astype(BF16)
                    schedule.in_loop(i, f"q{part}.", n // BLOCK)

            saves = [
                made.local("save normed", normed, out["normed"]),
                made.local("save qkv", qkv, out["qkv"]),
            ]
            for save in saves:
                save.start()

            @pl.loop(0, heads)
            def _(head):
                attend_pair(qkv, head, attended, logs)
                schedule.in_loop(head, "h", heads)

            saves += [
                made.local("save attended", attended, out["attended"]),
                made.local("save logs", logs, out["logs"]),
            ]
            for save in saves[2:]:
                save.start()
            schedule.need("wo", gather, [3])
            load_wo = made.local("wo", out["wo_full"], wo)
            load_wo.start()
            load_wo.wait()

            @pl.loop(0, n // BLOCK)
            def _(i):
                rows = pl.ds(pl.multiple_of(i * BLOCK, BLOCK), BLOCK)
                added = dot(attended[rows], as_rows(wo[...], d)) + vectors[0:1, 2 * d :]
                residual[rows] = tok[rows].astype(F32) + added
                scaled, _ = row_stats(residual[rows])
                normed_two[rows] = (scaled * vectors[0:1, d : 2 * d] + vectors[1:2, d : 2 * d]).astype(BF16)
                schedule.in_loop(i, "o", n // BLOCK)


            saves.append(made.local("save residual", residual, out["residual"]))
            saves[-1].start()
            pick_rows(picked.at[1], slots[1:2, :], normed_two[...])
            theirs = made.far("rows", picked.at[1], out["rows"].at[1], place.sibling())
            theirs.start()
            schedule.at("d0")
            pick_rows(picked.at[0], slots[0:1, :], normed_two[...])
            saves.append(made.local("rows", picked.at[0], out["rows"].at[0]))
            saves[-1].start()
            schedule.at("d1")
            for save in saves:
                save.wait()
            theirs.wait()

        pl.run_scoped(
            forward_phase,
            pltpu.VMEM((n, d), BF16),
            pltpu.VMEM((nz, nx, 2, depth, 3 * d), BF16),
            pltpu.VMEM((nz, nx, 2, depth, d), BF16),
            pltpu.VMEM((n, d), BF16),
            pltpu.VMEM((n, 3 * d), BF16),
            pltpu.VMEM((n, d), BF16),
            pltpu.VMEM((heads, 8, n), F32),
            pltpu.VMEM((n, d), F32),
            pltpu.VMEM((n, d), BF16),
            pltpu.VMEM((2, MOST, d), BF16),
        )

        def expert_phase(rows, grads, turned, made_total, back_total, w_in, w_hidden, grad_in, grad_hidden):
            loads = [
                made.local("load rows", out["rows"], rows),
                made.local("load grads", out["grad_rows"], grads),
            ]
            for copy in loads:
                copy.start()

            def cut_rows(t):
                return pl.ds(pl.multiple_of(t * hidden_cut, hidden_cut), hidden_cut)

            def weights(step):
                slot, chunk, t = lax.rem(step, 2), lax.div(step, tiles), lax.rem(step, tiles)
                at_columns = pl.ds(pl.multiple_of(t * tile, tile), tile)
                return [
                    made.local("w in", out["in_full"].at[chunk, :, :, :, :, at_columns], w_in.at[slot]),
                    made.local("w hidden", out["hidden_full"].at[chunk, :, :, cut_rows(t)], w_hidden.at[slot]),
                ]

            def stores(step):
                chunk, t = lax.div(step, tiles), lax.rem(step, tiles)
                at_columns = pl.ds(pl.multiple_of(t * tile, tile), tile)
                return [
                    made.local("store in", grad_in, out["in_terms"].at[chunk, :, :, :, :, at_columns]),
                    made.local("store hidden", grad_hidden, out["hidden_terms"].at[chunk, :, :, cut_rows(t)]),
                ]

            terms[0] = jnp.zeros(terms.shape[1:], F32)
            made_total[...] = jnp.zeros_like(made_total)
            back_total[...] = jnp.zeros_like(back_total)
            for copy in loads:
                copy.wait()
            turned[...] = as_rows(rows[...], count).T
            line = jnp.sum(as_rows(grads[...], count).astype(F32), axis=0, keepdims=True)
            for expert in range(EXPERTS):
                sums[8 + expert : 9 + expert, :] = jnp.where(core == expert, line, 0.0)

            def arrive(step):
                chunk, t = step // tiles, step % tiles
                first = 4 + chunk * 2 * CUTS + t
                schedule.need(f"e{step}", gather, [first, first + CUTS])
                for copy in weights(step):
                    copy.start()

            arrive(0)

            @pl.loop(0, CHUNKS * tiles)
            def _(step):
                slot = lax.rem(step, 2)
                for copy in weights(step):
                    copy.wait()

                def beside(spot):
                    schedule.in_loop(step, f"t{spot}.", CHUNKS * tiles)

                rows_now, grads_now = as_rows(rows[...], count), as_rows(grads[...], count)
                w_in_now = as_rows(w_in[slot], d)
                w_hidden_now = as_rows(w_hidden[slot], tile)
                hidden_pre = dot(rows_now, w_in_now) + in_bias[step, 0:1, :]
                hidden, slope = gelu_and_slope(hidden_pre)
                hidden = hidden.astype(BF16)
                grad_pre = dot_last(grads_now, w_hidden_now) * slope
                bias_sums[step, 0:1, :] = jnp.sum(grad_pre, axis=0, keepdims=True)
                grad_pre = grad_pre.astype(BF16)
                beside(0)
                made_total[...] += dot(hidden, w_hidden_now)
                back_total[...] += dot_last(grad_pre, w_in_now)

                @pl.when(step >= 1)
                def _():
                    for copy in stores(step - 1):
                        copy.wait()

                beside(1)
                for k in range(1, CHUNKS * tiles):
                    @pl.when(step == k - 1)
                    def _(k=k):
                        arrive(k)

                grad_hidden[...] = split_rows(dot(hidden.T, grads_now).astype(BF16), (nz, nx, hidden_cut, d))
                grad_in[...] = split_rows(dot(turned[...], grad_pre).astype(BF16), (nz, nx, 2, depth, tile))
                for copy in stores(step):
                    copy.start()
                beside(2)

            for copy in stores(CHUNKS * tiles - 1):
                copy.wait()

            rows[...] = split_rows((made_total[...] + out_bias[0:1, :]).astype(BF16), (2, MOST, d))
            grads[...] = split_rows(back_total[...].astype(BF16), (2, MOST, d))
            results = []
            for name, source in (("made_rows", rows), ("back_rows", grads)):
                results.append(made.far(name, source.at[1], out[name].at[1], place.sibling()))
                results.append(made.local(name, source.at[0], out[name].at[0]))
            for copy in results:
                copy.start()
            schedule.at("x")
            for copy in results:
                copy.wait()

        pl.run_scoped(
            expert_phase,
            pltpu.VMEM((2, MOST, d), BF16),
            pltpu.VMEM((2, MOST, d), BF16),
            pltpu.VMEM((d, count), BF16),
            pltpu.VMEM((count, d), F32),
            pltpu.VMEM((count, d), F32),
            pltpu.VMEM((2, nz, nx, 2, depth, tile), BF16),
            pltpu.VMEM((2, nz, nx, hidden_cut, d), BF16),
            pltpu.VMEM((nz, nx, 2, depth, tile), BF16),
            pltpu.VMEM((nz, nx, hidden_cut, d), BF16),
        )

        def backward_phase(grad_res, branch, grad_att, att, projected, normed, wide, acc):
            def load(name, source, target):
                copy = made.local(("back", name), source, target)
                copy.start()
                return copy

            late_loads = [load("att", out["attended"], att), load("normed", out["normed"], normed)]

            for i in range(4):
                at = CUTS + i
                columns = pl.ds(i * d, d)
                pieces.append(
                    PairPiece(
                        reduce_order[len(pieces)],
                        lambda which, spot=(1, 2, 0, 0)[i]: wide.at[spot, :, :, which],
                        out["pair_terms"].at[i],
                        acc.at[i],
                        landing[at * per_piece : (at + 1) * per_piece],
                        out["wo_sum"] if i == 3 else out["qkv_sum"].at[:, columns],
                    )
                )

            def residual_phase(made_rows, back_rows, cot, wo, block, slots_turned):
                loads = [
                    load("residual", out["residual"], grad_res),
                    load("made", out["made_rows"], made_rows),
                    load("back", out["back_rows"], back_rows),
                    load("cot", cot_hbm, cot),
                    load("wo", out["wo_full"], wo),
                ]
                slots_turned[...] = slots[...].astype(F32).T
                for copy in loads:
                    copy.wait()

                @pl.loop(0, n // BLOCK)
                def _(i):
                    rows = pl.ds(pl.multiple_of(i * BLOCK, BLOCK), BLOCK)
                    columns = lax.broadcasted_iota(jnp.int32, (BLOCK, MOST), 1).astype(F32)
                    chosen = jnp.concatenate(
                        [
                            jnp.where(columns == slots_turned[rows, k : k + 1], 1.0, 0.0).astype(BF16)
                            for k in range(2)
                        ],
                        axis=1,
                    )
                    values = grad_res[rows]
                    block[rows] = (values + dot(chosen, as_rows(made_rows[...], count))).astype(BF16)
                    grad = dot(chosen, as_rows(back_rows[...], count))
                    term, gain_sum, shift_sum = norm_backward(values, vectors[0:1, d : 2 * d], grad)
                    sums[1:2, :] += gain_sum
                    sums[3:4, :] += shift_sum
                    now = cot[rows].astype(F32) + term
                    grad_res[rows] = now
                    low = now.astype(BF16)
                    branch[rows] = low
                    sums[6:7, :] += jnp.sum(low.astype(F32), axis=0, keepdims=True)
                    grad_att[rows] = dot_last(low, as_rows(wo[...], d)).astype(BF16)
                    schedule.in_loop(i, "b", n // BLOCK)

                load("block", block, out["block_out"]).wait()

            pl.run_scoped(
                residual_phase,
                pltpu.VMEM((2, MOST, d), BF16),
                pltpu.VMEM((2, MOST, d), BF16),
                pltpu.VMEM((n, d), BF16),
                pltpu.VMEM((nz, nx, 2, depth, d), BF16),
                pltpu.VMEM((n, d), BF16),
                pltpu.VMEM((n, 8), F32),
            )
            for copy in late_loads:
                copy.wait()
            wide[0] = split_rows(dot(att[...].T, branch[...]).astype(BF16), wide.shape[1:])
            schedule.at("wo2")

            def attend_phase(qkv, logs, turned):
                loads = [load("qkv", out["qkv"], qkv), load("logs", out["logs"], logs)]
                for copy in loads:
                    copy.wait()

                @pl.loop(0, heads)
                def _(head):
                    attend_pair_backward(qkv, head, att, grad_att, logs, projected, turned)
                    schedule.in_loop(head, "a", heads)

            pl.run_scoped(
                attend_phase,
                pltpu.VMEM((n, 3 * d), BF16),
                pltpu.VMEM((heads, 8, n), F32),
                pltpu.VMEM((128, n), F32),
            )

            schedule.need("free", reduce, range(2 * CUTS))
            senders = place.partners()[:-1]
            for device in senders:
                pl.semaphore_signal(free, inc=1, device_id=device, device_id_type=MESH_ID)

            def input_phase(w, tok):
                loads = [load("w", out["qkv_full"], w), load("tok", tokens_hbm, tok)]
                normed_turned = normed[...].T
                for part in range(3):
                    columns = slice(part * d, (part + 1) * d)
                    wide[(1, 2, 0)[part]] = split_rows(
                        dot(normed_turned, projected[:, columns]).astype(BF16), wide.shape[1:]
                    )
                    if part == 1:
                        pl.semaphore_wait(free, len(senders))
                    schedule.at(f"p{part}")
                    if part == 1:
                        schedule.force(reduce, 19, 1)
                    if part != 1:
                        sums[4 + part // 2 : 5 + part // 2, :] = jnp.sum(
                            projected[:, columns].astype(F32), axis=0, keepdims=True
                        )
                for copy in loads:
                    copy.wait()

                @pl.loop(0, n // BLOCK)
                def _(i):
                    rows = pl.ds(pl.multiple_of(i * BLOCK, BLOCK), BLOCK)
                    grad = dot_last(projected[rows], as_rows(w[...], d))
                    term, gain_sum, shift_sum = norm_backward(tok[rows].astype(F32), vectors[0:1, :d], grad)
                    grad_res[rows] += term
                    sums[0:1, :] += gain_sum
                    sums[2:3, :] += shift_sum
                    schedule.in_loop(i, "i", n // BLOCK)

                save = load("input_grad", grad_res, out["input_grad"])
                lines = width // d
                for step in range(CHUNKS * tiles):
                    first = (step % tiles) * tile
                    for expert in range(EXPERTS):
                        row = 10 + expert * CHUNKS * lines + step // tiles * lines + first // d
                        sums[row : row + 1, first % d : first % d + tile] = jnp.where(
                            core == expert, bias_sums[step, 0:1, :], 0.0
                        )
                for stage in range(total.stages):
                    total.begin(stage)
                    schedule.at(f"m{stage}")
                    total.finish(stage)
                out["small_sum"][...] = terms[total.stages % 2]
                schedule.need("end", reduce, range(2 * CUTS, len(pieces)))
                save.wait()

            pl.run_scoped(
                input_phase, pltpu.VMEM((nz, nx, 2, depth, 3 * d), BF16), pltpu.VMEM((n, d), BF16)
            )

        pl.run_scoped(
            backward_phase,
            pltpu.VMEM((n, d), F32),
            pltpu.VMEM((n, d), BF16),
            pltpu.VMEM((n, d), BF16),
            pltpu.VMEM((n, d), BF16),
            pltpu.VMEM((n, 3 * d), BF16),
            pltpu.VMEM((n, d), BF16),
            pltpu.VMEM((3, nz, nx, 2, depth, d), BF16),
            pltpu.VMEM((4, nz, nx, depth, d), BF16),
        )

    exchanged = nz + nx
    results = pl.pallas_call(
        kernel,
        out_shape=list(outputs.values()) + list(small_outputs.values()),
        in_specs=[HBM, HBM] + [VMEM] * 6 + [HBM] * 4,
        out_specs=[HBM] * len(outputs) + [VMEM] * len(small_outputs),
        scratch_shapes=[
            pltpu.VMEM((8, n), jnp.int32),
            pltpu.VMEM((16, 128), F32),
            pltpu.VMEM((nz, nx, 2, 16, 128), BF16),
            pltpu.VMEM((CHUNKS * tiles, 8, tile), F32),
            pltpu.VMEM((8, d), F32),
            pltpu.VMEM((CHUNKS * tiles, 8, tile), F32),
            pltpu.VMEM((8, 3 * d), F32),
            pltpu.VMEM((2, small_rows, d), F32),
            pltpu.VMEM((partners, small_rows, d), F32),
            pltpu.SemaphoreType.REGULAR,
            *spares,
            *landing_scratch,
            *semaphores(40 * exchanged + 48, 16 * (max(nx, nz) // 2 + 2) + 56),
        ],
        compiler_params=pltpu.CompilerParams(
            collective_id=1, has_side_effects=True, vmem_limit_bytes=64 * MIB - 64 * 1024
        ),
        name="block",
    )(tokens, cotangent, ids, *small, w_qkv, w_out, in_shard, hidden_own)
    return dict(zip(names, results))


PARTS = 4


def result_kernel(nz, nx, block, running_load, share, hidden_share):
    devices = nz * nx * 2
    n, d = block["block_out"].shape
    depth, width = block["in_sum"].shape[2:]
    lines = width // d

    def kernel(
        block_hbm, input_hbm, qkv_ref, wo_ref, in_ref, hidden_ref, small_ref, counts_ref, load_ref,
        block_out, input_grad, gain, shift, qkv, attn_bias, wo, in_grad, in_bias, hidden, out_bias, counts, loads,
        block_buffer, input_buffer, here,
    ):
        copies = []
        for i in range(2 * PARTS):
            source, buffer, target = ((block_hbm, block_buffer, block_out), (input_hbm, input_buffer, input_grad))[i % 2]
            rows = pl.ds(i // 2 * (n // PARTS), n // PARTS)
            copies.append(
                (
                    pltpu.make_async_copy(source.at[rows], buffer.at[rows], here.at[2 * i]),
                    pltpu.make_async_copy(buffer.at[rows], target.at[rows], here.at[2 * i + 1]),
                )
            )
        for copy in copies:
            copy[0].start()
        for copy in copies:
            copy[0].wait()
            copy[1].start()
        core = lax.axis_index("core")
        chip = lax.axis_index("dp") * nx + lax.axis_index("xy")
        first = (chip * 2 + core) * share
        own = pltpu.roll(small_ref[...], lax.rem(d - first, d), axis=1)
        gain[...] = own[0:2, :share]
        shift[...] = own[2:4, :share]
        attn_bias[...] = own[4:7, :share]
        out_bias[...] = own[8:10, :share]
        cut = hidden_share // CUTS
        first = chip * cut
        rows = lax.broadcasted_iota(jnp.int32, small_ref.shape, 0)
        for expert in range(EXPERTS):
            for k in range(CUTS):
                start = k * (width // CUTS)
                row = 10 + (expert * CHUNKS + core) * lines + start // d
                line = jnp.sum(jnp.where(rows == row, small_ref[...], 0.0), axis=0, keepdims=True)
                line = pltpu.roll(jnp.broadcast_to(line, (8, d)), lax.rem(2 * d - start % d - first, d), axis=1)
                in_bias[expert : expert + 1, k * cut : (k + 1) * cut] = line[0:1, :cut]
        qkv[...] = qkv_ref[...].astype(F32)
        wo[...] = wo_ref[...].astype(F32)
        hidden[...] = hidden_ref[...].astype(F32)
        join_columns(in_ref, in_grad, hidden_share)
        lane = lax.broadcasted_iota(jnp.int32, (1, 128), 1)
        digits = counts_ref[0:1, :]
        second = jnp.sum(jnp.where(lane == 0, digits * 32, jnp.where(lane == 1, digits, 0.0)))
        for expert, count in enumerate((n * devices - second, second)):
            counts[expert] = count.astype(jnp.int32)
            loads[expert] = 0.9 * load_ref[expert] + 0.1 * (count * (EXPERTS / (n * devices)))
        for copy in copies:
            copy[1].wait()

    def f32(*shape):
        return jax.ShapeDtypeStruct(shape, F32)

    scalars = pl.BlockSpec(memory_space=pltpu.SMEM)
    return pl.pallas_call(
        kernel,
        out_shape=[
            jax.ShapeDtypeStruct((n, d), BF16),
            f32(n, d),
            f32(2, share),
            f32(2, share),
            f32(depth, 3 * d),
            f32(3, share),
            f32(depth, d),
            f32(EXPERTS, depth, CHUNKS * width),
            f32(EXPERTS, hidden_share),
            f32(EXPERTS, hidden_share, d),
            f32(EXPERTS, share),
            jax.ShapeDtypeStruct((EXPERTS,), jnp.int32),
            f32(EXPERTS),
        ],
        in_specs=[HBM] * 2 + [VMEM] * 6 + [scalars],
        out_specs=[HBM] * 2 + [VMEM] * 9 + [scalars] * 2,
        scratch_shapes=[
            pltpu.VMEM((n, d), BF16),
            pltpu.VMEM((n, d), F32),
            pltpu.SemaphoreType.DMA((4 * PARTS,)),
        ],
        compiler_params=pltpu.CompilerParams(vmem_limit_bytes=60 * MIB),
        name="results",
    )(
        block["block_out"], block["input_grad"], block["qkv_sum"], block["wo_sum"], block["in_sum"], block["hidden_sum"],
        block["small_sum"], block["counts"], running_load,
    )


def shards(
    nz, nx, tokens, norm_gain, norm_bias, w_qkv, attn_bias, w_attn_out, expert_in, expert_in_bias, expert_out,
    expert_out_bias, expert_ids, running_load, cotangent,
):
    chips = nz * nx
    depth, width = expert_in.shape[1:]
    share, hidden_share = norm_gain.shape[1], expert_out.shape[1]

    tiled = (EXPERTS, depth, CHUNKS, CUTS, chips, hidden_share // CUTS)
    if not whole_tiles(hidden_share):
        expert_in = expert_in.reshape(EXPERTS, depth, chips, CHUNKS, CUTS, -1).transpose(0, 1, 3, 4, 2, 5)
        expert_in = expert_in.reshape(EXPERTS, depth, width)
    small = (norm_gain, norm_bias, attn_bias, expert_out_bias, expert_in_bias)
    ids = expert_ids.reshape(1, tokens.shape[0])
    block = block_kernel(nz, nx, tokens, cotangent, ids, small, w_qkv, w_attn_out, expert_in, expert_out)
    results = list(result_kernel(nz, nx, block, running_load, share, hidden_share))
    if not whole_tiles(hidden_share):
        in_grad = results[7].reshape(tiled).transpose(0, 1, 4, 2, 3, 5)
        results[7] = in_grad.reshape(EXPERTS, depth, width)
    return tuple(results)


def solution(mesh):
    nz, nx = mesh.shape["dp"], mesh.shape["fsdp"] // 2
    fine = Mesh(mesh.devices.reshape(nz, nx, 2), ("dp", "xy", "core"))
    every = ("dp", "xy", "core")
    row, column, middle = P(every, None), P(None, every), P(None, every, None)
    return jax.shard_map(
        functools.partial(shards, nz, nx),
        mesh=fine,
        in_specs=(
            row, column, column, row, column, row, middle, column, middle, column, row, P(), row,
        ),
        out_specs=(row, row, column, column, row, column, row, middle, column, middle, column, P(), P()),
        check_vma=False,
    )
```
